32 devices in a mesh: pipe: 2 (over core), group: 2 (over x), rep: 8 (over z, y).
Axes of the slice: x: 2, y: 2, z: 4, core: 2. Of those that a mesh axis runs over, the one named last changes fastest.
Arguments:
- images: bfloat16 [128, 196, 512], P(('group', 'rep')), may hold values from -6 to 6
- out_grad: bfloat16 [128, 196, 512], P(('group', 'rep')), may hold values from -6 to 6
- window_order: int32 [196], replicated, may hold values from 0 to 195, each once
- regions: int32 [196], replicated, may hold values from 0 to 8
- counts: int32 [16], P(('group', 'rep')), may hold values from 1 to 8, as said below
- norm1_gain: bfloat16 [2, 512], P('pipe', 'group'), may hold values from 0.25 to 1.75
- norm1_bias: bfloat16 [2, 512], P('pipe', 'group'), may hold values from -1.75 to 1.75
- qkv_weight: bfloat16 [2, 512, 1536], P('pipe', 'group'), may hold values from -0.25 to 0.25
- bias_table: bfloat16 [2, 169, 16], P('pipe', None, 'group'), may hold values from -6 to 6
- proj_weight: bfloat16 [2, 512, 512], P('pipe', 'group'), may hold values from -0.75 to 0.75
- proj_bias: bfloat16 [2, 512], P('pipe', 'group'), may hold values from -1.75 to 1.75
- norm2_gain: bfloat16 [2, 512], P('pipe', 'group'), may hold values from 0.25 to 1.75
- norm2_bias: bfloat16 [2, 512], P('pipe', 'group'), may hold values from -1.75 to 1.75
- fc1_weight: bfloat16 [2, 512, 2048], P('pipe', 'group'), may hold values from -0.25 to 0.25
- fc1_bias: bfloat16 [2, 2048], P('pipe', 'group'), may hold values from -1.75 to 1.75
- fc2_weight: bfloat16 [2, 2048, 512], P('pipe', 'group'), may hold values from -0.125 to 0.125
- fc2_bias: bfloat16 [2, 512], P('pipe', 'group'), may hold values from -1.75 to 1.75
Outputs:
- activations: bfloat16 [2, 128, 196, 512], P('pipe', ('group', 'rep'))
- input_grads: bfloat16 [2, 128, 196, 512], P('pipe', ('group', 'rep'))
- grad_norm1_gain: float32 [2, 512], P('pipe', 'group')
- grad_norm1_bias: float32 [2, 512], P('pipe', 'group')
- grad_qkv_weight: float32 [2, 512, 1536], P('pipe', 'group')
- grad_bias_table: float32 [2, 169, 16], P('pipe', None, 'group')
- grad_proj_weight: float32 [2, 512, 512], P('pipe', 'group')
- grad_proj_bias: float32 [2, 512], P('pipe', 'group')
- grad_norm2_gain: float32 [2, 512], P('pipe', 'group')
- grad_norm2_bias: float32 [2, 512], P('pipe', 'group')
- grad_fc1_weight: float32 [2, 512, 2048], P('pipe', 'group')
- grad_fc1_bias: float32 [2, 2048], P('pipe', 'group')
- grad_fc2_weight: float32 [2, 2048, 512], P('pipe', 'group')
- grad_fc2_bias: float32 [2, 512], P('pipe', 'group')
The draws below stay inside these ranges and needn't reach their ends.
Inputs may be any that keep to these rules, and one draw needn't show every extreme that they name: `counts`: a device's number of live images; some device has all 8 live in every draw. `window_order`: each grid position once.
All inputs are finite; a program needn't handle non-finite values.
Results may differ from the reference program's by a relative error of at most 0.02.
Values may be sent and summed in bfloat16 or wider, within the bound.
No kernel may reach another device: no remote copies, remote signals or barrier semaphores. Data moves between devices by JAX's collectives and lax.ppermute only.
A program may use at most 256 MiB of HBM per device.

```python
import jax
import jax.numpy as jnp
from jax import lax

D = 512
FF = 2048
HEADS = 16
WIN = 7
SIDE = 14
SHIFT = 3
IMG_DEV = 8
HEAD_DIM = 32
TOK = 196
WINDOWS = 4
TABLE = 169
SHARDS = 16
IMAGES = 128


def draw_counts(key, part):
    key = jax.random.fold_in(key, 7)
    first_key, second_key = jax.random.split(key)
    drawn = jax.random.randint(first_key, (SHARDS,), 1, IMG_DEV + 1)
    fullest = jax.random.randint(second_key, (), 0, SHARDS)
    return jnp.where(jnp.arange(SHARDS) == fullest, IMG_DEV, drawn).astype(jnp.int32)


def place_ends(values, own_key, smallest, high):
    longest = values.shape.index(max(values.shape))
    spots = []
    for shift in (0, 1):
        where = [jax.random.randint(jax.random.fold_in(own_key, axis), (), 0, length) for axis, length in enumerate(values.shape)]
        where[longest] = (where[longest] + shift) % values.shape[longest]
        spots.append(tuple(where))
    return values.at[spots[0]].set(smallest).at[spots[1]].set(high)


def block_scale(rng, shape, cuts, low, top_value):
    level, own = 1.0, jax.random.fold_in(rng, 6)
    for dim, shards_of in cuts:
        heights = jnp.exp(jax.random.uniform(jax.random.fold_in(own, dim), (shards_of,), jnp.float32, low / len(cuts), top_value / len(cuts)))
        level = level * jnp.repeat(heights, shape[dim] // shards_of).reshape([-1 if axis == dim else 1 for axis in range(len(shape))])
    return level


def centred(stream_key, extent, deviation, reach, shards=(), kind=jnp.bfloat16):
    factor_of = block_scale(stream_key, extent, shards, -0.22, 0.18) if shards else 1.0
    values = jax.random.normal(stream_key, extent, jnp.float32) * deviation * factor_of
    return jnp.minimum(jnp.maximum(values, -reach), reach).astype(kind)


def setup_inputs(seed: int = 0) -> dict:
    key_of = jax.random.split(jax.random.key(seed), 18)
    return {
        "images": centred(key_of[0], (IMAGES, TOK, D), 1.0, 6.0, ((0, 16),)),
        "out_grad": centred(key_of[1], (IMAGES, TOK, D), 1.0, 6.0, ((0, 16),)),
        "window_order": jax.random.permutation(key_of[2], TOK).astype(jnp.int32),
        "regions": place_ends(jax.random.randint(key_of[3], (TOK,), 0, 9), jax.random.fold_in(key_of[3], 1), 0, 8).astype(jnp.int32),
        "counts": draw_counts(jax.random.fold_in(key_of[17], 71), 0),
        "norm1_gain": jnp.clip(1.0 + 0.15 * jax.random.normal(key_of[5], (2, D), jnp.float32), 0.25, 1.75).astype(jnp.bfloat16),
        "norm1_bias": centred(key_of[6], (2, D), 0.3, 1.75, ((0, 2), (1, 2))),
        "qkv_weight": centred(key_of[7], (2, D, 3 * D), D ** -0.5, 0.25, ((0, 2), (1, 2))),
        "bias_table": centred(key_of[8], (2, TABLE, HEADS), 1.0, 6.0, ((0, 2), (2, 2))),
        "proj_weight": centred(key_of[9], (2, D, D), (D // 7) ** -0.5, 0.75, ((0, 2), (1, 2))),
        "proj_bias": centred(key_of[10], (2, D), 0.3, 1.75, ((0, 2), (1, 2))),
        "norm2_gain": jnp.clip(1.0 + 0.15 * jax.random.normal(key_of[11], (2, D), jnp.float32), 0.25, 1.75).astype(jnp.bfloat16),
        "norm2_bias": centred(key_of[12], (2, D), 0.3, 1.75, ((0, 2), (1, 2))),
        "fc1_weight": centred(key_of[13], (2, D, FF), D ** -0.5, 0.25, ((0, 2), (1, 2))),
        "fc1_bias": centred(key_of[14], (2, FF), 0.3, 1.75, ((0, 2), (1, 2))),
        "fc2_weight": centred(key_of[15], (2, FF, D), FF ** -0.5, 0.125, ((0, 2), (1, 2))),
        "fc2_bias": centred(key_of[16], (2, D), 0.3, 1.75, ((0, 2), (1, 2))),
    }


HIGHEST = lax.Precision.HIGHEST
EPSILON = 1e-05

@jax.custom_vjp
def low(v):
    return lax.optimization_barrier(v.astype(jnp.bfloat16)).astype(jnp.float32)

@jax.custom_vjp
def low_back(v):
    return v

def low_keep(v):
    return (low(v), None)

def low_pass(kept, grad):
    return (grad,)

def back_keep(v):
    return (v, None)

def back_low(kept, grad):
    return (low(grad),)
low.defvjp(low_keep, low_pass)
low_back.defvjp(back_keep, back_low)

def tables(window_order, regions, layer_flag):
    places = jnp.arange(TOK, dtype=jnp.int32)
    offset = layer_flag * SHIFT
    rolled = (places // SIDE + offset) % SIDE * SIDE + (places % SIDE + offset) % SIDE
    source = jnp.take(rolled, window_order).astype(jnp.int32)
    inverse = jnp.zeros((TOK,), jnp.int32).at[source].set(places)
    slot_region = jnp.take(regions, window_order).reshape(WINDOWS, WIN * WIN)
    differs = slot_region[:, :, None] != slot_region[:, None, :]
    masking = jnp.where(differs, -100.0, 0.0).astype(jnp.float32) * float(layer_flag)
    slots = jnp.arange(WIN * WIN, dtype=jnp.int32)
    slot_rows = slots // WIN
    slot_cols = slots % WIN
    relative = (slot_rows[:, None] - slot_rows[None, :] + WIN - 1) * (2 * WIN - 1) + slot_cols[:, None] - slot_cols[None, :] + WIN - 1
    return (source, inverse, masking, relative)

def layer_norm(values, gain_vec, offset_vec):
    centre = lax.optimization_barrier(jnp.mean(values, -1, keepdims=True))
    spread = lax.optimization_barrier(jnp.mean((values - centre) * (values - centre), -1, keepdims=True))
    return (values - centre) * lax.rsqrt(spread + EPSILON) * gain_vec + offset_vec

def product(values, weight):
    return jnp.einsum('btd,de->bte', values, weight, precision=HIGHEST)

def layer(params, index, inputs, layout):
    source, inverse, masking, relative = layout
    gain_one, shift_one, qkv_mat, table, proj_mat, proj_shift, gain_two, shift_two, fc1_mat, fc1_shift, fc2_mat, fc2_shift = [array[index] for array in params]
    batch = inputs.shape[0]
    windowed = jnp.take(inputs, source, axis=1)
    normed = layer_norm(windowed, gain_one, shift_one)
    mixed = low(low_back(product(low(normed), qkv_mat)))
    mixed = mixed.reshape(batch, WINDOWS, WIN * WIN, 3, HEADS, HEAD_DIM)
    queries = mixed[:, :, :, 0]
    keys = mixed[:, :, :, 1]
    values = mixed[:, :, :, 2]
    bias_add = jnp.transpose(table[relative], (2, 0, 1))
    scores = jnp.einsum('bwqhd,bwkhd->bwhqk', queries, keys, precision=HIGHEST) * HEAD_DIM ** (-0.5)
    scores = low_back(scores + bias_add[None, None] + masking[None, :, None])
    probs = jax.nn.softmax(scores, axis=-1)
    attended = jnp.einsum('bwhqk,bwkhd->bwqhd', low(probs), values, precision=HIGHEST)
    attended = low(low_back(attended.reshape(batch, TOK, D)))
    residual = windowed + low_back(product(attended, proj_mat) + proj_shift)
    hidden = low_back(product(low(layer_norm(residual, gain_two, shift_two)), fc1_mat) + fc1_shift)
    activated = low(jax.nn.gelu(hidden, approximate=False))
    result = residual + low_back(product(activated, fc2_mat) + fc2_shift)
    return jnp.take(result, inverse, axis=1)

def reference(images, out_grad, window_order, regions, counts, norm1_gain, norm1_bias, qkv_weight, bias_table, proj_weight, proj_bias, norm2_gain, norm2_bias, fc1_weight, fc1_bias, fc2_weight, fc2_bias):
    params = tuple((array.astype(jnp.float32) for array in (norm1_gain, norm1_bias, qkv_weight, bias_table, proj_weight, proj_bias, norm2_gain, norm2_bias, fc1_weight, fc1_bias, fc2_weight, fc2_bias)))
    layout_first = tables(window_order, regions, 0)
    layout_second = tables(window_order, regions, 1)
    blocks = (images.reshape(SHARDS, IMG_DEV, TOK, D), out_grad.reshape(SHARDS, IMG_DEV, TOK, D), counts)

    def whole(weights, inputs, offset):
        leading = layer(weights, 0, inputs, layout_first)
        trailing = layer(weights, 1, low(low_back(leading + offset)), layout_second)
        return (leading, trailing)

    def visit(totals, item):
        span, cotangent, live_count = item
        valid = (jnp.arange(IMG_DEV) < live_count).astype(jnp.float32)[:, None, None]
        inputs = span.astype(jnp.float32)
        outputs, pullback = jax.vjp(whole, params, inputs, jnp.zeros_like(inputs))
        leading, trailing = outputs
        grads_weights, grad_inputs, grad_middle = pullback((jnp.zeros_like(leading), cotangent.astype(jnp.float32) * valid))
        totals = jax.tree.map(jnp.add, totals, grads_weights)
        layer_outs = jnp.stack([leading * valid, trailing * valid]).astype(jnp.bfloat16)
        layer_backs = jnp.stack([grad_inputs, grad_middle]).astype(jnp.bfloat16)
        return (totals, (layer_outs, layer_backs))
    zeros = jax.tree.map(jnp.zeros_like, params)
    totals, (layer_outs, layer_backs) = lax.scan(visit, zeros, blocks)
    activations = jnp.transpose(layer_outs, (1, 0, 2, 3, 4)).reshape(2, IMAGES, TOK, D)
    input_grads = jnp.transpose(layer_backs, (1, 0, 2, 3, 4)).reshape(2, IMAGES, TOK, D)
    return (activations, input_grads, totals[0], totals[1], totals[2], totals[3], totals[4], totals[5], totals[6], totals[7], totals[8], totals[9], totals[10], totals[11])
```

```python
import functools

import jax
import jax.numpy as jnp
from jax import lax
from jax.experimental import pallas as pl
from jax.experimental.pallas import tpu as pltpu
from jax.sharding import PartitionSpec as P

D = 512
FF = 2048
HEADS = 16
WIN = 7
SIDE = 14
SHIFT = 3
HEAD_DIM = 32
TOK = 196
WINDOWS = 4
SLOTS = WIN * WIN
TABLE = 169
ROWS = 56
PAD = 64
IMG = WINDOWS * ROWS
PACK = 4
WIDE = PACK * HEAD_DIM
LANES = PACK * PAD
PACKS = HEADS // PACK
TILE = 512

EPSILON = 1e-05
ROOT_HALF = 0.7071067811865476
DENSITY = 0.3989422804014327
SCALE = HEAD_DIM ** (-0.5)
NEVER = -1e30
F32 = jnp.float32
BF16 = jnp.bfloat16
VMEM_LIMIT = 60 * 1024 * 1024

NN = (((1,), (0,)), ((), ()))
NT = (((1,), (1,)), ((), ()))
TN = (((0,), (0,)), ((), ()))


def mxu(left, right, dims=NN):
    return lax.dot_general(left, right, dims, preferred_element_type=F32)


def normalize(values):
    centre = jnp.mean(values, -1, keepdims=True)
    centred = values - centre
    inv_std = lax.rsqrt(jnp.mean(centred * centred, -1, keepdims=True) + EPSILON)
    return centred * inv_std, inv_std


def norm_back(grad_rows, unit_rows, inv_std, gain):
    scaled = grad_rows * gain
    average = jnp.mean(scaled, -1, keepdims=True)
    aligned = jnp.mean(scaled * unit_rows, -1, keepdims=True)
    return inv_std * (scaled - average - unit_rows * aligned)


def head_masks():
    lane = lax.broadcasted_iota(jnp.int32, (1, WIDE), 1) // HEAD_DIM
    return [(lane == h).astype(F32) for h in range(PACK)]


def spread(block, masks):
    return jnp.concatenate([block * m.astype(BF16) for m in masks], axis=0)


def collect(product, masks):
    total = product[:PAD] * masks[0]
    for h in range(1, PACK):
        total = total + product[h * PAD : (h + 1) * PAD] * masks[h]
    return total


def softmax_t(keys, queries_wide, bias):
    scores = mxu(keys, queries_wide, NT) * SCALE + bias
    weights = jnp.exp(scores - jnp.max(scores, axis=0, keepdims=True))
    return weights * (1.0 / jnp.sum(weights, axis=0, keepdims=True))


def slots_of(which, flags, refs, target):
    side, low = flags[1], flags[3]
    rows = refs[0].shape[1]
    part = rows // 2
    far = (1 - side) * rows
    return (
        target.at[pl.ds(pl.multiple_of(side * rows, rows), rows)],
        target.at[pl.ds(pl.multiple_of(far + low * part, part), part)],
        target.at[pl.ds(pl.multiple_of(far + (1 - low) * part, part), part)],
    )


def load_weights(which, flags, sources, targets, sems):
    for k, (refs, target) in enumerate(zip(sources, targets)):
        places = slots_of(which, flags, refs, target)

        @pl.when(flags[0] == which)
        def _():
            for m in range(3):
                pltpu.make_async_copy(refs[m].at[0], places[m], sems.at[3 * k + m]).start()

        @pl.when(flags[0] != which)
        def _():
            for m in range(3):
                pltpu.make_async_copy(refs[3 + m].at[0], places[m], sems.at[3 * k + m]).start()


def wait_weight(which, flags, k, sources, targets, sems):
    places = slots_of(which, flags, sources[k], targets[k])
    for m in range(3):
        pltpu.make_async_copy(sources[k][m].at[0], places[m], sems.at[3 * k + m]).wait()


def vec(vecs, row, count=1):
    rows = [vecs[row + i : row + i + 1, :] for i in range(count)]
    return rows[0] if count == 1 else jnp.concatenate(rows, axis=1)


def attention_forward(mixed, bias, att):
    masks = head_masks()

    def image(n, carry):
        for w in range(WINDOWS):
            parts = []
            for g in range(PACKS):
                c = g * WIDE
                wide = spread(mixed[n, w, :, c : c + WIDE], masks)
                keys = mixed[n, w, :, D + c : D + c + WIDE]
                values = mixed[n, w, :, 2 * D + c : 2 * D + c + WIDE]
                probs = softmax_t(keys, wide, bias[w, :, g * LANES : (g + 1) * LANES]).astype(BF16)
                parts.append(collect(mxu(probs, values, TN), masks)[:ROWS])
            att[n, w] = jnp.concatenate(parts, axis=1)
        return carry

    lax.fori_loop(0, mixed.shape[0], image, 0)


def attention_backward(mixed, bias, datt, dmix, dscore):
    masks = head_masks()

    def image(n, carry):
        for g in range(PACKS):
            c = g * WIDE
            lanes = slice(g * LANES, (g + 1) * LANES)
            total = None
            for w in range(WINDOWS):
                wide = spread(mixed[n, w, :, c : c + WIDE], masks)
                keys = mixed[n, w, :, D + c : D + c + WIDE]
                values = mixed[n, w, :, 2 * D + c : 2 * D + c + WIDE]
                probs = softmax_t(keys, wide, bias[w, :, lanes])
                dwide = spread(datt[n, w, :, c : c + WIDE], masks)
                dprobs = mxu(values, dwide, NT)
                inner = jnp.sum(dprobs * probs, axis=0, keepdims=True)
                ds = (probs * (dprobs - inner)).astype(BF16)
                total = ds.astype(F32) if total is None else total + ds.astype(F32)
                dmix[n, w, :, 2 * D + c : 2 * D + c + WIDE] = mxu(probs.astype(BF16), dwide)[:ROWS]
                dmix[n, w, :, D + c : D + c + WIDE] = mxu(ds, wide)[:ROWS] * SCALE
                dmix[n, w, :, c : c + WIDE] = collect(mxu(ds, keys, TN), masks)[:ROWS] * SCALE
            dscore[:, lanes] += total
        return carry

    lax.fori_loop(0, mixed.shape[0], image, 0)


def tall(values):
    width = values.shape[-1]
    split = values.reshape(-1, ROWS, width)
    blank = jnp.zeros((split.shape[0], PAD - ROWS, width), F32)
    made = jnp.concatenate([split, blank], axis=1).astype(BF16)
    return made.reshape(-1, WINDOWS, PAD, width)


def place(perm, x):
    return jnp.concatenate([mxu(perm[...], x[n]) for n in range(x.shape[0])], axis=0)


def unplace(perm_back, rows, out, alive=None):
    for n in range(out.shape[0]):
        image = mxu(perm_back[...], rows[n * IMG : (n + 1) * IMG])
        out[n] = (image if alive is None else image * alive(n)).astype(BF16)


def flat(ref):
    return ref[...].reshape(-1, ref.shape[-1])


def attention_part(which, flags, x, perm, bias, vecs, *rest):
    sources = [rest[:6], rest[6:12]]
    residual_out, mixed, att_out, wqkv, wproj, att, sems = rest[12:]
    targets = (wqkv, wproj)
    first = pl.program_id(0) == 0

    @pl.when(first)
    def _():
        load_weights(which, flags, sources, targets, sems)

    windowed = place(perm, x)
    unit, _ = normalize(windowed)
    low = (unit * vec(vecs, 0) + vec(vecs, 1)).astype(BF16)

    @pl.when(first)
    def _():
        wait_weight(which, flags, 0, sources, targets, sems)
        wait_weight(which, flags, 1, sources, targets, sems)

    for j in range(3):
        cols = slice(j * D, (j + 1) * D)
        mixed[:, :, :, cols] = tall(mxu(low, wqkv[:, cols]))
    attention_forward(mixed, bias, att)
    attended = att[...].reshape(-1, D).astype(BF16)
    att_out[...] = attended.reshape(att_out.shape)
    residual = windowed + mxu(attended, wproj[...]) + vec(vecs, 2)
    residual_out[...] = residual.reshape(residual_out.shape)


def hidden_part(which, images, flags, residual_in, perm_back, vecs, *rest):
    sources = [rest[:6], rest[6:12]]
    out, act, slope, wfc1, wfc2, sems = rest[12:]
    targets = (wfc1, wfc2)
    i = pl.program_id(0)

    @pl.when(i == 0)
    def _():
        load_weights(which, flags, sources, targets, sems)

    residual = flat(residual_in)
    unit, _ = normalize(residual)
    low = (unit * vec(vecs, 3) + vec(vecs, 4)).astype(BF16)

    @pl.when(i == 0)
    def _():
        wait_weight(which, flags, 0, sources, targets, sems)
        wait_weight(which, flags, 1, sources, targets, sems)

    result = residual + vec(vecs, 5)
    block = act.shape[:2]
    for j in range(FF // TILE):
        cols = slice(j * TILE, (j + 1) * TILE)
        hidden = mxu(low, wfc1[:, cols]) + vec(vecs, 6 + j)
        below = 0.5 * (1.0 + lax.erf(hidden * ROOT_HALF))
        low_act = (hidden * below).astype(BF16)
        act[:, :, cols] = low_act.reshape(block + (TILE,))
        steep = below + hidden * jnp.exp(-0.5 * hidden * hidden) * DENSITY
        slope[:, :, cols] = steep.astype(BF16).reshape(block + (TILE,))
        result = result + mxu(low_act, wfc2[cols, :])
    step = out.shape[0]

    def alive(n):
        return (flags[0] * images + i * step + n < flags[2]).astype(F32)

    unplace(perm_back, result.astype(BF16), out, alive)


def split_grads(part, left, right, outs, row):
    low = left[:, pl.ds(pl.multiple_of(part * 128, 128), 128)]
    high = left[:, pl.ds(pl.multiple_of(256 + part * 128, 128), 128)]
    both = jnp.concatenate([low, high], axis=1)
    for j in range(right.shape[1] // TILE):
        product = mxu(both, right[:, j * TILE : (j + 1) * TILE], TN).astype(BF16)
        outs[0, row : row + 128, :] = product[:128]
        outs[1, row : row + 128, :] = product[128:]
        row += 128


def hidden_back(which, images, flags, residual_in, act, slope, og, perm, vecs, *rest):
    sources = [rest[:6], rest[6:12]]
    dres, grads_keep, grads_send, sums, wfc1, wfc2, k_two, k_act, k_go, k_dh, sems = rest[12:]
    targets = (wfc1, wfc2)
    i = pl.program_id(0)
    step = og.shape[0]

    @pl.when(i == 0)
    def _():
        load_weights(which, flags, sources, targets, sems)
        sums[...] = jnp.zeros(sums.shape, F32)

    rows = pl.ds(pl.multiple_of(i * step * IMG, step * IMG), step * IMG)
    unit, inv_std = normalize(flat(residual_in))
    k_two[rows, :] = (unit * vec(vecs, 3) + vec(vecs, 4)).astype(BF16)
    placed = []
    for n in range(step):
        image = mxu(perm[...], og[n])
        if which == 1:
            image = image * (flags[0] * images + i * step + n < flags[2]).astype(F32)
        placed.append(image)
    grad_out = jnp.concatenate(placed, axis=0)
    go = grad_out.astype(BF16)
    k_go[rows, :] = go
    k_act[rows, :] = flat(act)

    @pl.when(i == 0)
    def _():
        wait_weight(which, flags, 1, sources, targets, sems)
        wait_weight(which, flags, 0, sources, targets, sems)

    grad_two = jnp.zeros((step * IMG, D), F32)
    for j in range(FF // TILE):
        cols = slice(j * TILE, (j + 1) * TILE)
        steep = slope[:, :, cols].reshape(-1, TILE).astype(F32)
        dh = (mxu(go, wfc2[cols, :], NT) * steep).astype(BF16)
        k_dh[rows, cols] = dh
        sums[6 + j : 7 + j, :] += jnp.sum(dh.astype(F32), axis=0, keepdims=True)
        grad_two = grad_two + mxu(dh, wfc1[:, cols], NT)
    sums[5:6, :] += jnp.sum(grad_out, axis=0, keepdims=True)
    sums[3:4, :] += jnp.sum(grad_two * unit, axis=0, keepdims=True)
    sums[4:5, :] += jnp.sum(grad_two, axis=0, keepdims=True)
    dres[...] = (grad_out + norm_back(grad_two, unit, inv_std, vec(vecs, 3))).reshape(dres.shape)

    @pl.when(i == pl.num_programs(0) - 1)
    def _():
        for slot, out in enumerate((grads_keep, grads_send)):
            part = flags[0] if slot == 0 else 1 - flags[0]
            for half in range(2):
                for q in range(2):
                    left = k_act[:, pl.ds(pl.multiple_of(half * 1024 + part * 512 + q * 256, 256), 256)]
                    out[half, 512 + q * 256 : 768 + q * 256, :] = mxu(left, k_go[...], TN).astype(BF16)
            split_grads(part, k_two, k_dh, out, 0)


def attention_back(which, flags, x, mixed, att, dres, perm, perm_back, bias, vecs, *rest):
    sources = [rest[:6], rest[6:12]]
    dx, grads_keep, grads_send, sums, dscore, wqkv, wproj, datt, dmix, k_one, k_att, k_dp, k_dm, sems = rest[12:]
    targets = (wqkv, wproj)
    i = pl.program_id(0)
    step = x.shape[0]

    @pl.when(i == 0)
    def _():
        load_weights(which, flags, sources, targets, sems)
        sums[...] = jnp.zeros(sums.shape, F32)
        dscore[...] = jnp.zeros(dscore.shape, F32)

    rows = pl.ds(pl.multiple_of(i * step * IMG, step * IMG), step * IMG)
    unit, inv_std = normalize(place(perm, x))
    k_one[rows, :] = (unit * vec(vecs, 0) + vec(vecs, 1)).astype(BF16)
    k_att[rows, :] = flat(att)
    dp = flat(dres).astype(BF16)
    k_dp[rows, :] = dp
    sums[2:3, :] += jnp.sum(dp.astype(F32), axis=0, keepdims=True)

    @pl.when(i == 0)
    def _():
        wait_weight(which, flags, 1, sources, targets, sems)
        wait_weight(which, flags, 0, sources, targets, sems)

    datt[...] = tall(mxu(dp, wproj[...], NT))
    attention_backward(mixed, bias, datt, dmix, dscore)
    dm = dmix[...].reshape(-1, 3 * D).astype(BF16)
    k_dm[rows, :] = dm
    grad_one = mxu(dm, wqkv[...], NT)
    sums[0:1, :] += jnp.sum(grad_one * unit, axis=0, keepdims=True)
    sums[1:2, :] += jnp.sum(grad_one, axis=0, keepdims=True)
    grad = flat(dres) + norm_back(grad_one, unit, inv_std, vec(vecs, 0))
    unplace(perm_back, grad.astype(BF16), dx)

    @pl.when(i == pl.num_programs(0) - 1)
    def _():
        for slot, out in enumerate((grads_keep, grads_send)):
            part = flags[0] if slot == 0 else 1 - flags[0]
            split_grads(part, k_one, k_dm, out, 0)
            split_grads(part, k_att, k_dp, out, 384)


ANY = pl.BlockSpec(memory_space=pl.ANY)
W_ATT = [pltpu.VMEM((D, 3 * D), BF16), pltpu.VMEM((D, D), BF16)]
W_MLP = [pltpu.VMEM((D, FF), BF16), pltpu.VMEM((FF, D), BF16)]
SEMS = [pltpu.SemaphoreType.DMA((6,))]
STEPS = {"attention": 2, "hidden": 2, "hidden_back": 2, "attention_back": 2}


def whole(*shape):
    return pl.BlockSpec(shape, lambda i, flags: (0,) * len(shape), pipeline_mode=pl.Buffered(1))


def block(step, *shape):
    return pl.BlockSpec((step,) + shape, lambda i, flags: (i,) + (0,) * len(shape))


def core_block(step, count):
    return pl.BlockSpec((step, TOK, D), lambda i, flags: (flags[0] * (count // step) + i, 0, 0))


def struct(kind, *shape):
    return jax.ShapeDtypeStruct(shape, kind)


def call(body, images, step, in_specs, outs, scratch, flops, name):
    return pl.pallas_call(
        body,
        grid_spec=pltpu.PrefetchScalarGridSpec(
            num_scalar_prefetch=1,
            grid=(images // step,),
            in_specs=in_specs,
            out_specs=[spec for spec, _ in outs],
            scratch_shapes=scratch,
        ),
        out_shape=[shape for _, shape in outs],
        compiler_params=pltpu.CompilerParams(vmem_limit_bytes=VMEM_LIMIT, dimension_semantics=("arbitrary",)),
        cost_estimate=pl.CostEstimate(flops=flops * images, bytes_accessed=20_000_000, transcendentals=0),
        name=name,
    )


def step_of(name, images):
    step = STEPS[name]
    return step if images % step == 0 else 1


BIAS = (WINDOWS, PAD, HEADS * PAD)
MIXED = (WINDOWS, PAD, 3 * D)


def run_attention(which, flags, x, shared, weights, images):
    step = step_of("attention", images)
    perm, _, bias, vecs = shared
    entry = core_block(step, images) if which == 0 else block(step, TOK, D)
    return call(
        functools.partial(attention_part, which),
        images,
        step,
        [entry, whole(IMG, TOK), whole(*BIAS), whole(16, D)] + [ANY] * 12,
        [
            (block(step, IMG, D), struct(F32, images, IMG, D)),
            (block(step, *MIXED), struct(BF16, images, *MIXED)),
            (block(step, IMG, D), struct(BF16, images, IMG, D)),
        ],
        W_ATT + [pltpu.VMEM((step, WINDOWS, ROWS, D), F32)] + SEMS,
        800_000_000,
        "layer%d_attention" % which,
    )(flags, x, perm, bias, vecs, *weights)


def run_hidden(which, flags, residual, shared, weights, images):
    step = step_of("hidden", images)
    _, perm_back, _, vecs = shared
    return call(
        functools.partial(hidden_part, which, images),
        images,
        step,
        [block(step, IMG, D), whole(TOK, IMG), whole(16, D)] + [ANY] * 12,
        [
            (block(step, TOK, D), struct(BF16, images, TOK, D)),
            (block(step, IMG, FF), struct(BF16, images, IMG, FF)),
            (block(step, IMG, FF), struct(BF16, images, IMG, FF)),
        ],
        W_MLP + SEMS,
        1_000_000_000,
        "layer%d_hidden" % which,
    )(flags, residual, perm_back, vecs, *weights)


def run_hidden_back(which, flags, residual, act, slope, og, shared, weights, images):
    step = step_of("hidden_back", images)
    perm, _, _, vecs = shared
    rows = images * IMG
    cotangent = block(step, TOK, D) if which == 0 else core_block(step, images)
    return call(
        functools.partial(hidden_back, which, images),
        images,
        step,
        [block(step, IMG, D), block(step, IMG, FF), block(step, IMG, FF), cotangent, whole(IMG, TOK), whole(16, D)]
        + [ANY] * 12,
        [
            (block(step, IMG, D), struct(F32, images, IMG, D)),
            (whole(2, 1024, D), struct(BF16, 2, 1024, D)),
            (whole(2, 1024, D), struct(BF16, 2, 1024, D)),
            (whole(16, D), struct(F32, 16, D)),
        ],
        W_MLP + [pltpu.VMEM((rows, width), BF16) for width in (D, FF, D, FF)] + SEMS,
        2_000_000_000,
        "layer%d_hidden_back" % which,
    )(flags, residual, act, slope, og, perm, vecs, *weights)


def run_attention_back(which, flags, x, mixed, att, dres, shared, weights, images):
    step = step_of("attention_back", images)
    perm, perm_back, bias, vecs = shared
    rows = images * IMG
    entry = core_block(step, images) if which == 0 else block(step, TOK, D)
    return call(
        functools.partial(attention_back, which),
        images,
        step,
        [entry, block(step, *MIXED), block(step, IMG, D), block(step, IMG, D)]
        + [whole(IMG, TOK), whole(TOK, IMG), whole(*BIAS), whole(16, D)]
        + [ANY] * 12,
        [
            (block(step, TOK, D), struct(BF16, images, TOK, D)),
            (whole(2, 512, D), struct(BF16, 2, 512, D)),
            (whole(2, 512, D), struct(BF16, 2, 512, D)),
            (whole(16, D), struct(F32, 16, D)),
            (whole(PAD, HEADS * PAD), struct(F32, PAD, HEADS * PAD)),
        ],
        W_ATT
        + [pltpu.VMEM((step, WINDOWS, PAD, D), BF16), pltpu.VMEM((step, WINDOWS, ROWS, 3 * D), F32)]
        + [pltpu.VMEM((rows, width), BF16) for width in (D, D, D, 3 * D)]
        + SEMS,
        2_000_000_000,
        "layer%d_attention_back" % which,
    )(flags, x, mixed, att, dres, perm, perm_back, bias, vecs, *weights)


SWAP = [(0, 1), (1, 0)]


def swap(array, axis):
    return lax.ppermute(array, axis, SWAP)


def relative_onehot():
    t = jnp.arange(PAD, dtype=jnp.int32)[:, None]
    s = jnp.arange(PAD, dtype=jnp.int32)[None, :]
    relative = (s // WIN - t // WIN + WIN - 1) * (2 * WIN - 1) + s % WIN - t % WIN + WIN - 1
    relative = jnp.where((t < SLOTS) & (s < SLOTS), relative, -1).reshape(-1)
    return relative[None, :] == jnp.arange(TABLE, dtype=jnp.int32)[:, None]


def geometry(window_order, regions, layer):
    offset = layer * SHIFT
    source = (window_order // SIDE + offset) % SIDE * SIDE + (window_order % SIDE + offset) % SIDE
    padded = jnp.pad(source.reshape(WINDOWS, SLOTS), ((0, 0), (0, ROWS - SLOTS)), constant_values=-1).reshape(-1)
    places = jnp.arange(TOK, dtype=jnp.int32)
    perm = (padded[:, None] == places[None, :]).astype(BF16)
    perm_back = (places[:, None] == padded[None, :]).astype(BF16)
    masking = jnp.zeros((WINDOWS, PAD, PAD), F32)
    if layer:
        hits = window_order[:, None] == places[None, :]
        region = jnp.sum(jnp.where(hits, regions[None, :], 0), axis=1).reshape(WINDOWS, SLOTS)
        region = jnp.pad(region, ((0, 0), (0, PAD - SLOTS)))
        masking = jnp.where(region[:, :, None] != region[:, None, :], -100.0 * layer, 0.0)
    masking = jnp.where(jnp.arange(PAD)[None, :, None] < SLOTS, masking, NEVER)
    return perm, perm_back, masking.astype(F32)


def bias_of(table, masking):
    spread_bias = jnp.dot(table.T, relative_onehot().astype(BF16), preferred_element_type=F32)
    spread_bias = spread_bias.reshape(HEADS, PAD, PAD).transpose(1, 0, 2)
    return (spread_bias[None] + masking[:, :, None, :]).reshape(WINDOWS, PAD, HEADS * PAD)


def pick(array, index):
    return lax.dynamic_index_in_dim(array, index, 0, keepdims=False)


def after(values, *others):
    return lax.optimization_barrier((values, others))[0]


class Place:
    def __init__(self, replicas):
        self.replicas = replicas
        self.outer = replicas // 2
        self.core = lax.axis_index("pipe")
        self.side = lax.axis_index("group")
        rep = lax.axis_index("rep")
        self.low = rep % 2
        self.high = rep // 2
        self.near = [(r, r ^ 1) for r in range(replicas)]

    def hop(self, array, by):
        count = self.replicas
        return lax.ppermute(array, "rep", [(r, (r + 2 * by) % count) for r in range(count)])


def fetch(place, layer, arrays, *earlier):
    count = place.replicas
    x_pairs = [(2 * layer, 2 * layer + 1), (2 * layer + 1, 2 * layer)]
    y_pairs = [(layer * count + a, layer * count + b) for a, b in place.near]
    parts = [lax.dynamic_slice_in_dim(w, place.low * (w.shape[1] // 2), w.shape[1] // 2, 1) for w in arrays]
    if earlier:
        parts = after(parts, *earlier)
    over_x = [lax.ppermute(part, ("pipe", "group"), x_pairs) for part in parts]
    over_y = [lax.ppermute(part, ("pipe", "rep"), y_pairs) for part in over_x]
    pieces = []
    for trio in zip(arrays, over_x, over_y):
        pieces += list(trio)
        pieces += [lax.ppermute(piece, "pipe", [(layer, 1 - layer)]) for piece in trio]
    return pieces, over_x


class Chain:
    def __init__(self, place, keep, send):
        self.place, self.keep, self.rows = place, keep, keep.shape[1]
        self.got = swap(send, "pipe")

    def over_x(self, *earlier):
        side = self.place.side
        far = pick(self.keep, 1 - side).astype(F32) + pick(self.got, 1 - side)
        self.far = far.astype(BF16)
        if earlier:
            self.far = after(self.far, *earlier)
        self.got_x = swap(self.far, "group")

    def over_y(self):
        place = self.place
        total = pick(self.keep, place.side).astype(F32) + pick(self.got, place.side) + self.got_x
        total = total.reshape(2, self.rows // 2, D)
        self.away = pick(total, 1 - place.low).astype(BF16)
        got = lax.ppermute(self.away, "rep", place.near)
        self.mine = pick(total, place.low) + got

    def over_z(self):
        place = self.place
        mine = self.mine.reshape(place.outer, self.rows // place.replicas, D)
        self.low_mine = mine.astype(BF16)
        arrived = [place.hop(pick(self.low_mine, (place.high + by) % place.outer), by) for by in range(1, place.outer)]
        total = pick(mine, place.high)
        for piece in arrived:
            total = total + piece.astype(F32)
        self.total = total.astype(BF16)

    def back(self):
        place = self.place
        self.line = jnp.stack([self.total] + [place.hop(self.total, by) for by in range(1, place.outer)])
        self.other = lax.ppermute(self.line, "rep", place.near)

    def ordered(self, line, other):
        place = self.place
        both = jnp.where(place.low == 0, jnp.stack([line, other]), jnp.stack([other, line]))
        turned = jnp.concatenate([both[:, :1], both[:, :0:-1]], axis=1)
        twice = jnp.concatenate([turned, turned], axis=1)
        kept = lax.dynamic_slice_in_dim(twice, place.outer - place.high, place.outer, 1)
        return kept.reshape(self.rows, D)

    def finish(self, layer, rows):
        pairs = [(1 - layer, layer)]
        line, other = lax.ppermute(self.line, "pipe", pairs), lax.ppermute(self.other, "pipe", pairs)
        own, came = self.ordered(self.line, self.other), self.ordered(line, other)
        parts = [own, came] if layer == 0 else [came, own]
        return jnp.stack([part[:rows] for part in parts]), own


def per_device(replicas, images, out_grad, window_order, regions, counts, *params):
    place = Place(replicas)
    core, side = place.core, place.side
    count = images.shape[0] // 2
    flags = jnp.stack([core, side, counts[0], place.low]).astype(jnp.int32)
    (gain_one, shift_one, qkv, table, proj, proj_shift, gain_two, shift_two, fc1, fc1_shift, fc2, fc2_shift) = params

    small = jnp.concatenate(
        [v for v in (gain_one, shift_one, proj_shift, gain_two, shift_two, fc2_shift)] + [fc1_shift.reshape(4, 256)], axis=0
    )
    small_x = swap(small, "group")
    table_x = swap(table[0], "group")
    joined = jnp.where(
        side == 0, jnp.concatenate([small, small_x], axis=1), jnp.concatenate([small_x, small], axis=1)
    )
    ordered = jnp.where(side == 0, jnp.concatenate([small[6:], small_x[6:]]), jnp.concatenate([small_x[6:], small[6:]]))
    joined = jnp.concatenate([joined[:6], ordered.reshape(4, D), jnp.zeros((6, D), BF16)], axis=0)
    joined_table = jnp.where(
        side == 0, jnp.concatenate([table[0], table_x], axis=1), jnp.concatenate([table_x, table[0]], axis=1)
    )
    joined_o = swap(joined, "pipe")
    table_o = swap(joined_table, "pipe")
    vecs = [jnp.where(core == l, joined, joined_o).astype(F32) for l in range(2)]
    tables = [jnp.where(core == l, joined_table, table_o) for l in range(2)]

    att_zero, came = fetch(place, 0, (qkv, proj))
    mlp_zero, came = fetch(place, 0, (fc1, fc2), *came)
    att_one, came = fetch(place, 1, (qkv, proj), *came)
    mlp_one, came = fetch(place, 1, (fc1, fc2), *came)

    shared = []
    for layer in range(2):
        perm, perm_back, masking = geometry(window_order, regions, layer)
        shared.append((perm, perm_back, bias_of(tables[layer], masking), vecs[layer]))

    residual_zero, mixed_zero, attended_zero = run_attention(0, flags, images, shared[0], att_zero, count)
    out_zero, act_zero, slope_zero = run_hidden(0, flags, residual_zero, shared[0], mlp_zero, count)
    residual_one, mixed_one, attended_one = run_attention(1, flags, out_zero, shared[1], att_one, count)
    out_one, act_one, slope_one = run_hidden(1, flags, residual_one, shared[1], mlp_one, count)
    dres_one, keep, send, sums_mlp_one = run_hidden_back(
        1, flags, residual_one, act_one, slope_one, out_grad, shared[1], mlp_one, count
    )
    chain_a = Chain(place, keep, send)
    chain_a.over_x()
    dres_one = after(dres_one, chain_a.far)
    grad_one, keep, send, sums_att_one, score_one = run_attention_back(
        1, flags, out_zero, mixed_one, attended_one, dres_one, shared[1], att_one, count
    )
    chain_b = Chain(place, keep, send)
    chain_a.over_y()
    chain_b.over_x(chain_a.got_x)
    entry = after(grad_one, chain_a.away, chain_b.far)
    dres_zero, keep, send, sums_mlp_zero = run_hidden_back(
        0, flags, residual_zero, act_zero, slope_zero, entry, shared[0], mlp_zero, count
    )
    chain_c = Chain(place, keep, send)
    chain_a.over_z()
    chain_b.over_y()
    chain_c.over_x(chain_b.got_x)
    dres_zero = after(dres_zero, chain_a.low_mine, chain_b.away, chain_c.far)
    grad_zero, keep, send, sums_att_zero, score_zero = run_attention_back(
        0, flags, images, mixed_zero, attended_zero, dres_zero, shared[0], att_zero, count
    )

    def both(first_array, second_array):
        mine = jnp.where(core == 0, first_array, second_array)
        other = swap(jnp.where(core == 0, second_array, first_array), "pipe")
        return jnp.where(
            core == 0, jnp.concatenate([mine, other], axis=0), jnp.concatenate([other, mine], axis=0)
        )[None]

    activations = both(out_zero, out_one)
    input_grads = both(grad_zero, grad_one)

    def packed(sums, score):
        lookup = relative_onehot().astype(F32)
        flat_score = score.reshape(PAD, HEADS, PAD).transpose(1, 0, 2).reshape(HEADS, PAD * PAD)
        grad_table = lax.dot_general(lookup, flat_score, NT, precision=lax.Precision.HIGHEST)
        halves = [
            sums[:6].reshape(6, 2, 256).transpose(1, 0, 2).reshape(2, 1536),
            sums[6:10].reshape(2, 1024),
            grad_table.reshape(TABLE, 2, 8).transpose(1, 0, 2).reshape(2, TABLE * 8),
            jnp.zeros((2, 8 * D - 1536 - 1024 - TABLE * 8), F32),
        ]
        line = jnp.concatenate(halves, axis=1).astype(BF16).reshape(2, 8, D)
        return jnp.pad(line, ((0, 0), (0, max(replicas - 8, 0)), (0, 0)))

    pack_zero = packed(sums_mlp_zero + sums_att_zero, score_zero)
    pack_one = packed(sums_mlp_one + sums_att_one, score_one)
    pack_keep = jnp.where(core == 0, pack_zero, pack_one)
    pack_send = jnp.where(core == 0, pack_one, pack_zero)

    chain_d = Chain(
        place, jnp.concatenate([keep, pack_keep], axis=1), jnp.concatenate([send, pack_send], axis=1)
    )
    chain_a.back()
    chain_b.over_z()
    chain_c.over_y()
    chain_d.over_x(chain_c.got_x)
    chain_b.back()
    chain_c.over_z()
    chain_d.over_y()
    chain_c.back()
    chain_d.over_z()
    chain_d.back()

    mlp_parts = jnp.where(core == 0, chain_c.finish(0, 1024)[0], chain_a.finish(1, 1024)[0]).astype(F32)
    last, tail = chain_d.finish(0, 512)
    att_parts = jnp.where(core == 0, last, chain_b.finish(1, 512)[0]).astype(F32)
    tail = tail[512:520].reshape(-1).astype(F32)

    def wide(parts, start, blocks):
        rows = parts[:, start : start + 128 * blocks].reshape(2, blocks, 128, D)
        return rows.transpose(0, 2, 1, 3).reshape(1, 256, blocks * D)

    vectors = tail[:1536].reshape(6, 1, 256)
    return (
        activations,
        input_grads,
        vectors[0],
        vectors[1],
        wide(att_parts, 0, 3),
        tail[2560 : 2560 + TABLE * 8].reshape(1, TABLE, 8),
        wide(att_parts, 384, 1),
        vectors[2],
        vectors[3],
        vectors[4],
        wide(mlp_parts, 0, 4),
        tail[1536:2560].reshape(1, 1024),
        mlp_parts[:, 512:].reshape(1, 1024, D),
        vectors[5],
    )


def solution(mesh):
    return jax.shard_map(
        functools.partial(per_device, mesh.shape["rep"]),
        mesh=mesh,
        in_specs=(
            P(("group", "rep"), None, None),
            P(("group", "rep"), None, None),
            P(),
            P(),
            P(("group", "rep")),
            P("pipe", "group"),
            P("pipe", "group"),
            P("pipe", "group", None),
            P("pipe", None, "group"),
            P("pipe", "group", None),
            P("pipe", "group"),
            P("pipe", "group"),
            P("pipe", "group"),
            P("pipe", "group", None),
            P("pipe", "group"),
            P("pipe", "group", None),
            P("pipe", "group"),
        ),
        out_specs=(
            P("pipe", ("group", "rep"), None, None),
            P("pipe", ("group", "rep"), None, None),
            P("pipe", "group"),
            P("pipe", "group"),
            P("pipe", "group", None),
            P("pipe", None, "group"),
            P("pipe", "group", None),
            P("pipe", "group"),
            P("pipe", "group"),
            P("pipe", "group"),
            P("pipe", "group", None),
            P("pipe", "group"),
            P("pipe", "group", None),
            P("pipe", "group"),
        ),
        check_vma=False,
    )
```

```python
import functools

import jax
import jax.numpy as jnp
from jax import lax
from jax.experimental import pallas as pl
from jax.experimental.pallas import tpu as pltpu
from jax.sharding import PartitionSpec as P

D = 512
FF = 2048
HEADS = 16
WIN = 7
SIDE = 14
SHIFT = 3
HEAD_DIM = 32
TOK = 196
WINDOWS = 4
SLOTS = WIN * WIN
TABLE = 169
ROWS = 56
PAD = 64
IMG = WINDOWS * ROWS
PACK = 4
WIDE = PACK * HEAD_DIM
LANES = PACK * PAD
PACKS = HEADS // PACK
TILE = 512

EPSILON = 1e-05
ROOT_HALF = 0.7071067811865476
DENSITY = 0.3989422804014327
SCALE = HEAD_DIM ** (-0.5)
NEVER = -1e30
F32 = jnp.float32
BF16 = jnp.bfloat16
VMEM_LIMIT = 60 * 1024 * 1024

NN = (((1,), (0,)), ((), ()))
NT = (((1,), (1,)), ((), ()))
TN = (((0,), (0,)), ((), ()))


def mxu(left, right, dims=NN):
    return lax.dot_general(left, right, dims, preferred_element_type=F32)


def normalize(values):
    centre = jnp.mean(values, -1, keepdims=True)
    centred = values - centre
    inv_std = lax.rsqrt(jnp.mean(centred * centred, -1, keepdims=True) + EPSILON)
    return centred * inv_std, inv_std


def norm_back(grad_rows, unit_rows, inv_std, gain):
    scaled = grad_rows * gain
    average = jnp.mean(scaled, -1, keepdims=True)
    aligned = jnp.mean(scaled * unit_rows, -1, keepdims=True)
    return inv_std * (scaled - average - unit_rows * aligned)


def head_masks():
    lane = lax.broadcasted_iota(jnp.int32, (1, WIDE), 1) // HEAD_DIM
    return [(lane == h).astype(F32) for h in range(PACK)]


def spread(block, masks):
    return jnp.concatenate([block * m.astype(BF16) for m in masks], axis=0)


def collect(product, masks):
    total = product[:PAD] * masks[0]
    for h in range(1, PACK):
        total = total + product[h * PAD : (h + 1) * PAD] * masks[h]
    return total


def softmax_t(keys, queries_wide, bias):
    scores = mxu(keys, queries_wide, NT) * SCALE + bias
    weights = jnp.exp(scores - jnp.max(scores, axis=0, keepdims=True))
    return weights * (1.0 / jnp.sum(weights, axis=0, keepdims=True))


def copies(which, flags, refs, sems):
    own, other, x_own, y_own, x_other, y_other, base, target = refs
    side, low = flags[1], flags[3]
    pairs = []
    for b in range(BLOCKS):
        here = pl.ds((base + b) * 256, 256)
        pairs.append((own.at[here], other.at[here], target(side, b)))
    for over, over_other, half in ((x_own, x_other, low), (y_own, y_other, 1 - low)):
        for b in range(2):
            here = pl.ds(b * 256, 256)
            pairs.append((over.at[here], over_other.at[here], target(1 - side, 2 * half + b)))
    return [[(refs[m], refs[2], sems.at[k]) for m in range(2)] for k, refs in enumerate(pairs)]


def load_weights(which, flags, segments, sems):
    made = [copies(which, flags, refs, sems.at[k]) for k, refs in enumerate(segments)]

    @pl.when(flags[0] == which)
    def _():
        for segment in made:
            for copy, _ in segment:
                pltpu.make_async_copy(*copy).start()

    @pl.when(flags[0] != which)
    def _():
        for segment in made:
            for _, copy in segment:
                pltpu.make_async_copy(*copy).start()


def wait_weights(which, flags, segments, sems):
    for k, refs in enumerate(segments):
        for copy, _ in copies(which, flags, refs, sems.at[k]):
            pltpu.make_async_copy(*copy).wait()


def by_columns(ref):
    return lambda half, b: ref.at[b, pl.ds(pl.multiple_of(half * 256, 256), 256)]


def by_rows(ref):
    return lambda half, b: ref.at[half * BLOCKS + b]


def att_segments(refs, wqkv):
    return [tuple(refs) + (0, by_columns(wqkv))]


def mlp_segments(refs, wfc1, wfc2):
    own = tuple(refs[:2])
    return [own + tuple(refs[2:6]) + (4, by_columns(wfc1)), own + tuple(refs[6:10]) + (8, by_rows(wfc2))]


def vec(vecs, row, count=1):
    rows = [vecs[row + i : row + i + 1, :] for i in range(count)]
    return rows[0] if count == 1 else jnp.concatenate(rows, axis=1)


def attention_forward(mixed, bias, att):
    masks = head_masks()

    def image(n, carry):
        for w in range(WINDOWS):
            parts = []
            for g in range(PACKS):
                c = g * WIDE
                wide = spread(mixed[n, w, :, c : c + WIDE], masks)
                keys = mixed[n, w, :, D + c : D + c + WIDE]
                values = mixed[n, w, :, 2 * D + c : 2 * D + c + WIDE]
                probs = softmax_t(keys, wide, bias[w, :, g * LANES : (g + 1) * LANES]).astype(BF16)
                parts.append(collect(mxu(probs, values, TN), masks)[:ROWS])
            att[n, w] = jnp.concatenate(parts, axis=1)
        return carry

    lax.fori_loop(0, mixed.shape[0], image, 0)


def attention_backward(mixed, bias, datt, dmix, dscore):
    masks = head_masks()

    def image(n, carry):
        for g in range(PACKS):
            c = g * WIDE
            lanes = slice(g * LANES, (g + 1) * LANES)
            total = None
            for w in range(WINDOWS):
                wide = spread(mixed[n, w, :, c : c + WIDE], masks)
                keys = mixed[n, w, :, D + c : D + c + WIDE]
                values = mixed[n, w, :, 2 * D + c : 2 * D + c + WIDE]
                probs = softmax_t(keys, wide, bias[w, :, lanes])
                dwide = spread(datt[n, w, :, c : c + WIDE], masks)
                dprobs = mxu(values, dwide, NT)
                inner = jnp.sum(dprobs * probs, axis=0, keepdims=True)
                ds = (probs * (dprobs - inner)).astype(BF16)
                total = ds.astype(F32) if total is None else total + ds.astype(F32)
                dmix[n, w, :, 2 * D + c : 2 * D + c + WIDE] = mxu(probs.astype(BF16), dwide)[:ROWS]
                dmix[n, w, :, D + c : D + c + WIDE] = mxu(ds, wide)[:ROWS] * SCALE
                dmix[n, w, :, c : c + WIDE] = collect(mxu(ds, keys, TN), masks)[:ROWS] * SCALE
            dscore[:, lanes] += total
        return carry

    lax.fori_loop(0, mixed.shape[0], image, 0)


def tall(values):
    width = values.shape[-1]
    split = values.reshape(-1, ROWS, width)
    blank = jnp.zeros((split.shape[0], PAD - ROWS, width), F32)
    made = jnp.concatenate([split, blank], axis=1).astype(BF16)
    return made.reshape(-1, WINDOWS, PAD, width)


def place(perm, x):
    return jnp.concatenate([mxu(perm[...], x[n]) for n in range(x.shape[0])], axis=0)


def unplace(perm_back, rows, out, alive=None):
    for n in range(out.shape[0]):
        image = mxu(perm_back[...], rows[n * IMG : (n + 1) * IMG])
        out[n] = (image if alive is None else image * alive(n)).astype(BF16)


def flat(ref):
    return ref[...].reshape(-1, ref.shape[-1])


def attention_part(which, flags, x, perm, bias, vecs, *rest):
    residual_out, mixed, att_out, weights, att, sems = rest[6:]
    segments = att_segments(rest[:6], weights)
    first = pl.program_id(0) == 0

    @pl.when(first)
    def _():
        load_weights(which, flags, segments, sems)

    windowed = place(perm, x)
    unit, _ = normalize(windowed)
    low = (unit * vec(vecs, 0) + vec(vecs, 1)).astype(BF16)

    @pl.when(first)
    def _():
        wait_weights(which, flags, segments, sems)

    for j in range(3):
        cols = slice(j * D, (j + 1) * D)
        mixed[:, :, :, cols] = tall(mxu(low, weights[j]))
    attention_forward(mixed, bias, att)
    attended = att[...].reshape(-1, D).astype(BF16)
    att_out[...] = attended.reshape(att_out.shape)
    residual = windowed + mxu(attended, weights[3]) + vec(vecs, 2)
    residual_out[...] = residual.reshape(residual_out.shape)


def hidden_part(which, images, flags, residual_in, perm_back, vecs, *rest):
    out, act, slope, wfc1, wfc2, sems = rest[10:]
    segments = mlp_segments(rest[:10], wfc1, wfc2)
    i = pl.program_id(0)

    @pl.when(i == 0)
    def _():
        load_weights(which, flags, segments, sems)

    residual = flat(residual_in)
    unit, _ = normalize(residual)
    low = (unit * vec(vecs, 3) + vec(vecs, 4)).astype(BF16)

    @pl.when(i == 0)
    def _():
        wait_weights(which, flags, segments, sems)

    result = residual + vec(vecs, 5)
    block = act.shape[:2]
    for j in range(FF // TILE):
        cols = slice(j * TILE, (j + 1) * TILE)
        hidden = mxu(low, wfc1[j]) + vec(vecs, 6 + j)
        below = 0.5 * (1.0 + lax.erf(hidden * ROOT_HALF))
        low_act = (hidden * below).astype(BF16)
        act[:, :, cols] = low_act.reshape(block + (TILE,))
        steep = below + hidden * jnp.exp(-0.5 * hidden * hidden) * DENSITY
        slope[:, :, cols] = steep.astype(BF16).reshape(block + (TILE,))
        result = result + mxu(low_act, wfc2[2 * j : 2 * j + 2].reshape(TILE, D))
    step = out.shape[0]

    def alive(n):
        return (flags[0] * images + i * step + n < flags[2]).astype(F32)

    unplace(perm_back, result.astype(BF16), out, alive)


def split_grads(part, left, right, outs, row):
    low = left[:, pl.ds(pl.multiple_of(part * 128, 128), 128)]
    high = left[:, pl.ds(pl.multiple_of(256 + part * 128, 128), 128)]
    both = jnp.concatenate([low, high], axis=1)
    for j in range(right.shape[1] // TILE):
        product = mxu(both, right[:, j * TILE : (j + 1) * TILE], TN).astype(BF16)
        outs[0, row : row + 128, :] = product[:128]
        outs[1, row : row + 128, :] = product[128:]
        row += 128


def hidden_back(which, images, flags, residual_in, act, slope, att, og, perm, vecs, *rest):
    dres, grads_keep, grads_send, sums, wfc1, wfc2, k_two, k_act, k_go, k_dh, k_att, k_dp, sems = rest[10:]
    segments = mlp_segments(rest[:10], wfc1, wfc2)
    i = pl.program_id(0)
    step = og.shape[0]

    @pl.when(i == 0)
    def _():
        load_weights(which, flags, segments, sems)
        sums[...] = jnp.zeros(sums.shape, F32)

    rows = pl.ds(pl.multiple_of(i * step * IMG, step * IMG), step * IMG)
    unit, inv_std = normalize(flat(residual_in))
    k_two[rows, :] = (unit * vec(vecs, 3) + vec(vecs, 4)).astype(BF16)
    placed = []
    for n in range(step):
        image = mxu(perm[...], og[n])
        if which == 1:
            image = image * (flags[0] * images + i * step + n < flags[2]).astype(F32)
        placed.append(image)
    grad_out = jnp.concatenate(placed, axis=0)
    go = grad_out.astype(BF16)
    k_go[rows, :] = go
    k_act[rows, :] = flat(act)

    @pl.when(i == 0)
    def _():
        wait_weights(which, flags, segments, sems)

    grad_two = jnp.zeros((step * IMG, D), F32)
    for j in range(FF // TILE):
        cols = slice(j * TILE, (j + 1) * TILE)
        steep = slope[:, :, cols].reshape(-1, TILE).astype(F32)
        dh = (mxu(go, wfc2[2 * j : 2 * j + 2].reshape(TILE, D), NT) * steep).astype(BF16)
        k_dh[rows, cols] = dh
        sums[6 + j : 7 + j, :] += jnp.sum(dh.astype(F32), axis=0, keepdims=True)
        grad_two = grad_two + mxu(dh, wfc1[j], NT)
    sums[5:6, :] += jnp.sum(grad_out, axis=0, keepdims=True)
    sums[3:4, :] += jnp.sum(grad_two * unit, axis=0, keepdims=True)
    sums[4:5, :] += jnp.sum(grad_two, axis=0, keepdims=True)
    grad = grad_out + norm_back(grad_two, unit, inv_std, vec(vecs, 3))
    dres[...] = grad.reshape(dres.shape)
    dp = grad.astype(BF16)
    sums[2:3, :] += jnp.sum(dp.astype(F32), axis=0, keepdims=True)
    k_dp[rows, :] = dp
    k_att[rows, :] = flat(att)

    @pl.when(i == pl.num_programs(0) - 1)
    def _():
        for slot, out in enumerate((grads_keep, grads_send)):
            part = flags[0] if slot == 0 else 1 - flags[0]
            for half in range(2):
                for q in range(2):
                    left = k_act[:, pl.ds(pl.multiple_of(half * 1024 + part * 512 + q * 256, 256), 256)]
                    out[half, 512 + q * 256 : 768 + q * 256, :] = mxu(left, k_go[...], TN).astype(BF16)
            split_grads(part, k_two, k_dh, out, 0)
            split_grads(part, k_att, k_dp, out, 1024)


def attention_back(which, flags, x, mixed, dres, perm, perm_back, bias, vecs, *rest):
    dx, grads_keep, grads_send, sums, dscore, weights, datt, dmix, k_one, k_dm, sems = rest[6:]
    segments = att_segments(rest[:6], weights)
    i = pl.program_id(0)
    step = x.shape[0]

    @pl.when(i == 0)
    def _():
        load_weights(which, flags, segments, sems)
        sums[...] = jnp.zeros(sums.shape, F32)
        dscore[...] = jnp.zeros(dscore.shape, F32)

    rows = pl.ds(pl.multiple_of(i * step * IMG, step * IMG), step * IMG)
    unit, inv_std = normalize(place(perm, x))
    k_one[rows, :] = (unit * vec(vecs, 0) + vec(vecs, 1)).astype(BF16)
    dp = flat(dres).astype(BF16)

    @pl.when(i == 0)
    def _():
        wait_weights(which, flags, segments, sems)

    datt[...] = tall(mxu(dp, weights[3], NT))
    attention_backward(mixed, bias, datt, dmix, dscore)
    dm = dmix[...].reshape(-1, 3 * D).astype(BF16)
    k_dm[rows, :] = dm
    grad_one = sum(mxu(dm[:, j * D : (j + 1) * D], weights[j], NT) for j in range(3))
    sums[0:1, :] += jnp.sum(grad_one * unit, axis=0, keepdims=True)
    sums[1:2, :] += jnp.sum(grad_one, axis=0, keepdims=True)
    grad = flat(dres) + norm_back(grad_one, unit, inv_std, vec(vecs, 0))
    unplace(perm_back, grad.astype(BF16), dx)

    @pl.when(i == pl.num_programs(0) - 1)
    def _():
        for slot, out in enumerate((grads_keep, grads_send)):
            part = flags[0] if slot == 0 else 1 - flags[0]
            split_grads(part, k_one, k_dm, out, 0)


ANY = pl.BlockSpec(memory_space=pl.ANY)
BLOCKS = 4
W_ATT = [pltpu.VMEM((BLOCKS, D, D), BF16)]
W_MLP = [pltpu.VMEM((BLOCKS, D, D), BF16), pltpu.VMEM((2 * BLOCKS, 256, D), BF16)]
SEMS = [pltpu.SemaphoreType.DMA((2, 8))]
STEPS = {"attention": 2, "hidden": 2, "hidden_back": 2, "attention_back": 2}


def whole(*shape):
    return pl.BlockSpec(shape, lambda i, flags: (0,) * len(shape), pipeline_mode=pl.Buffered(1))


def block(step, *shape):
    return pl.BlockSpec((step,) + shape, lambda i, flags: (i,) + (0,) * len(shape))


def core_block(step, count):
    return pl.BlockSpec((step, TOK, D), lambda i, flags: (flags[0] * (count // step) + i, 0, 0))


def struct(kind, *shape):
    return jax.ShapeDtypeStruct(shape, kind)


def call(body, images, step, in_specs, outs, scratch, flops, name):
    return pl.pallas_call(
        body,
        grid_spec=pltpu.PrefetchScalarGridSpec(
            num_scalar_prefetch=1,
            grid=(images // step,),
            in_specs=in_specs,
            out_specs=[spec for spec, _ in outs],
            scratch_shapes=scratch,
        ),
        out_shape=[shape for _, shape in outs],
        compiler_params=pltpu.CompilerParams(vmem_limit_bytes=VMEM_LIMIT, dimension_semantics=("arbitrary",)),
        cost_estimate=pl.CostEstimate(flops=flops * images, bytes_accessed=20_000_000, transcendentals=0),
        name=name,
    )


def step_of(name, images):
    step = STEPS[name]
    return step if images % step == 0 else 1


BIAS = (WINDOWS, PAD, HEADS * PAD)
MIXED = (WINDOWS, PAD, 3 * D)


def run_attention(which, flags, x, shared, weights, images):
    step = step_of("attention", images)
    perm, _, bias, vecs = shared
    entry = core_block(step, images) if which == 0 else block(step, TOK, D)
    return call(
        functools.partial(attention_part, which),
        images,
        step,
        [entry, whole(IMG, TOK), whole(*BIAS), whole(16, D)] + [ANY] * 6,
        [
            (block(step, IMG, D), struct(F32, images, IMG, D)),
            (block(step, *MIXED), struct(BF16, images, *MIXED)),
            (block(step, IMG, D), struct(BF16, images, IMG, D)),
        ],
        W_ATT + [pltpu.VMEM((step, WINDOWS, ROWS, D), F32)] + SEMS,
        800_000_000,
        "layer%d_attention" % which,
    )(flags, x, perm, bias, vecs, *weights)


def run_hidden(which, flags, residual, shared, weights, images):
    step = step_of("hidden", images)
    _, perm_back, _, vecs = shared
    return call(
        functools.partial(hidden_part, which, images),
        images,
        step,
        [block(step, IMG, D), whole(TOK, IMG), whole(16, D)] + [ANY] * 10,
        [
            (block(step, TOK, D), struct(BF16, images, TOK, D)),
            (block(step, IMG, FF), struct(BF16, images, IMG, FF)),
            (block(step, IMG, FF), struct(BF16, images, IMG, FF)),
        ],
        W_MLP + SEMS,
        1_000_000_000,
        "layer%d_hidden" % which,
    )(flags, residual, perm_back, vecs, *weights)


def run_hidden_back(which, flags, residual, act, slope, att, og, shared, weights, images):
    step = step_of("hidden_back", images)
    perm, _, _, vecs = shared
    rows = images * IMG
    cotangent = block(step, TOK, D) if which == 0 else core_block(step, images)
    return call(
        functools.partial(hidden_back, which, images),
        images,
        step,
        [block(step, IMG, D), block(step, IMG, FF), block(step, IMG, FF), block(step, IMG, D), cotangent]
        + [whole(IMG, TOK), whole(16, D)]
        + [ANY] * 10,
        [
            (block(step, IMG, D), struct(F32, images, IMG, D)),
            (whole(2, 1152, D), struct(BF16, 2, 1152, D)),
            (whole(2, 1152, D), struct(BF16, 2, 1152, D)),
            (whole(16, D), struct(F32, 16, D)),
        ],
        W_MLP + [pltpu.VMEM((rows, width), BF16) for width in (D, FF, D, FF, D, D)] + SEMS,
        2_000_000_000,
        "layer%d_hidden_back" % which,
    )(flags, residual, act, slope, att, og, perm, vecs, *weights)


def run_attention_back(which, flags, x, mixed, dres, shared, weights, images):
    step = step_of("attention_back", images)
    perm, perm_back, bias, vecs = shared
    rows = images * IMG
    entry = core_block(step, images) if which == 0 else block(step, TOK, D)
    return call(
        functools.partial(attention_back, which),
        images,
        step,
        [entry, block(step, *MIXED), block(step, IMG, D)]
        + [whole(IMG, TOK), whole(TOK, IMG), whole(*BIAS), whole(16, D)]
        + [ANY] * 6,
        [
            (block(step, TOK, D), struct(BF16, images, TOK, D)),
            (whole(2, 384, D), struct(BF16, 2, 384, D)),
            (whole(2, 384, D), struct(BF16, 2, 384, D)),
            (whole(16, D), struct(F32, 16, D)),
            (whole(PAD, HEADS * PAD), struct(F32, PAD, HEADS * PAD)),
        ],
        W_ATT
        + [pltpu.VMEM((step, WINDOWS, PAD, D), BF16), pltpu.VMEM((step, WINDOWS, ROWS, 3 * D), F32)]
        + [pltpu.VMEM((rows, width), BF16) for width in (D, 3 * D)]
        + SEMS,
        2_000_000_000,
        "layer%d_attention_back" % which,
    )(flags, x, mixed, dres, perm, perm_back, bias, vecs, *weights)


SWAP = [(0, 1), (1, 0)]


def swap(array, axis):
    return lax.ppermute(array, axis, SWAP)


def relative_onehot():
    t = jnp.arange(PAD, dtype=jnp.int32)[:, None]
    s = jnp.arange(PAD, dtype=jnp.int32)[None, :]
    relative = (s // WIN - t // WIN + WIN - 1) * (2 * WIN - 1) + s % WIN - t % WIN + WIN - 1
    relative = jnp.where((t < SLOTS) & (s < SLOTS), relative, -1).reshape(-1)
    return relative[None, :] == jnp.arange(TABLE, dtype=jnp.int32)[:, None]


def geometry(window_order, regions, layer):
    offset = layer * SHIFT
    source = (window_order // SIDE + offset) % SIDE * SIDE + (window_order % SIDE + offset) % SIDE
    padded = jnp.pad(source.reshape(WINDOWS, SLOTS), ((0, 0), (0, ROWS - SLOTS)), constant_values=-1).reshape(-1)
    places = jnp.arange(TOK, dtype=jnp.int32)
    perm = (padded[:, None] == places[None, :]).astype(BF16)
    perm_back = (places[:, None] == padded[None, :]).astype(BF16)
    masking = jnp.zeros((WINDOWS, PAD, PAD), F32)
    if layer:
        hits = window_order[:, None] == places[None, :]
        region = jnp.sum(jnp.where(hits, regions[None, :], 0), axis=1).reshape(WINDOWS, SLOTS)
        region = jnp.pad(region, ((0, 0), (0, PAD - SLOTS)))
        masking = jnp.where(region[:, :, None] != region[:, None, :], -100.0 * layer, 0.0)
    masking = jnp.where(jnp.arange(PAD)[None, :, None] < SLOTS, masking, NEVER)
    return perm, perm_back, masking.astype(F32)


def bias_of(table, masking):
    spread_bias = jnp.dot(table.T, relative_onehot().astype(BF16), preferred_element_type=F32)
    spread_bias = spread_bias.reshape(HEADS, PAD, PAD).transpose(1, 0, 2)
    return (spread_bias[None] + masking[:, :, None, :]).reshape(WINDOWS, PAD, HEADS * PAD)


def pick(array, index):
    return lax.dynamic_index_in_dim(array, index, 0, keepdims=False)


def after(values, *others):
    return lax.optimization_barrier((values, others))[0]


class Place:
    def __init__(self, replicas):
        self.replicas = replicas
        self.core = lax.axis_index("pipe")
        self.side = lax.axis_index("group")
        self.low = lax.axis_index("rep") % 2

    def trade(self, array, bit):
        return lax.ppermute(array, "rep", [(r, r ^ bit) for r in range(self.replicas)])


def in_order(flag, mine, other):
    return jnp.where(flag == 0, jnp.concatenate([mine, other]), jnp.concatenate([other, mine]))


class Chain:
    def __init__(self, place, keep, send):
        self.place, self.keep, self.rows = place, keep, keep.shape[1]
        self.got = swap(send, "pipe")

    def over_x(self, *earlier):
        side = self.place.side
        far = pick(self.keep, 1 - side).astype(F32) + pick(self.got, 1 - side)
        self.sent = far.astype(BF16)
        if earlier:
            self.sent = after(self.sent, *earlier)
        self.arrived = swap(self.sent, "group")

    def over_y(self):
        place = self.place
        total = pick(self.keep, place.side).astype(F32) + pick(self.got, place.side) + self.arrived
        total = total.reshape(2, self.rows // 2, D)
        self.sent = pick(total, 1 - place.low).astype(BF16)
        self.arrived = place.trade(self.sent, 1)
        self.mine = (pick(total, place.low) + self.arrived).astype(BF16)
        self.bit = 2

    def over_z(self):
        self.sent = self.mine
        self.arrived = self.place.trade(self.mine, self.bit)
        self.mine = (self.mine.astype(F32) + self.arrived.astype(F32)).astype(BF16)
        self.bit *= 2

    def rest_of_z(self):
        while self.bit < self.place.replicas:
            self.over_z()

    def back(self):
        self.full = in_order(self.place.low, self.mine, self.place.trade(self.mine, 1))

    def finish(self, layer):
        came = lax.ppermute(self.full, "pipe", [(1 - layer, layer)])
        return jnp.stack([self.full, came] if layer == 0 else [came, self.full])


def blocks_of(array):
    return jnp.concatenate([array[:, c : c + D] for c in range(0, array.shape[1], D)], axis=0)


def per_device(replicas, images, out_grad, window_order, regions, counts, *params):
    place = Place(replicas)
    core, side = place.core, place.side
    count = images.shape[0] // 2
    flags = jnp.stack([core, side, counts[0], place.low]).astype(jnp.int32)
    (gain_one, shift_one, qkv, table, proj, proj_shift, gain_two, shift_two, fc1, fc1_shift, fc2, fc2_shift) = params

    vectors = [gain_one, shift_one, proj_shift, gain_two, shift_two, fc2_shift, fc1_shift, table]
    small = jnp.concatenate([v.reshape(-1) for v in vectors])
    small = jnp.pad(small, (0, 16 * D - small.shape[0])).reshape(16, D)
    parts = [jnp.concatenate([blocks_of(qkv[0]), proj[0]], axis=0), blocks_of(fc1[0]), fc2[0]]
    own = jnp.concatenate(parts + [small], axis=0)
    own_other = swap(own, "pipe")
    over_x, over_y = [], []
    for part in parts:
        half = lax.dynamic_slice_in_dim(part, place.low * 512, 512, 0)
        if over_x:
            half = after(half, over_x[-1])
        else:
            half = jnp.concatenate([half, small], axis=0)
        over_x.append(swap(half, "group"))
        over_y.append(place.trade(over_x[-1], 1))
    pieces = [(x, y, swap(x, "pipe"), swap(y, "pipe")) for x, y in zip(over_x, over_y)]
    att_weights = (own, own_other) + pieces[0]
    mlp_weights = (own, own_other) + pieces[1] + pieces[2]

    shared = []
    for layer in range(2):
        here = jnp.where(core == layer, small, own_other[3072:]).reshape(-1)
        there = jnp.where(core == layer, over_x[0][512:], pieces[0][2][512:]).reshape(-1)
        pair = jnp.stack([jnp.where(side == 0, here, there), jnp.where(side == 0, there, here)])
        six = pair[:, :1536].reshape(2, 6, 256).transpose(1, 0, 2).reshape(6, D)
        vecs = jnp.concatenate([six, pair[:, 1536:2560].reshape(4, D), jnp.zeros((6, D), BF16)]).astype(F32)
        joined = pair[:, 2560 : 2560 + TABLE * 8].reshape(2, TABLE, 8).transpose(1, 0, 2).reshape(TABLE, HEADS)
        perm, perm_back, masking = geometry(window_order, regions, layer)
        shared.append((perm, perm_back, bias_of(joined, masking), vecs))

    residual_zero, mixed_zero, attended_zero = run_attention(0, flags, images, shared[0], att_weights, count)
    out_zero, act_zero, slope_zero = run_hidden(0, flags, residual_zero, shared[0], mlp_weights, count)
    residual_one, mixed_one, attended_one = run_attention(1, flags, out_zero, shared[1], att_weights, count)
    out_one, act_one, slope_one = run_hidden(1, flags, residual_one, shared[1], mlp_weights, count)
    dres_one, keep, send, sums_mlp_one = run_hidden_back(
        1, flags, residual_one, act_one, slope_one, attended_one, out_grad, shared[1], mlp_weights, count
    )
    chain_a = Chain(place, keep, send)
    chain_a.over_x()
    dres_one = after(dres_one, chain_a.sent)
    grad_one, keep, send, sums_att_one, score_one = run_attention_back(
        1, flags, out_zero, mixed_one, dres_one, shared[1], att_weights, count
    )
    chain_b = Chain(place, keep, send)
    chain_a.over_y()
    entry = after(grad_one, chain_a.sent)
    dres_zero, keep, send, sums_mlp_zero = run_hidden_back(
        0, flags, residual_zero, act_zero, slope_zero, attended_zero, entry, shared[0], mlp_weights, count
    )
    chain_b.over_x()
    chain_c = Chain(place, keep[:, :512], send[:, :512])
    chain_e = Chain(place, keep[:, 512:], send[:, 512:])
    chain_a.over_z()
    chain_c.over_x(chain_b.sent)
    chain_e.over_x(chain_c.sent)
    dres_zero = after(dres_zero, chain_a.sent, chain_b.sent, chain_c.sent, chain_e.sent)
    grad_zero, keep, send, sums_att_zero, score_zero = run_attention_back(
        0, flags, images, mixed_zero, dres_zero, shared[0], att_weights, count
    )

    def packed(sums, score):
        lookup = relative_onehot().astype(F32)
        flat_score = score.reshape(PAD, HEADS, PAD).transpose(1, 0, 2).reshape(HEADS, PAD * PAD)
        grad_table = lax.dot_general(lookup, flat_score, NT, precision=lax.Precision.HIGHEST)
        halves = [
            sums[:6].reshape(6, 2, 256).transpose(1, 0, 2).reshape(2, 1536),
            sums[6:10].reshape(2, 1024),
            grad_table.reshape(TABLE, 2, 8).transpose(1, 0, 2).reshape(2, TABLE * 8),
            jnp.zeros((2, 8 * D - 1536 - 1024 - TABLE * 8), F32),
        ]
        return jnp.concatenate(halves, axis=1).astype(BF16).reshape(2, 8, D)

    pack_zero = packed(sums_mlp_zero + sums_att_zero, score_zero)
    pack_one = packed(sums_mlp_one + sums_att_one, score_one)
    pack_keep = jnp.where(core == 0, pack_zero, pack_one)
    pack_send = jnp.where(core == 0, pack_one, pack_zero)
    chain_d = Chain(
        place, jnp.concatenate([keep, pack_keep], axis=1), jnp.concatenate([send, pack_send], axis=1)
    )

    def both(first_array, second_array):
        mine = jnp.where(core == 0, first_array, second_array)
        other = swap(jnp.where(core == 0, second_array, first_array), "pipe")
        return in_order(core, mine, other)[None]

    activations = both(out_zero, out_one)
    input_grads = both(grad_zero, grad_one)

    chain_d.over_x()
    chains = (chain_a, chain_b, chain_c, chain_e, chain_d)
    for chain in chains[1:]:
        chain.over_y()
    for chain in chains:
        chain.rest_of_z()
        chain.back()

    done = {name: chain.finish(layer) for name, chain, layer in (
        ("a", chain_a, 1), ("b", chain_b, 1), ("c", chain_c, 0), ("e", chain_e, 0), ("d", chain_d, 0)
    )}

    def wide(zero, one, blocks):
        rows = jnp.where(core == 0, zero, one).astype(F32).reshape(2, blocks, 128, D)
        return rows.transpose(0, 2, 1, 3).reshape(1, 256, blocks * D)

    tail = chain_d.full[384:392].reshape(-1).astype(F32)
    vectors = tail[:1536].reshape(6, 1, 256)
    fc2_rows = jnp.where(core == 0, done["e"][:, :512], done["a"][:, 512:1024]).astype(F32)
    return (
        activations,
        input_grads,
        vectors[0],
        vectors[1],
        wide(done["d"][:, :384], done["b"], 3),
        tail[2560 : 2560 + TABLE * 8].reshape(1, TABLE, 8),
        wide(done["e"][:, 512:], done["a"][:, 1024:], 1),
        vectors[2],
        vectors[3],
        vectors[4],
        wide(done["c"], done["a"][:, :512], 4),
        tail[1536:2560].reshape(1, 1024),
        fc2_rows.reshape(1, 1024, D),
        vectors[5],
    )


def solution(mesh):
    return jax.shard_map(
        functools.partial(per_device, mesh.shape["rep"]),
        mesh=mesh,
        in_specs=(
            P(("group", "rep"), None, None),
            P(("group", "rep"), None, None),
            P(),
            P(),
            P(("group", "rep")),
            P("pipe", "group"),
            P("pipe", "group"),
            P("pipe", "group", None),
            P("pipe", None, "group"),
            P("pipe", "group", None),
            P("pipe", "group"),
            P("pipe", "group"),
            P("pipe", "group"),
            P("pipe", "group", None),
            P("pipe", "group"),
            P("pipe", "group", None),
            P("pipe", "group"),
        ),
        out_specs=(
            P("pipe", ("group", "rep"), None, None),
            P("pipe", ("group", "rep"), None, None),
            P("pipe", "group"),
            P("pipe", "group"),
            P("pipe", "group", None),
            P("pipe", None, "group"),
            P("pipe", "group", None),
            P("pipe", "group"),
            P("pipe", "group"),
            P("pipe", "group"),
            P("pipe", "group", None),
            P("pipe", "group"),
            P("pipe", "group", None),
            P("pipe", "group"),
        ),
        check_vma=False,
    )
```

```python
import functools

import jax
import jax.numpy as jnp
from jax import lax
from jax.experimental import pallas as pl
from jax.experimental.pallas import tpu as pltpu
from jax.sharding import PartitionSpec as P

D = 512
FF = 2048
HEADS = 16
WIN = 7
SIDE = 14
SHIFT = 3
HEAD_DIM = 32
TOK = 196
WINDOWS = 4
SLOTS = WIN * WIN
TABLE = 169
ROWS = 56
PAD = 64
IMG = WINDOWS * ROWS
PACK = 4
WIDE = PACK * HEAD_DIM
LANES = PACK * PAD
PACKS = HEADS // PACK
TILE = 512

EPSILON = 1e-05
ROOT_HALF = 0.7071067811865476
DENSITY = 0.3989422804014327
SCALE = HEAD_DIM ** (-0.5)
NEVER = -1e30
F32 = jnp.float32
BF16 = jnp.bfloat16
VMEM_LIMIT = 60 * 1024 * 1024

NN = (((1,), (0,)), ((), ()))
NT = (((1,), (1,)), ((), ()))
TN = (((0,), (0,)), ((), ()))


def mxu(left, right, dims=NN):
    return lax.dot_general(left, right, dims, preferred_element_type=F32)


def normalize(values):
    centre = jnp.mean(values, -1, keepdims=True)
    centred = values - centre
    inv_std = lax.rsqrt(jnp.mean(centred * centred, -1, keepdims=True) + EPSILON)
    return centred * inv_std, inv_std


def norm_back(grad_rows, unit_rows, inv_std, gain):
    scaled = grad_rows * gain
    average = jnp.mean(scaled, -1, keepdims=True)
    aligned = jnp.mean(scaled * unit_rows, -1, keepdims=True)
    return inv_std * (scaled - average - unit_rows * aligned)


def head_masks():
    lane = lax.broadcasted_iota(jnp.int32, (1, WIDE), 1) // HEAD_DIM
    return [(lane == h).astype(F32) for h in range(PACK)]


def spread(block, masks):
    return jnp.concatenate([block * m.astype(BF16) for m in masks], axis=0)


def collect(product, masks):
    total = product[:PAD] * masks[0]
    for h in range(1, PACK):
        total = total + product[h * PAD : (h + 1) * PAD] * masks[h]
    return total


def softmax_t(keys, queries_wide, bias):
    scores = mxu(keys, queries_wide, NT) * SCALE + bias
    weights = jnp.exp(scores - jnp.max(scores, axis=0, keepdims=True))
    return weights * (1.0 / jnp.sum(weights, axis=0, keepdims=True))


def copies(which, flags, refs, sems):
    own, other, x_own, y_own, x_other, y_other, base, target = refs
    side, low = flags[1], flags[3]
    pairs = []
    for b in range(BLOCKS):
        here = pl.ds((base + b) * 256, 256)
        pairs.append((own.at[here], other.at[here], target(side, b)))
    for over, over_other, half in ((x_own, x_other, low), (y_own, y_other, 1 - low)):
        for b in range(2):
            here = pl.ds(b * 256, 256)
            pairs.append((over.at[here], over_other.at[here], target(1 - side, 2 * half + b)))
    return [[(refs[m], refs[2], sems.at[k]) for m in range(2)] for k, refs in enumerate(pairs)]


def load_weights(which, flags, segments, sems):
    made = [copies(which, flags, refs, sems.at[k]) for k, refs in enumerate(segments)]

    @pl.when(flags[0] == which)
    def _():
        for segment in made:
            for copy, _ in segment:
                pltpu.make_async_copy(*copy).start()

    @pl.when(flags[0] != which)
    def _():
        for segment in made:
            for _, copy in segment:
                pltpu.make_async_copy(*copy).start()


def wait_weights(which, flags, segments, sems):
    for k, refs in enumerate(segments):
        for copy, _ in copies(which, flags, refs, sems.at[k]):
            pltpu.make_async_copy(*copy).wait()


def by_columns(ref):
    return lambda half, b: ref.at[b, pl.ds(pl.multiple_of(half * 256, 256), 256)]


def by_rows(ref):
    return lambda half, b: ref.at[half * BLOCKS + b]


def att_segments(refs, wqkv):
    return [tuple(refs) + (0, by_columns(wqkv))]


def mlp_segments(refs, wfc1, wfc2):
    own = tuple(refs[:2])
    return [own + tuple(refs[2:6]) + (4, by_columns(wfc1)), own + tuple(refs[6:10]) + (8, by_rows(wfc2))]


def vec(vecs, row, count=1):
    rows = [vecs[row + i : row + i + 1, :] for i in range(count)]
    return rows[0] if count == 1 else jnp.concatenate(rows, axis=1)


def attention_forward(mixed, bias, att):
    masks = head_masks()

    def image(n, carry):
        for w in range(WINDOWS):
            parts = []
            for g in range(PACKS):
                c = g * WIDE
                wide = spread(mixed[n, w, :, c : c + WIDE], masks)
                keys = mixed[n, w, :, D + c : D + c + WIDE]
                values = mixed[n, w, :, 2 * D + c : 2 * D + c + WIDE]
                probs = softmax_t(keys, wide, bias[w, :, g * LANES : (g + 1) * LANES]).astype(BF16)
                parts.append(collect(mxu(probs, values, TN), masks)[:ROWS])
            att[n, w] = jnp.concatenate(parts, axis=1)
        return carry

    lax.fori_loop(0, mixed.shape[0], image, 0)


def attention_backward(mixed, bias, datt, dmix, dscore):
    masks = head_masks()

    def image(n, carry):
        for w in range(WINDOWS):
            units = [slice(g * WIDE, (g + 1) * WIDE) for g in range(PACKS)]
            keys = [mixed[n, w, :, D + u.start : D + u.stop] for u in units]
            values = [mixed[n, w, :, 2 * D + u.start : 2 * D + u.stop] for u in units]
            wide = [spread(mixed[n, w, :, u], masks) for u in units]
            dwide = [spread(datt[n, w, :, u], masks) for u in units]
            probs = [softmax_t(k, q, bias[w, :, g * LANES : (g + 1) * LANES]) for g, (k, q) in enumerate(zip(keys, wide))]
            dprobs = [mxu(v, q, NT) for v, q in zip(values, dwide)]
            ds = []
            for p, d in zip(probs, dprobs):
                inner = jnp.sum(d * p, axis=0, keepdims=True)
                ds.append((p * (d - inner)).astype(BF16))
            dv = [mxu(p.astype(BF16), q)[:ROWS] for p, q in zip(probs, dwide)]
            dk = [mxu(s, q)[:ROWS] * SCALE for s, q in zip(ds, wide)]
            dq = [collect(mxu(s, k, TN), masks)[:ROWS] * SCALE for s, k in zip(ds, keys)]
            for g in range(PACKS):
                dscore[:, g * LANES : (g + 1) * LANES] += ds[g].astype(F32)
            dmix[n, w] = jnp.concatenate(dq + dk + dv, axis=1)
        return carry

    lax.fori_loop(0, mixed.shape[0], image, 0)


def tall(values):
    width = values.shape[-1]
    split = values.reshape(-1, ROWS, width)
    blank = jnp.zeros((split.shape[0], PAD - ROWS, width), F32)
    made = jnp.concatenate([split, blank], axis=1).astype(BF16)
    return made.reshape(-1, WINDOWS, PAD, width)


def place(perm, x):
    return jnp.concatenate([mxu(perm[...], x[n]) for n in range(x.shape[0])], axis=0)


def unplace(perm_back, rows, out, alive=None):
    for n in range(out.shape[0]):
        image = mxu(perm_back[...], rows[n * IMG : (n + 1) * IMG])
        out[n] = (image if alive is None else image * alive(n)).astype(BF16)


def flat(ref):
    return ref[...].reshape(-1, ref.shape[-1])


def attention_part(which, flags, x, perm, bias, vecs, *rest):
    residual_out, mixed, att_out, weights, att, sems = rest[6:]
    segments = att_segments(rest[:6], weights)
    first = pl.program_id(0) == 0

    @pl.when(first)
    def _():
        load_weights(which, flags, segments, sems)

    windowed = place(perm, x)
    unit, _ = normalize(windowed)
    low = (unit * vec(vecs, 0) + vec(vecs, 1)).astype(BF16)

    @pl.when(first)
    def _():
        wait_weights(which, flags, segments, sems)

    for j in range(3):
        cols = slice(j * D, (j + 1) * D)
        mixed[:, :, :, cols] = tall(mxu(low, weights[j]))
    attention_forward(mixed, bias, att)
    attended = att[...].reshape(-1, D).astype(BF16)
    att_out[...] = attended.reshape(att_out.shape)
    residual = windowed + mxu(attended, weights[3]) + vec(vecs, 2)
    residual_out[...] = residual.reshape(residual_out.shape)


def hidden_part(which, images, flags, residual_in, perm_back, vecs, *rest):
    out, act, slope, wfc1, wfc2, sems = rest[10:]
    segments = mlp_segments(rest[:10], wfc1, wfc2)
    i = pl.program_id(0)

    @pl.when(i == 0)
    def _():
        load_weights(which, flags, segments, sems)

    residual = flat(residual_in)
    unit, _ = normalize(residual)
    low = (unit * vec(vecs, 3) + vec(vecs, 4)).astype(BF16)

    @pl.when(i == 0)
    def _():
        wait_weights(which, flags, segments, sems)

    result = residual + vec(vecs, 5)
    block = act.shape[:2]
    for j in range(FF // TILE):
        cols = slice(j * TILE, (j + 1) * TILE)
        hidden = mxu(low, wfc1[j]) + vec(vecs, 6 + j)
        below = 0.5 * (1.0 + lax.erf(hidden * ROOT_HALF))
        low_act = (hidden * below).astype(BF16)
        act[:, :, cols] = low_act.reshape(block + (TILE,))
        steep = below + hidden * jnp.exp(-0.5 * hidden * hidden) * DENSITY
        slope[:, :, cols] = steep.astype(BF16).reshape(block + (TILE,))
        result = result + mxu(low_act, wfc2[2 * j : 2 * j + 2].reshape(TILE, D))
    step = out.shape[0]

    def alive(n):
        return (flags[0] * images + i * step + n < flags[2]).astype(F32)

    unplace(perm_back, result.astype(BF16), out, alive)


def split_grads(part, left, right, outs, row):
    low = left[:, pl.ds(pl.multiple_of(part * 128, 128), 128)]
    high = left[:, pl.ds(pl.multiple_of(256 + part * 128, 128), 128)]
    both = jnp.concatenate([low, high], axis=1)
    for j in range(right.shape[1] // TILE):
        product = mxu(both, right[:, j * TILE : (j + 1) * TILE], TN).astype(BF16)
        outs[0, row : row + 128, :] = product[:128]
        outs[1, row : row + 128, :] = product[128:]
        row += 128


def hidden_back(which, images, flags, residual_in, act, slope, att, og, perm, vecs, *rest):
    dres, two_keep, two_send, one_keep, one_send, sums, wfc1, wfc2, k_two, k_act, k_go, k_dh, k_att, k_dp, sems = rest[10:]
    segments = mlp_segments(rest[:10], wfc1, wfc2)
    i = pl.program_id(0)
    step = og.shape[0]

    @pl.when(i == 0)
    def _():
        load_weights(which, flags, segments, sems)
        sums[...] = jnp.zeros(sums.shape, F32)

    rows = pl.ds(pl.multiple_of(i * step * IMG, step * IMG), step * IMG)
    unit, inv_std = normalize(flat(residual_in))
    k_two[rows, :] = (unit * vec(vecs, 3) + vec(vecs, 4)).astype(BF16)
    placed = []
    for n in range(step):
        image = mxu(perm[...], og[n])
        if which == 1:
            image = image * (flags[0] * images + i * step + n < flags[2]).astype(F32)
        placed.append(image)
    grad_out = jnp.concatenate(placed, axis=0)
    go = grad_out.astype(BF16)
    k_go[rows, :] = go
    k_act[rows, :] = flat(act)

    @pl.when(i == 0)
    def _():
        wait_weights(which, flags, segments, sems)

    grad_two = jnp.zeros((step * IMG, D), F32)
    for j in range(FF // TILE):
        cols = slice(j * TILE, (j + 1) * TILE)
        steep = slope[:, :, cols].reshape(-1, TILE).astype(F32)
        dh = (mxu(go, wfc2[2 * j : 2 * j + 2].reshape(TILE, D), NT) * steep).astype(BF16)
        k_dh[rows, cols] = dh
        sums[6 + j : 7 + j, :] += jnp.sum(dh.astype(F32), axis=0, keepdims=True)
        grad_two = grad_two + mxu(dh, wfc1[j], NT)
    sums[5:6, :] += jnp.sum(grad_out, axis=0, keepdims=True)
    sums[3:4, :] += jnp.sum(grad_two * unit, axis=0, keepdims=True)
    sums[4:5, :] += jnp.sum(grad_two, axis=0, keepdims=True)
    grad = grad_out + norm_back(grad_two, unit, inv_std, vec(vecs, 3))
    dres[...] = grad.reshape(dres.shape)
    dp = grad.astype(BF16)
    sums[2:3, :] += jnp.sum(dp.astype(F32), axis=0, keepdims=True)
    k_dp[rows, :] = dp
    k_att[rows, :] = flat(att)

    @pl.when(i == pl.num_programs(0) - 1)
    def _():
        for slot, (two, one) in enumerate(((two_keep, one_keep), (two_send, one_send))):
            part = flags[0] if slot == 0 else 1 - flags[0]
            for half in range(2):
                for q in range(2):
                    left = k_act[:, pl.ds(pl.multiple_of(half * 1024 + part * 512 + q * 256, 256), 256)]
                    two[half, q * 256 : (q + 1) * 256, :] = mxu(left, k_go[...], TN).astype(BF16)
            split_grads(part, k_two, k_dh, one, 0)
            split_grads(part, k_att, k_dp, one, 512)


def attention_back(which, flags, x, mixed, dres, perm, perm_back, bias, vecs, *rest):
    dx, grads_keep, grads_send, sums, dscore, weights, datt, dmix, k_one, k_dm, sems = rest[6:]
    segments = att_segments(rest[:6], weights)
    i = pl.program_id(0)
    step = x.shape[0]

    @pl.when(i == 0)
    def _():
        load_weights(which, flags, segments, sems)
        sums[...] = jnp.zeros(sums.shape, F32)
        dscore[...] = jnp.zeros(dscore.shape, F32)

    rows = pl.ds(pl.multiple_of(i * step * IMG, step * IMG), step * IMG)
    unit, inv_std = normalize(place(perm, x))
    k_one[rows, :] = (unit * vec(vecs, 0) + vec(vecs, 1)).astype(BF16)
    dp = flat(dres).astype(BF16)

    @pl.when(i == 0)
    def _():
        wait_weights(which, flags, segments, sems)

    datt[...] = tall(mxu(dp, weights[3], NT))
    attention_backward(mixed, bias, datt, dmix, dscore)
    dm = dmix[...].reshape(-1, 3 * D).astype(BF16)
    k_dm[rows, :] = dm
    grad_one = sum(mxu(dm[:, j * D : (j + 1) * D], weights[j], NT) for j in range(3))
    sums[0:1, :] += jnp.sum(grad_one * unit, axis=0, keepdims=True)
    sums[1:2, :] += jnp.sum(grad_one, axis=0, keepdims=True)
    grad = flat(dres) + norm_back(grad_one, unit, inv_std, vec(vecs, 0))
    unplace(perm_back, grad.astype(BF16), dx)

    @pl.when(i == pl.num_programs(0) - 1)
    def _():
        for slot, out in enumerate((grads_keep, grads_send)):
            part = flags[0] if slot == 0 else 1 - flags[0]
            split_grads(part, k_one, k_dm, out, 0)


ANY = pl.BlockSpec(memory_space=pl.ANY)
BLOCKS = 4
W_ATT = [pltpu.VMEM((BLOCKS, D, D), BF16)]
W_MLP = [pltpu.VMEM((BLOCKS, D, D), BF16), pltpu.VMEM((2 * BLOCKS, 256, D), BF16)]
SEMS = [pltpu.SemaphoreType.DMA((2, 8))]
STEPS = {"attention": 2, "hidden": 2, "hidden_back": 2, "attention_back": 2}


def whole(*shape):
    return pl.BlockSpec(shape, lambda i, flags: (0,) * len(shape), pipeline_mode=pl.Buffered(1))


def block(step, *shape):
    return pl.BlockSpec((step,) + shape, lambda i, flags: (i,) + (0,) * len(shape))


def core_block(step, count):
    return pl.BlockSpec((step, TOK, D), lambda i, flags: (flags[0] * (count // step) + i, 0, 0))


def struct(kind, *shape):
    return jax.ShapeDtypeStruct(shape, kind)


def call(body, images, step, in_specs, outs, scratch, flops, name):
    return pl.pallas_call(
        body,
        grid_spec=pltpu.PrefetchScalarGridSpec(
            num_scalar_prefetch=1,
            grid=(images // step,),
            in_specs=in_specs,
            out_specs=[spec for spec, _ in outs],
            scratch_shapes=scratch,
        ),
        out_shape=[shape for _, shape in outs],
        compiler_params=pltpu.CompilerParams(vmem_limit_bytes=VMEM_LIMIT, dimension_semantics=("arbitrary",)),
        cost_estimate=pl.CostEstimate(flops=flops * images, bytes_accessed=20_000_000, transcendentals=0),
        name=name,
    )


def step_of(name, images):
    step = STEPS[name]
    return step if images % step == 0 else 1


BIAS = (WINDOWS, PAD, HEADS * PAD)
MIXED = (WINDOWS, PAD, 3 * D)


def run_attention(which, flags, x, shared, weights, images):
    step = step_of("attention", images)
    perm, _, bias, vecs = shared
    entry = core_block(step, images) if which == 0 else block(step, TOK, D)
    return call(
        functools.partial(attention_part, which),
        images,
        step,
        [entry, whole(IMG, TOK), whole(*BIAS), whole(16, D)] + [ANY] * 6,
        [
            (block(step, IMG, D), struct(F32, images, IMG, D)),
            (block(step, *MIXED), struct(BF16, images, *MIXED)),
            (block(step, IMG, D), struct(BF16, images, IMG, D)),
        ],
        W_ATT + [pltpu.VMEM((step, WINDOWS, ROWS, D), F32)] + SEMS,
        800_000_000,
        "layer%d_attention" % which,
    )(flags, x, perm, bias, vecs, *weights)


def run_hidden(which, flags, residual, shared, weights, images):
    step = step_of("hidden", images)
    _, perm_back, _, vecs = shared
    return call(
        functools.partial(hidden_part, which, images),
        images,
        step,
        [block(step, IMG, D), whole(TOK, IMG), whole(16, D)] + [ANY] * 10,
        [
            (block(step, TOK, D), struct(BF16, images, TOK, D)),
            (block(step, IMG, FF), struct(BF16, images, IMG, FF)),
            (block(step, IMG, FF), struct(BF16, images, IMG, FF)),
        ],
        W_MLP + SEMS,
        1_000_000_000,
        "layer%d_hidden" % which,
    )(flags, residual, perm_back, vecs, *weights)


def run_hidden_back(which, flags, residual, act, slope, att, og, shared, weights, images):
    step = step_of("hidden_back", images)
    perm, _, _, vecs = shared
    rows = images * IMG
    cotangent = block(step, TOK, D) if which == 0 else core_block(step, images)
    return call(
        functools.partial(hidden_back, which, images),
        images,
        step,
        [block(step, IMG, D), block(step, IMG, FF), block(step, IMG, FF), block(step, IMG, D), cotangent]
        + [whole(IMG, TOK), whole(16, D)]
        + [ANY] * 10,
        [
            (block(step, IMG, D), struct(F32, images, IMG, D)),
            (whole(2, 512, D), struct(BF16, 2, 512, D)),
            (whole(2, 512, D), struct(BF16, 2, 512, D)),
            (whole(2, 640, D), struct(BF16, 2, 640, D)),
            (whole(2, 640, D), struct(BF16, 2, 640, D)),
            (whole(16, D), struct(F32, 16, D)),
        ],
        W_MLP + [pltpu.VMEM((rows, width), BF16) for width in (D, FF, D, FF, D, D)] + SEMS,
        2_000_000_000,
        "layer%d_hidden_back" % which,
    )(flags, residual, act, slope, att, og, perm, vecs, *weights)


def run_attention_back(which, flags, x, mixed, dres, shared, weights, images):
    step = step_of("attention_back", images)
    perm, perm_back, bias, vecs = shared
    rows = images * IMG
    entry = core_block(step, images) if which == 0 else block(step, TOK, D)
    return call(
        functools.partial(attention_back, which),
        images,
        step,
        [entry, block(step, *MIXED), block(step, IMG, D)]
        + [whole(IMG, TOK), whole(TOK, IMG), whole(*BIAS), whole(16, D)]
        + [ANY] * 6,
        [
            (block(step, TOK, D), struct(BF16, images, TOK, D)),
            (whole(2, 384, D), struct(BF16, 2, 384, D)),
            (whole(2, 384, D), struct(BF16, 2, 384, D)),
            (whole(16, D), struct(F32, 16, D)),
            (whole(PAD, HEADS * PAD), struct(F32, PAD, HEADS * PAD)),
        ],
        W_ATT
        + [pltpu.VMEM((step, WINDOWS, PAD, D), BF16), pltpu.VMEM((step, WINDOWS, ROWS, 3 * D), F32)]
        + [pltpu.VMEM((rows, width), BF16) for width in (D, 3 * D)]
        + SEMS,
        2_000_000_000,
        "layer%d_attention_back" % which,
    )(flags, x, mixed, dres, perm, perm_back, bias, vecs, *weights)


def choose(flags, zero, one, target, sems):
    rows = target.shape[1]

    def start(refs, order):
        for m in range(2):
            pltpu.make_async_copy(refs[m].at[pl.ds(0, rows)], target.at[order[m]], sems.at[m]).start()

    @pl.when(flags[0] == 0)
    def _():
        start(zero, (0, 1))

    @pl.when(flags[0] != 0)
    def _():
        start(one, (1, 0))


def arrived(zero, target, sems):
    rows = target.shape[1]
    for m in range(2):
        pltpu.make_async_copy(zero[m].at[pl.ds(0, rows)], target.at[m], sems.at[m]).wait()


def assemble_mlp(flags, *refs):
    two_zero, one_zero, two_one, one_one = (refs[2 * k : 2 * k + 2] for k in range(4))
    fc1_out, fc2_out, proj_out, two, one, sems = refs[8:]
    choose(flags, two_zero, two_one, two, sems.at[0])
    choose(flags, one_zero, one_one, one, sems.at[1])
    arrived(two_zero, two, sems.at[0])
    fc2_out[0] = two[...].reshape(1024, D).astype(F32)
    arrived(one_zero, one, sems.at[1])
    for part in range(2):
        rows = slice(part * 128, (part + 1) * 128)
        for j in range(FF // TILE):
            fc1_out[0, rows, j * TILE : (j + 1) * TILE] = one[part, j * 128 : (j + 1) * 128, :].astype(F32)
        proj_out[0, rows, :] = one[part, 512:640, :].astype(F32)


def assemble_qkv(flags, *refs):
    zero, one = refs[:2], refs[2:4]
    out, parts, sems = refs[4:]
    choose(flags, zero, one, parts, sems)
    arrived(zero, parts, sems)
    for part in range(2):
        for j in range(3):
            out[0, part * 128 : (part + 1) * 128, j * D : (j + 1) * D] = parts[part, j * 128 : (j + 1) * 128, :].astype(F32)


def assemble(body, flags, arrays, shapes, scratch, name):
    return pl.pallas_call(
        body,
        grid_spec=pltpu.PrefetchScalarGridSpec(
            num_scalar_prefetch=1,
            grid=(1,),
            in_specs=[ANY] * len(arrays),
            out_specs=[whole(*shape) for shape in shapes],
            scratch_shapes=scratch,
        ),
        out_shape=[struct(F32, *shape) for shape in shapes],
        compiler_params=pltpu.CompilerParams(vmem_limit_bytes=VMEM_LIMIT),
        cost_estimate=pl.CostEstimate(flops=0, bytes_accessed=8_000_000, transcendentals=0),
        name=name,
    )(flags, *arrays)


def run_assemble_mlp(flags, arrays):
    shapes = [(1, 256, FF), (1, 1024, D), (1, 256, D)]
    scratch = [pltpu.VMEM((2, 512, D), BF16), pltpu.VMEM((2, 640, D), BF16), pltpu.SemaphoreType.DMA((2, 2))]
    return assemble(assemble_mlp, flags, arrays, shapes, scratch, "assemble_mlp")


def run_assemble_qkv(flags, arrays):
    scratch = [pltpu.VMEM((2, 384, D), BF16), pltpu.SemaphoreType.DMA((2,))]
    return assemble(assemble_qkv, flags, arrays, [(1, 256, 3 * D)], scratch, "assemble_qkv")


SWAP = [(0, 1), (1, 0)]


def swap(array, axis):
    return lax.ppermute(array, axis, SWAP)


def relative_onehot():
    t = jnp.arange(PAD, dtype=jnp.int32)[:, None]
    s = jnp.arange(PAD, dtype=jnp.int32)[None, :]
    relative = (s // WIN - t // WIN + WIN - 1) * (2 * WIN - 1) + s % WIN - t % WIN + WIN - 1
    relative = jnp.where((t < SLOTS) & (s < SLOTS), relative, -1).reshape(-1)
    return relative[None, :] == jnp.arange(TABLE, dtype=jnp.int32)[:, None]


def geometry(window_order, regions, layer):
    offset = layer * SHIFT
    source = (window_order // SIDE + offset) % SIDE * SIDE + (window_order % SIDE + offset) % SIDE
    padded = jnp.pad(source.reshape(WINDOWS, SLOTS), ((0, 0), (0, ROWS - SLOTS)), constant_values=-1).reshape(-1)
    places = jnp.arange(TOK, dtype=jnp.int32)
    perm = (padded[:, None] == places[None, :]).astype(BF16)
    perm_back = (places[:, None] == padded[None, :]).astype(BF16)
    masking = jnp.zeros((WINDOWS, PAD, PAD), F32)
    if layer:
        hits = window_order[:, None] == places[None, :]
        region = jnp.sum(jnp.where(hits, regions[None, :], 0), axis=1).reshape(WINDOWS, SLOTS)
        region = jnp.pad(region, ((0, 0), (0, PAD - SLOTS)))
        masking = jnp.where(region[:, :, None] != region[:, None, :], -100.0 * layer, 0.0)
    masking = jnp.where(jnp.arange(PAD)[None, :, None] < SLOTS, masking, NEVER)
    return perm, perm_back, masking.astype(F32)


def bias_of(table, masking):
    spread_bias = jnp.dot(table.T, relative_onehot().astype(BF16), preferred_element_type=F32)
    spread_bias = spread_bias.reshape(HEADS, PAD, PAD).transpose(1, 0, 2)
    return (spread_bias[None] + masking[:, :, None, :]).reshape(WINDOWS, PAD, HEADS * PAD)


def pick(array, index):
    return lax.dynamic_index_in_dim(array, index, 0, keepdims=False)


def after(values, *others):
    return lax.optimization_barrier((values, others))[0]


class Place:
    def __init__(self, replicas):
        self.replicas = replicas
        self.core = lax.axis_index("pipe")
        self.side = lax.axis_index("group")
        self.low = lax.axis_index("rep") % 2

    def trade(self, array, bit):
        return lax.ppermute(array, "rep", [(r, r ^ bit) for r in range(self.replicas)])


def in_order(flag, mine, other):
    return jnp.where(flag == 0, jnp.concatenate([mine, other]), jnp.concatenate([other, mine]))


class Chain:
    def __init__(self, place, keep, send, *beside):
        self.place, self.keep, self.rows = place, keep, keep.shape[1]
        if beside:
            send = after(send, *[chain.arrived for chain in beside])
        self.got = swap(send, "pipe")

    def ready_x(self):
        side = self.place.side
        self.sent = (pick(self.keep, 1 - side).astype(F32) + pick(self.got, 1 - side)).astype(BF16)
        self.move = lambda array: swap(array, "group")
        return self

    def ready_y(self):
        place = self.place
        total = pick(self.keep, place.side).astype(F32) + pick(self.got, place.side) + self.arrived
        total = total.reshape(2, self.rows // 2, D)
        self.sent, self.here = pick(total, 1 - place.low).astype(BF16), pick(total, place.low)
        self.move = lambda array: place.trade(array, 1)
        self.bit = 1
        return self

    def ready_z(self):
        self.sent = self.here = self.sum()
        self.bit *= 2
        self.move = lambda array: self.place.trade(array, self.bit)
        return self

    def sum(self):
        return (self.here.astype(F32) + self.arrived.astype(F32)).astype(BF16)

    def send(self):
        self.arrived = self.move(self.sent)

    def rest_of_z(self):
        while 2 * self.bit < self.place.replicas:
            self.ready_z().send()

    def back(self):
        total = self.sum()
        self.full = in_order(self.place.low, total, self.place.trade(total, 1))

    def finish(self, layer):
        return self.full, lax.ppermute(self.full, "pipe", [(1 - layer, layer)])


def send_before(flags, *chains):
    flags, sent = lax.optimization_barrier((flags, [chain.sent for chain in chains]))
    for chain, array in zip(chains, sent):
        chain.sent = array
        chain.send()
    return flags


def blocks_of(array):
    return jnp.concatenate([array[:, c : c + D] for c in range(0, array.shape[1], D)], axis=0)


def per_device(replicas, images, out_grad, window_order, regions, counts, *params):
    place = Place(replicas)
    core, side = place.core, place.side
    count = images.shape[0] // 2
    flags = jnp.stack([core, side, counts[0], place.low]).astype(jnp.int32)
    (gain_one, shift_one, qkv, table, proj, proj_shift, gain_two, shift_two, fc1, fc1_shift, fc2, fc2_shift) = params

    vectors = [gain_one, shift_one, proj_shift, gain_two, shift_two, fc2_shift, fc1_shift, table]
    small = jnp.concatenate([v.reshape(-1) for v in vectors])
    small = jnp.pad(small, (0, 16 * D - small.shape[0])).reshape(16, D)
    parts = [jnp.concatenate([blocks_of(qkv[0]), proj[0]], axis=0), blocks_of(fc1[0]), fc2[0]]
    halves = [lax.dynamic_slice_in_dim(part, place.low * 512, 512, 0) for part in parts]
    over_x = [swap(halves[0], "group")]
    own = jnp.concatenate(parts, axis=0)
    own_other = swap(own, "pipe")
    small_x = swap(small, "group")
    small_both = jnp.concatenate([small, small_x], axis=0)
    small_other = swap(small_both, "pipe")
    over_x.append(swap(after(halves[1], over_x[0]), "group"))
    over_x.append(swap(after(halves[2], over_x[1]), "group"))
    over_y = [place.trade(over_x[0], 1), place.trade(over_x[1], 1)]
    att_weights = (own, own_other, over_x[0], over_y[0], swap(over_x[0], "pipe"), swap(over_y[0], "pipe"))

    shared = []
    for layer in range(2):
        chosen = jnp.where(core == layer, small_both, small_other).reshape(2, -1)
        pair = jnp.where(side == 0, chosen, chosen[::-1])
        six = pair[:, :1536].reshape(2, 6, 256).transpose(1, 0, 2).reshape(6, D)
        vecs = jnp.concatenate([six, pair[:, 1536:2560].reshape(4, D), jnp.zeros((6, D), BF16)]).astype(F32)
        joined = pair[:, 2560 : 2560 + TABLE * 8].reshape(2, TABLE, 8).transpose(1, 0, 2).reshape(TABLE, HEADS)
        perm, perm_back, masking = geometry(window_order, regions, layer)
        shared.append((perm, perm_back, bias_of(joined, masking), vecs))

    residual_zero, mixed_zero, attended_zero = run_attention(
        0, after(flags, over_x[1]), images, shared[0], att_weights, count
    )
    over_y.append(place.trade(after(over_x[2], residual_zero), 1))
    mlp_weights = (own, own_other)
    for k in (1, 2):
        mlp_weights += (over_x[k], over_y[k], swap(after(over_x[k], residual_zero), "pipe"), swap(after(over_y[k], residual_zero), "pipe"))
    out_zero, act_zero, slope_zero = run_hidden(0, flags, residual_zero, shared[0], mlp_weights, count)
    residual_one, mixed_one, attended_one = run_attention(1, flags, out_zero, shared[1], att_weights, count)
    out_one, act_one, slope_one = run_hidden(1, flags, residual_one, shared[1], mlp_weights, count)
    dres_one, two_keep, two_send, one_keep, one_send, sums_mlp_one = run_hidden_back(
        1, flags, residual_one, act_one, slope_one, attended_one, out_grad, shared[1], mlp_weights, count
    )
    first_two, first_one = Chain(place, two_keep, two_send), Chain(place, one_keep, one_send)
    tied = send_before(flags, first_two.ready_x(), first_one.ready_x())
    grad_one, keep, send, sums_att_one, score_one = run_attention_back(
        1, tied, out_zero, mixed_one, dres_one, shared[1], att_weights, count
    )
    first_qkv = Chain(place, keep, send, first_two, first_one)
    tied = send_before(flags, first_two.ready_y(), first_one.ready_y(), first_qkv.ready_x())
    dres_zero, two_keep, two_send, one_keep, one_send, sums_mlp_zero = run_hidden_back(
        0, tied, residual_zero, act_zero, slope_zero, attended_zero, grad_one, shared[0], mlp_weights, count
    )
    beside = (first_two, first_one, first_qkv)
    last_two, last_one = Chain(place, two_keep, two_send, *beside), Chain(place, one_keep, one_send, *beside)
    tied = send_before(
        flags, last_two.ready_x(), last_one.ready_x(), first_two.ready_z(), first_one.ready_z(), first_qkv.ready_y()
    )
    grad_zero, keep, send, sums_att_zero, score_zero = run_attention_back(
        0, tied, images, mixed_zero, dres_zero, shared[0], att_weights, count
    )

    def packed(sums, score):
        lookup = relative_onehot().astype(F32)
        flat_score = score.reshape(PAD, HEADS, PAD).transpose(1, 0, 2).reshape(HEADS, PAD * PAD)
        grad_table = lax.dot_general(lookup, flat_score, NT, precision=lax.Precision.HIGHEST)
        halves = [
            sums[:6].reshape(6, 2, 256).transpose(1, 0, 2).reshape(2, 1536),
            sums[6:10].reshape(2, 1024),
            grad_table.reshape(TABLE, 2, 8).transpose(1, 0, 2).reshape(2, TABLE * 8),
            jnp.zeros((2, 8 * D - 1536 - 1024 - TABLE * 8), F32),
        ]
        return jnp.concatenate(halves, axis=1).astype(BF16).reshape(2, 8, D)

    pack_zero = packed(sums_mlp_zero + sums_att_zero, score_zero)
    pack_one = packed(sums_mlp_one + sums_att_one, score_one)
    pack_keep = jnp.where(core == 0, pack_zero, pack_one)
    pack_send = jnp.where(core == 0, pack_one, pack_zero)
    last_qkv = Chain(
        place,
        jnp.concatenate([keep, pack_keep], axis=1),
        jnp.concatenate([send, pack_send], axis=1),
        last_two,
        last_one,
        *beside,
    )

    def both(first_array, second_array):
        mine = jnp.where(core == 0, first_array, second_array)
        other = swap(jnp.where(core == 0, second_array, first_array), "pipe")
        return in_order(core, mine, other)[None]

    activations = both(out_zero, out_one)
    input_grads = both(grad_zero, grad_one)

    last_qkv.ready_x().send()
    for chain in (last_two, last_one, last_qkv):
        chain.ready_y().send()
    for chain in (first_two, first_one, first_qkv, last_two, last_one, last_qkv):
        chain.rest_of_z()
        chain.back()
    fc1_out, fc2_out, proj_out = run_assemble_mlp(
        flags, last_two.finish(0) + last_one.finish(0) + first_two.finish(1) + first_one.finish(1)
    )
    (qkv_out,) = run_assemble_qkv(flags, last_qkv.finish(0) + first_qkv.finish(1))
    tail = last_qkv.full[384:392].reshape(-1).astype(F32)
    vectors = tail[:1536].reshape(6, 1, 256)
    return (
        activations,
        input_grads,
        vectors[0],
        vectors[1],
        qkv_out,
        tail[2560 : 2560 + TABLE * 8].reshape(1, TABLE, 8),
        proj_out,
        vectors[2],
        vectors[3],
        vectors[4],
        fc1_out,
        tail[1536:2560].reshape(1, 1024),
        fc2_out,
        vectors[5],
    )


def solution(mesh):
    return jax.shard_map(
        functools.partial(per_device, mesh.shape["rep"]),
        mesh=mesh,
        in_specs=(
            P(("group", "rep"), None, None),
            P(("group", "rep"), None, None),
            P(),
            P(),
            P(("group", "rep")),
            P("pipe", "group"),
            P("pipe", "group"),
            P("pipe", "group", None),
            P("pipe", None, "group"),
            P("pipe", "group", None),
            P("pipe", "group"),
            P("pipe", "group"),
            P("pipe", "group"),
            P("pipe", "group", None),
            P("pipe", "group"),
            P("pipe", "group", None),
            P("pipe", "group"),
        ),
        out_specs=(
            P("pipe", ("group", "rep"), None, None),
            P("pipe", ("group", "rep"), None, None),
            P("pipe", "group"),
            P("pipe", "group"),
            P("pipe", "group", None),
            P("pipe", None, "group"),
            P("pipe", "group", None),
            P("pipe", "group"),
            P("pipe", "group"),
            P("pipe", "group"),
            P("pipe", "group", None),
            P("pipe", "group"),
            P("pipe", "group", None),
            P("pipe", "group"),
        ),
        check_vma=False,
    )
```

```python
import functools

import jax
import jax.numpy as jnp
from jax import lax
from jax.experimental import pallas as pl
from jax.experimental.pallas import tpu as pltpu
from jax.sharding import PartitionSpec as P

D = 512
FF = 2048
HEADS = 16
WIN = 7
SIDE = 14
SHIFT = 3
HEAD_DIM = 32
TOK = 196
WINDOWS = 4
SLOTS = WIN * WIN
TABLE = 169
ROWS = 56
PAD = 64
IMG = WINDOWS * ROWS
PACK = 4
WIDE = PACK * HEAD_DIM
LANES = PACK * PAD
PACKS = HEADS // PACK
TILE = 512

EPSILON = 1e-05
ROOT_HALF = 0.7071067811865476
DENSITY = 0.3989422804014327
SCALE = HEAD_DIM ** (-0.5)
NEVER = -1e30
F32 = jnp.float32
BF16 = jnp.bfloat16
VMEM_LIMIT = 60 * 1024 * 1024

NN = (((1,), (0,)), ((), ()))
NT = (((1,), (1,)), ((), ()))
TN = (((0,), (0,)), ((), ()))


def mxu(left, right, dims=NN):
    return lax.dot_general(left, right, dims, preferred_element_type=F32)


def normalize(values):
    centre = jnp.mean(values, -1, keepdims=True)
    centred = values - centre
    inv_std = lax.rsqrt(jnp.mean(centred * centred, -1, keepdims=True) + EPSILON)
    return centred * inv_std, inv_std


def norm_back(grad_rows, unit_rows, inv_std, gain):
    scaled = grad_rows * gain
    average = jnp.mean(scaled, -1, keepdims=True)
    aligned = jnp.mean(scaled * unit_rows, -1, keepdims=True)
    return inv_std * (scaled - average - unit_rows * aligned)


def head_masks():
    lane = lax.broadcasted_iota(jnp.int32, (1, WIDE), 1) // HEAD_DIM
    return [(lane == h).astype(F32) for h in range(PACK)]


def spread(block, masks):
    return jnp.concatenate([block * m.astype(BF16) for m in masks], axis=0)


def collect(product, masks):
    total = product[:PAD] * masks[0]
    for h in range(1, PACK):
        total = total + product[h * PAD : (h + 1) * PAD] * masks[h]
    return total


def softmax_t(keys, queries_wide, bias):
    scores = mxu(keys, queries_wide, NT) * SCALE + bias
    weights = jnp.exp(scores - jnp.max(scores, axis=0, keepdims=True))
    return weights * (1.0 / jnp.sum(weights, axis=0, keepdims=True))


def copies(which, flags, refs, sems):
    own, other, x_own, y_own, x_other, y_other, base, target = refs
    side, low = flags[1], flags[3]
    pairs = []
    for b in range(BLOCKS):
        here = pl.ds((base + b) * 256, 256)
        pairs.append((own.at[here], other.at[here], target(side, b)))
    for over, over_other, half in ((x_own, x_other, low), (y_own, y_other, 1 - low)):
        for b in range(2):
            here = pl.ds(b * 256, 256)
            pairs.append((over.at[here], over_other.at[here], target(1 - side, 2 * half + b)))
    return [[(refs[m], refs[2], sems.at[k]) for m in range(2)] for k, refs in enumerate(pairs)]


def load_weights(which, flags, segments, sems):
    made = [copies(which, flags, refs, sems.at[k]) for k, refs in enumerate(segments)]

    @pl.when(flags[0] == which)
    def _():
        for segment in made:
            for copy, _ in segment:
                pltpu.make_async_copy(*copy).start()

    @pl.when(flags[0] != which)
    def _():
        for segment in made:
            for _, copy in segment:
                pltpu.make_async_copy(*copy).start()


def wait_weights(which, flags, segments, sems):
    for k, refs in enumerate(segments):
        for copy, _ in copies(which, flags, refs, sems.at[k]):
            pltpu.make_async_copy(*copy).wait()


def by_columns(ref):
    return lambda half, b: ref.at[b, pl.ds(pl.multiple_of(half * 256, 256), 256)]


def by_rows(ref):
    return lambda half, b: ref.at[half * BLOCKS + b]


def att_segments(refs, wqkv):
    return [tuple(refs) + (0, by_columns(wqkv))]


def mlp_segments(refs, wfc1, wfc2):
    own = tuple(refs[:2])
    return [own + tuple(refs[2:6]) + (4, by_columns(wfc1)), own + tuple(refs[6:10]) + (8, by_rows(wfc2))]


def vec(vecs, row, count=1):
    rows = [vecs[row + i : row + i + 1, :] for i in range(count)]
    return rows[0] if count == 1 else jnp.concatenate(rows, axis=1)


def attention_forward(mixed, bias, att):
    masks = head_masks()

    def image(n, carry):
        for w in range(WINDOWS):
            parts = []
            for g in range(PACKS):
                c = g * WIDE
                wide = spread(mixed[n, w, :, c : c + WIDE], masks)
                keys = mixed[n, w, :, D + c : D + c + WIDE]
                values = mixed[n, w, :, 2 * D + c : 2 * D + c + WIDE]
                probs = softmax_t(keys, wide, bias[w, :, g * LANES : (g + 1) * LANES]).astype(BF16)
                parts.append(collect(mxu(probs, values, TN), masks)[:ROWS])
            att[n, w] = jnp.concatenate(parts, axis=1)
        return carry

    lax.fori_loop(0, mixed.shape[0], image, 0)


def attention_backward(mixed, bias, datt, dmix, dscore):
    masks = head_masks()

    def image(n, carry):
        for w in range(WINDOWS):
            units = [slice(g * WIDE, (g + 1) * WIDE) for g in range(PACKS)]
            keys = [mixed[n, w, :, D + u.start : D + u.stop] for u in units]
            values = [mixed[n, w, :, 2 * D + u.start : 2 * D + u.stop] for u in units]
            wide = [spread(mixed[n, w, :, u], masks) for u in units]
            dwide = [spread(datt[n, w, :, u], masks) for u in units]
            probs = [softmax_t(k, q, bias[w, :, g * LANES : (g + 1) * LANES]) for g, (k, q) in enumerate(zip(keys, wide))]
            dprobs = [mxu(v, q, NT) for v, q in zip(values, dwide)]
            ds = []
            for p, d in zip(probs, dprobs):
                inner = jnp.sum(d * p, axis=0, keepdims=True)
                ds.append((p * (d - inner)).astype(BF16))
            dv = [mxu(p.astype(BF16), q)[:ROWS] for p, q in zip(probs, dwide)]
            dk = [mxu(s, q)[:ROWS] * SCALE for s, q in zip(ds, wide)]
            dq = [collect(mxu(s, k, TN), masks)[:ROWS] * SCALE for s, k in zip(ds, keys)]
            for g in range(PACKS):
                dscore[:, g * LANES : (g + 1) * LANES] += ds[g].astype(F32)
            dmix[n, w] = jnp.concatenate(dq + dk + dv, axis=1)
        return carry

    lax.fori_loop(0, mixed.shape[0], image, 0)


def tall(values):
    width = values.shape[-1]
    split = values.reshape(-1, ROWS, width)
    blank = jnp.zeros((split.shape[0], PAD - ROWS, width), F32)
    made = jnp.concatenate([split, blank], axis=1).astype(BF16)
    return made.reshape(-1, WINDOWS, PAD, width)


def place(perm, x):
    return jnp.concatenate([mxu(perm[...], x[n]) for n in range(x.shape[0])], axis=0)


def unplace(perm_back, rows, out, alive=None):
    for n in range(out.shape[0]):
        image = mxu(perm_back[...], rows[n * IMG : (n + 1) * IMG])
        out[n] = (image if alive is None else image * alive(n)).astype(BF16)


def flat(ref):
    return ref[...].reshape(-1, ref.shape[-1])


def attention_part(which, flags, x, perm, bias, vecs, *rest):
    residual_out, mixed, att_out, weights, att, sems = rest[6:]
    segments = att_segments(rest[:6], weights)
    first = pl.program_id(0) == 0

    @pl.when(first)
    def _():
        load_weights(which, flags, segments, sems)

    windowed = place(perm, x)
    unit, _ = normalize(windowed)
    low = (unit * vec(vecs, 0) + vec(vecs, 1)).astype(BF16)

    @pl.when(first)
    def _():
        wait_weights(which, flags, segments, sems)

    for j in range(3):
        cols = slice(j * D, (j + 1) * D)
        mixed[:, :, :, cols] = tall(mxu(low, weights[j]))
    attention_forward(mixed, bias, att)
    attended = att[...].reshape(-1, D).astype(BF16)
    att_out[...] = attended.reshape(att_out.shape)
    residual = windowed + mxu(attended, weights[3]) + vec(vecs, 2)
    residual_out[...] = residual.reshape(residual_out.shape)


def hidden_part(which, images, flags, residual_in, perm_back, vecs, *rest):
    out, act, slope, wfc1, wfc2, sems = rest[10:]
    segments = mlp_segments(rest[:10], wfc1, wfc2)
    i = pl.program_id(0)

    @pl.when(i == 0)
    def _():
        load_weights(which, flags, segments, sems)

    residual = flat(residual_in)
    unit, _ = normalize(residual)
    low = (unit * vec(vecs, 3) + vec(vecs, 4)).astype(BF16)

    @pl.when(i == 0)
    def _():
        wait_weights(which, flags, segments, sems)

    result = residual + vec(vecs, 5)
    block = act.shape[:2]
    for j in range(FF // TILE):
        cols = slice(j * TILE, (j + 1) * TILE)
        hidden = mxu(low, wfc1[j]) + vec(vecs, 6 + j)
        below = 0.5 * (1.0 + lax.erf(hidden * ROOT_HALF))
        low_act = (hidden * below).astype(BF16)
        act[:, :, cols] = low_act.reshape(block + (TILE,))
        steep = below + hidden * jnp.exp(-0.5 * hidden * hidden) * DENSITY
        slope[:, :, cols] = steep.astype(BF16).reshape(block + (TILE,))
        result = result + mxu(low_act, wfc2[2 * j : 2 * j + 2].reshape(TILE, D))
    step = out.shape[0]

    def alive(n):
        return (flags[0] * images + i * step + n < flags[2]).astype(F32)

    unplace(perm_back, result.astype(BF16), out, alive)


def split_grads(part, left, right, outs, row):
    low = left[:, pl.ds(pl.multiple_of(part * 128, 128), 128)]
    high = left[:, pl.ds(pl.multiple_of(256 + part * 128, 128), 128)]
    both = jnp.concatenate([low, high], axis=1)
    for j in range(right.shape[1] // TILE):
        product = mxu(both, right[:, j * TILE : (j + 1) * TILE], TN).astype(BF16)
        outs[0, row : row + 128, :] = product[:128]
        outs[1, row : row + 128, :] = product[128:]
        row += 128


def hidden_back(which, images, flags, residual_in, act, slope, att, og, perm, vecs, *rest):
    dres, two_keep, two_send, one_keep, one_send, sums, wfc1, wfc2, k_two, k_act, k_go, k_dh, k_att, k_dp, sems = rest[10:]
    segments = mlp_segments(rest[:10], wfc1, wfc2)
    i = pl.program_id(0)
    step = og.shape[0]

    @pl.when(i == 0)
    def _():
        load_weights(which, flags, segments, sems)
        sums[...] = jnp.zeros(sums.shape, F32)

    rows = pl.ds(pl.multiple_of(i * step * IMG, step * IMG), step * IMG)
    unit, inv_std = normalize(flat(residual_in))
    k_two[rows, :] = (unit * vec(vecs, 3) + vec(vecs, 4)).astype(BF16)
    placed = []
    for n in range(step):
        image = mxu(perm[...], og[n])
        if which == 1:
            image = image * (flags[0] * images + i * step + n < flags[2]).astype(F32)
        placed.append(image)
    grad_out = jnp.concatenate(placed, axis=0)
    go = grad_out.astype(BF16)
    k_go[rows, :] = go
    k_act[rows, :] = flat(act)

    @pl.when(i == 0)
    def _():
        wait_weights(which, flags, segments, sems)

    grad_two = jnp.zeros((step * IMG, D), F32)
    for j in range(FF // TILE):
        cols = slice(j * TILE, (j + 1) * TILE)
        steep = slope[:, :, cols].reshape(-1, TILE).astype(F32)
        dh = (mxu(go, wfc2[2 * j : 2 * j + 2].reshape(TILE, D), NT) * steep).astype(BF16)
        k_dh[rows, cols] = dh
        sums[6 + j : 7 + j, :] += jnp.sum(dh.astype(F32), axis=0, keepdims=True)
        grad_two = grad_two + mxu(dh, wfc1[j], NT)
    sums[5:6, :] += jnp.sum(grad_out, axis=0, keepdims=True)
    sums[3:4, :] += jnp.sum(grad_two * unit, axis=0, keepdims=True)
    sums[4:5, :] += jnp.sum(grad_two, axis=0, keepdims=True)
    grad = grad_out + norm_back(grad_two, unit, inv_std, vec(vecs, 3))
    dres[...] = grad.reshape(dres.shape)
    dp = grad.astype(BF16)
    sums[2:3, :] += jnp.sum(dp.astype(F32), axis=0, keepdims=True)
    k_dp[rows, :] = dp
    k_att[rows, :] = flat(att)

    @pl.when(i == pl.num_programs(0) - 1)
    def _():
        for slot, (two, one) in enumerate(((two_keep, one_keep), (two_send, one_send))):
            part = flags[0] if slot == 0 else 1 - flags[0]
            for half in range(2):
                for q in range(2):
                    left = k_act[:, pl.ds(pl.multiple_of(half * 1024 + part * 512 + q * 256, 256), 256)]
                    two[half, q * 256 : (q + 1) * 256, :] = mxu(left, k_go[...], TN).astype(BF16)
            split_grads(part, k_two, k_dh, one, 0)
            split_grads(part, k_att, k_dp, one, 512)


def attention_back(which, flags, x, mixed, dres, perm, perm_back, bias, vecs, *rest):
    dx, grads_keep, grads_send, sums, dscore, weights, datt, dmix, k_one, k_dm, sems = rest[6:]
    segments = att_segments(rest[:6], weights)
    i = pl.program_id(0)
    step = x.shape[0]

    @pl.when(i == 0)
    def _():
        load_weights(which, flags, segments, sems)
        sums[...] = jnp.zeros(sums.shape, F32)
        dscore[...] = jnp.zeros(dscore.shape, F32)

    rows = pl.ds(pl.multiple_of(i * step * IMG, step * IMG), step * IMG)
    unit, inv_std = normalize(place(perm, x))
    k_one[rows, :] = (unit * vec(vecs, 0) + vec(vecs, 1)).astype(BF16)
    dp = flat(dres).astype(BF16)

    @pl.when(i == 0)
    def _():
        wait_weights(which, flags, segments, sems)

    datt[...] = tall(mxu(dp, weights[3], NT))
    attention_backward(mixed, bias, datt, dmix, dscore)
    dm = dmix[...].reshape(-1, 3 * D).astype(BF16)
    k_dm[rows, :] = dm
    grad_one = sum(mxu(dm[:, j * D : (j + 1) * D], weights[j], NT) for j in range(3))
    sums[0:1, :] += jnp.sum(grad_one * unit, axis=0, keepdims=True)
    sums[1:2, :] += jnp.sum(grad_one, axis=0, keepdims=True)
    grad = flat(dres) + norm_back(grad_one, unit, inv_std, vec(vecs, 0))
    unplace(perm_back, grad.astype(BF16), dx)

    @pl.when(i == pl.num_programs(0) - 1)
    def _():
        for slot, out in enumerate((grads_keep, grads_send)):
            part = flags[0] if slot == 0 else 1 - flags[0]
            split_grads(part, k_one, k_dm, out, 0)


ANY = pl.BlockSpec(memory_space=pl.ANY)
BLOCKS = 4
W_ATT = [pltpu.VMEM((BLOCKS, D, D), BF16)]
W_MLP = [pltpu.VMEM((BLOCKS, D, D), BF16), pltpu.VMEM((2 * BLOCKS, 256, D), BF16)]
SEMS = [pltpu.SemaphoreType.DMA((2, 8))]
STEPS = {"attention": 2, "hidden": 2, "hidden_back": 2, "attention_back": 2}


def whole(*shape):
    return pl.BlockSpec(shape, lambda i, flags: (0,) * len(shape), pipeline_mode=pl.Buffered(1))


def block(step, *shape):
    return pl.BlockSpec((step,) + shape, lambda i, flags: (i,) + (0,) * len(shape))


def core_block(step, count):
    return pl.BlockSpec((step, TOK, D), lambda i, flags: (flags[0] * (count // step) + i, 0, 0))


def struct(kind, *shape):
    return jax.ShapeDtypeStruct(shape, kind)


def call(body, images, step, in_specs, outs, scratch, flops, name):
    return pl.pallas_call(
        body,
        grid_spec=pltpu.PrefetchScalarGridSpec(
            num_scalar_prefetch=1,
            grid=(images // step,),
            in_specs=in_specs,
            out_specs=[spec for spec, _ in outs],
            scratch_shapes=scratch,
        ),
        out_shape=[shape for _, shape in outs],
        compiler_params=pltpu.CompilerParams(vmem_limit_bytes=VMEM_LIMIT, dimension_semantics=("arbitrary",)),
        cost_estimate=pl.CostEstimate(flops=flops * images, bytes_accessed=20_000_000, transcendentals=0),
        name=name,
    )


def step_of(name, images):
    step = STEPS[name]
    return step if images % step == 0 else 1


BIAS = (WINDOWS, PAD, HEADS * PAD)
MIXED = (WINDOWS, PAD, 3 * D)


def run_attention(which, flags, x, shared, weights, images):
    step = step_of("attention", images)
    perm, _, bias, vecs = shared
    entry = core_block(step, images) if which == 0 else block(step, TOK, D)
    return call(
        functools.partial(attention_part, which),
        images,
        step,
        [entry, whole(IMG, TOK), whole(*BIAS), whole(16, D)] + [ANY] * 6,
        [
            (block(step, IMG, D), struct(F32, images, IMG, D)),
            (block(step, *MIXED), struct(BF16, images, *MIXED)),
            (block(step, IMG, D), struct(BF16, images, IMG, D)),
        ],
        W_ATT + [pltpu.VMEM((step, WINDOWS, ROWS, D), F32)] + SEMS,
        800_000_000,
        "layer%d_attention" % which,
    )(flags, x, perm, bias, vecs, *weights)


def run_hidden(which, flags, residual, shared, weights, images):
    step = step_of("hidden", images)
    _, perm_back, _, vecs = shared
    return call(
        functools.partial(hidden_part, which, images),
        images,
        step,
        [block(step, IMG, D), whole(TOK, IMG), whole(16, D)] + [ANY] * 10,
        [
            (block(step, TOK, D), struct(BF16, images, TOK, D)),
            (block(step, IMG, FF), struct(BF16, images, IMG, FF)),
            (block(step, IMG, FF), struct(BF16, images, IMG, FF)),
        ],
        W_MLP + SEMS,
        1_000_000_000,
        "layer%d_hidden" % which,
    )(flags, residual, perm_back, vecs, *weights)


def run_hidden_back(which, flags, residual, act, slope, att, og, shared, weights, images):
    step = step_of("hidden_back", images)
    perm, _, _, vecs = shared
    rows = images * IMG
    cotangent = block(step, TOK, D) if which == 0 else core_block(step, images)
    return call(
        functools.partial(hidden_back, which, images),
        images,
        step,
        [block(step, IMG, D), block(step, IMG, FF), block(step, IMG, FF), block(step, IMG, D), cotangent]
        + [whole(IMG, TOK), whole(16, D)]
        + [ANY] * 10,
        [
            (block(step, IMG, D), struct(F32, images, IMG, D)),
            (whole(2, 512, D), struct(BF16, 2, 512, D)),
            (whole(2, 512, D), struct(BF16, 2, 512, D)),
            (whole(2, 640, D), struct(BF16, 2, 640, D)),
            (whole(2, 640, D), struct(BF16, 2, 640, D)),
            (whole(16, D), struct(F32, 16, D)),
        ],
        W_MLP + [pltpu.VMEM((rows, width), BF16) for width in (D, FF, D, FF, D, D)] + SEMS,
        2_000_000_000,
        "layer%d_hidden_back" % which,
    )(flags, residual, act, slope, att, og, perm, vecs, *weights)


def run_attention_back(which, flags, x, mixed, dres, shared, weights, images):
    step = step_of("attention_back", images)
    perm, perm_back, bias, vecs = shared
    rows = images * IMG
    entry = core_block(step, images) if which == 0 else block(step, TOK, D)
    return call(
        functools.partial(attention_back, which),
        images,
        step,
        [entry, block(step, *MIXED), block(step, IMG, D)]
        + [whole(IMG, TOK), whole(TOK, IMG), whole(*BIAS), whole(16, D)]
        + [ANY] * 6,
        [
            (block(step, TOK, D), struct(BF16, images, TOK, D)),
            (whole(2, 384, D), struct(BF16, 2, 384, D)),
            (whole(2, 384, D), struct(BF16, 2, 384, D)),
            (whole(16, D), struct(F32, 16, D)),
            (whole(PAD, HEADS * PAD), struct(F32, PAD, HEADS * PAD)),
        ],
        W_ATT
        + [pltpu.VMEM((step, WINDOWS, PAD, D), BF16), pltpu.VMEM((step, WINDOWS, ROWS, 3 * D), F32)]
        + [pltpu.VMEM((rows, width), BF16) for width in (D, 3 * D)]
        + SEMS,
        2_000_000_000,
        "layer%d_attention_back" % which,
    )(flags, x, mixed, dres, perm, perm_back, bias, vecs, *weights)


def choose(flags, zero, one, target, sems):
    rows = target.shape[1]

    def start(refs, order):
        for m in range(2):
            pltpu.make_async_copy(refs[m].at[pl.ds(refs[2], rows)], target.at[order[m]], sems.at[m]).start()

    @pl.when(flags[0] == 0)
    def _():
        start(zero, (0, 1))

    @pl.when(flags[0] != 0)
    def _():
        start(one, (1, 0))


def arrived(zero, target, sems):
    rows = target.shape[1]
    for m in range(2):
        pltpu.make_async_copy(zero[m].at[pl.ds(zero[2], rows)], target.at[m], sems.at[m]).wait()


def assemble_mlp(flags, *refs):
    first, second, third = (refs[2 * k : 2 * k + 2] for k in range(3))
    fc1_out, fc2_out, proj_out, two, one, sems = refs[6:]
    choose(flags, second + (384,), first + (0,), two, sems.at[0])
    choose(flags, third + (0,), first + (512,), one, sems.at[1])
    arrived(second + (384,), two, sems.at[0])
    fc2_out[0] = two[...].reshape(1024, D).astype(F32)
    arrived(third + (0,), one, sems.at[1])
    for part in range(2):
        rows = slice(part * 128, (part + 1) * 128)
        for j in range(FF // TILE):
            fc1_out[0, rows, j * TILE : (j + 1) * TILE] = one[part, j * 128 : (j + 1) * 128, :].astype(F32)
        proj_out[0, rows, :] = one[part, 512:640, :].astype(F32)


def assemble_qkv(flags, *refs):
    second, fourth = refs[:2], refs[2:4]
    out, parts, sems = refs[4:]
    choose(flags, fourth + (0,), second + (0,), parts, sems)
    arrived(fourth + (0,), parts, sems)
    for part in range(2):
        for j in range(3):
            out[0, part * 128 : (part + 1) * 128, j * D : (j + 1) * D] = parts[part, j * 128 : (j + 1) * 128, :].astype(F32)


def assemble(body, flags, arrays, shapes, scratch, name):
    return pl.pallas_call(
        body,
        grid_spec=pltpu.PrefetchScalarGridSpec(
            num_scalar_prefetch=1,
            grid=(1,),
            in_specs=[ANY] * len(arrays),
            out_specs=[whole(*shape) for shape in shapes],
            scratch_shapes=scratch,
        ),
        out_shape=[struct(F32, *shape) for shape in shapes],
        compiler_params=pltpu.CompilerParams(vmem_limit_bytes=VMEM_LIMIT),
        cost_estimate=pl.CostEstimate(flops=0, bytes_accessed=8_000_000, transcendentals=0),
        name=name,
    )(flags, *arrays)


def run_assemble_mlp(flags, arrays):
    shapes = [(1, 256, FF), (1, 1024, D), (1, 256, D)]
    scratch = [pltpu.VMEM((2, 512, D), BF16), pltpu.VMEM((2, 640, D), BF16), pltpu.SemaphoreType.DMA((2, 2))]
    return assemble(assemble_mlp, flags, arrays, shapes, scratch, "assemble_mlp")


def run_assemble_qkv(flags, arrays):
    scratch = [pltpu.VMEM((2, 384, D), BF16), pltpu.SemaphoreType.DMA((2,))]
    return assemble(assemble_qkv, flags, arrays, [(1, 256, 3 * D)], scratch, "assemble_qkv")


SWAP = [(0, 1), (1, 0)]


def swap(array, axis):
    return lax.ppermute(array, axis, SWAP)


def relative_onehot():
    t = jnp.arange(PAD, dtype=jnp.int32)[:, None]
    s = jnp.arange(PAD, dtype=jnp.int32)[None, :]
    relative = (s // WIN - t // WIN + WIN - 1) * (2 * WIN - 1) + s % WIN - t % WIN + WIN - 1
    relative = jnp.where((t < SLOTS) & (s < SLOTS), relative, -1).reshape(-1)
    return relative[None, :] == jnp.arange(TABLE, dtype=jnp.int32)[:, None]


def geometry(window_order, regions, layer):
    offset = layer * SHIFT
    source = (window_order // SIDE + offset) % SIDE * SIDE + (window_order % SIDE + offset) % SIDE
    padded = jnp.pad(source.reshape(WINDOWS, SLOTS), ((0, 0), (0, ROWS - SLOTS)), constant_values=-1).reshape(-1)
    places = jnp.arange(TOK, dtype=jnp.int32)
    perm = (padded[:, None] == places[None, :]).astype(BF16)
    perm_back = (places[:, None] == padded[None, :]).astype(BF16)
    masking = jnp.zeros((WINDOWS, PAD, PAD), F32)
    if layer:
        hits = window_order[:, None] == places[None, :]
        region = jnp.sum(jnp.where(hits, regions[None, :], 0), axis=1).reshape(WINDOWS, SLOTS)
        region = jnp.pad(region, ((0, 0), (0, PAD - SLOTS)))
        masking = jnp.where(region[:, :, None] != region[:, None, :], -100.0 * layer, 0.0)
    masking = jnp.where(jnp.arange(PAD)[None, :, None] < SLOTS, masking, NEVER)
    return perm, perm_back, masking.astype(F32)


def bias_of(table, masking):
    spread_bias = jnp.dot(table.T, relative_onehot().astype(BF16), preferred_element_type=F32)
    spread_bias = spread_bias.reshape(HEADS, PAD, PAD).transpose(1, 0, 2)
    return (spread_bias[None] + masking[:, :, None, :]).reshape(WINDOWS, PAD, HEADS * PAD)


def pick(array, index):
    return lax.dynamic_index_in_dim(array, index, 0, keepdims=False)


def after(values, *others):
    return lax.optimization_barrier((values, others))[0]


class Place:
    def __init__(self, replicas):
        self.replicas = replicas
        self.core = lax.axis_index("pipe")
        self.side = lax.axis_index("group")
        self.rep = lax.axis_index("rep")
        self.low = self.rep % 2

    def trade(self, array, bit):
        return lax.ppermute(array, "rep", [(r, r ^ bit) for r in range(self.replicas)])


def in_order(flag, mine, other):
    return jnp.where(flag == 0, jnp.concatenate([mine, other]), jnp.concatenate([other, mine]))


class Chain:
    def __init__(self, place):
        self.place, self.parts, self.ways = place, [], []

    def add(self, keep, send):
        self.parts.append((keep, swap(send, "pipe")))

    def half_of(self, side):
        sums = [pick(keep, side).astype(F32) + pick(got, side) for keep, got in self.parts]
        return sums[0] if len(sums) == 1 else jnp.concatenate(sums, axis=0)

    def ready_x(self):
        side = self.place.side
        self.sent, self.here = self.half_of(1 - side).astype(BF16), self.half_of(side)
        self.move = lambda array: swap(array, "group")
        return self

    def total(self):
        return self.here.astype(F32) + self.arrived.astype(F32)

    def ready_half(self, bit):
        way = (self.place.rep // bit) % 2
        total = self.total()
        total = total.reshape(2, total.shape[0] // 2, D)
        self.sent, self.here = pick(total, 1 - way).astype(BF16), pick(total, way)
        self.move = lambda array: self.place.trade(array, bit)
        return self

    def ready_double(self, bit):
        self.sent = self.here = self.total().astype(BF16)
        self.move = lambda array: self.place.trade(array, bit)
        return self

    def ready_back(self, bit, last):
        way = (self.place.rep // bit) % 2
        if last is None:
            self.sent = self.total().astype(BF16)
        else:
            self.sent = self.joined(last)
        self.move = lambda array: self.place.trade(array, bit)
        return self

    def joined(self, bit):
        return in_order((self.place.rep // bit) % 2, self.sent, self.arrived)

    def send(self):
        self.arrived = self.move(self.sent)


def send_before(flags, *chains):
    flags, sent = lax.optimization_barrier((flags, [chain.sent for chain in chains]))
    for chain, array in zip(chains, sent):
        chain.sent = array
        chain.send()
    return flags


class Order:
    def __init__(self):
        self.last = None

    def go(self, chain):
        if self.last is not None:
            chain.sent = after(chain.sent, self.last)
        self.last = chain.sent
        chain.send()


def blocks_of(array):
    return jnp.concatenate([array[:, c : c + D] for c in range(0, array.shape[1], D)], axis=0)


def per_device(replicas, images, out_grad, window_order, regions, counts, *params):
    place = Place(replicas)
    core, side = place.core, place.side
    count = images.shape[0] // 2
    flags = jnp.stack([core, side, counts[0], place.low]).astype(jnp.int32)
    (gain_one, shift_one, qkv, table, proj, proj_shift, gain_two, shift_two, fc1, fc1_shift, fc2, fc2_shift) = params

    vectors = [gain_one, shift_one, proj_shift, gain_two, shift_two, fc2_shift, fc1_shift, table]
    small = jnp.concatenate([v.reshape(-1) for v in vectors])
    small = jnp.pad(small, (0, 16 * D - small.shape[0])).reshape(16, D)
    parts = [jnp.concatenate([blocks_of(qkv[0]), proj[0]], axis=0), blocks_of(fc1[0]), fc2[0]]
    halves = [lax.dynamic_slice_in_dim(part, place.low * 512, 512, 0) for part in parts]
    over_x = [swap(halves[0], "group")]
    own = jnp.concatenate(after(parts, halves[0]), axis=0)
    own_other = swap(own, "pipe")
    small_x = swap(small, "group")
    small_both = jnp.concatenate([small, small_x], axis=0)
    small_other = swap(small_both, "pipe")
    over_x.append(swap(after(halves[1], over_x[0]), "group"))
    over_x.append(swap(after(halves[2], over_x[1]), "group"))
    over_y = [place.trade(over_x[0], 1), place.trade(over_x[1], 1)]
    att_weights = (own, own_other, over_x[0], over_y[0], swap(over_x[0], "pipe"), swap(over_y[0], "pipe"))

    shared = []
    for layer in range(2):
        chosen = jnp.where(core == layer, small_both, small_other).reshape(2, -1)
        pair = jnp.where(side == 0, chosen, chosen[::-1])
        six = pair[:, :1536].reshape(2, 6, 256).transpose(1, 0, 2).reshape(6, D)
        vecs = jnp.concatenate([six, pair[:, 1536:2560].reshape(4, D), jnp.zeros((6, D), BF16)]).astype(F32)
        joined = pair[:, 2560 : 2560 + TABLE * 8].reshape(2, TABLE, 8).transpose(1, 0, 2).reshape(TABLE, HEADS)
        perm, perm_back, masking = geometry(window_order, regions, layer)
        shared.append((perm, perm_back, bias_of(joined, masking), vecs))

    residual_zero, mixed_zero, attended_zero = run_attention(
        0, after(flags, over_x[1]), images, shared[0], att_weights, count
    )
    over_y.append(place.trade(after(over_x[2], residual_zero), 1))
    mlp_weights = (own, own_other)
    for k in (1, 2):
        mlp_weights += (over_x[k], over_y[k], swap(after(over_x[k], residual_zero), "pipe"), swap(after(over_y[k], residual_zero), "pipe"))
    out_zero, act_zero, slope_zero = run_hidden(0, flags, residual_zero, shared[0], mlp_weights, count)
    residual_one, mixed_one, attended_one = run_attention(1, flags, out_zero, shared[1], att_weights, count)
    out_one, act_one, slope_one = run_hidden(1, flags, residual_one, shared[1], mlp_weights, count)
    dres_one, two_keep, two_send, one_keep, one_send, sums_mlp_one = run_hidden_back(
        1, flags, residual_one, act_one, slope_one, attended_one, out_grad, shared[1], mlp_weights, count
    )
    one = Chain(place)
    one.add(two_keep, two_send)
    one.add(one_keep, one_send)
    tied = send_before(flags, one.ready_x())
    outs = run_attention_back(1, tied, out_zero, mixed_one, dres_one, shared[1], att_weights, count)
    grad_one, keep, send, sums_att_one, score_one = after(outs, one.arrived)
    two = Chain(place)
    two.add(keep, send)
    tied = send_before(flags, one.ready_half(1))
    outs = run_hidden_back(
        0, tied, residual_zero, act_zero, slope_zero, attended_zero, grad_one, shared[0], mlp_weights, count
    )
    dres_zero, two_keep, two_send, one_keep, one_send, sums_mlp_zero = after(outs, one.arrived)
    two.add(two_keep, two_send)
    three = Chain(place)
    three.add(one_keep, one_send)
    tied = send_before(flags, one.ready_half(2), two.ready_x())
    outs = run_attention_back(0, tied, images, mixed_zero, dres_zero, shared[0], att_weights, count)
    grad_zero, keep, send, sums_att_zero, score_zero = after(outs, one.arrived, two.arrived)

    def packed(sums, score):
        lookup = relative_onehot().astype(F32)
        flat_score = score.reshape(PAD, HEADS, PAD).transpose(1, 0, 2).reshape(HEADS, PAD * PAD)
        grad_table = lax.dot_general(lookup, flat_score, NT, precision=lax.Precision.HIGHEST)
        halves = [
            sums[:6].reshape(6, 2, 256).transpose(1, 0, 2).reshape(2, 1536),
            sums[6:10].reshape(2, 1024),
            grad_table.reshape(TABLE, 2, 8).transpose(1, 0, 2).reshape(2, TABLE * 8),
            jnp.zeros((2, 8 * D - 1536 - 1024 - TABLE * 8), F32),
        ]
        return jnp.concatenate(halves, axis=1).astype(BF16).reshape(2, 8, D)

    pack_zero = packed(sums_mlp_zero + sums_att_zero, score_zero)
    pack_one = packed(sums_mlp_one + sums_att_one, score_one)
    pack_keep = jnp.where(core == 0, pack_zero, pack_one)
    pack_send = jnp.where(core == 0, pack_one, pack_zero)
    four = Chain(place)
    four.add(jnp.concatenate([keep, pack_keep], axis=1), jnp.concatenate([send, pack_send], axis=1))

    def both(first_array, second_array):
        mine = jnp.where(core == 0, first_array, second_array)
        other = swap(jnp.where(core == 0, second_array, first_array), "pipe")
        return in_order(core, mine, other)[None]

    activations = both(*after((out_zero, out_one), score_zero))
    input_grads = both(grad_zero, grad_one)

    order = Order()
    far = [bit for bit in (4, 8, 16, 32, 64, 128, 256) if bit < replicas]

    def doubled(chain):
        for bit in far:
            order.go(chain.ready_double(bit))

    order.go(two.ready_half(1))
    doubled(one)
    order.go(three.ready_x())
    order.go(four.ready_x())
    order.go(two.ready_half(2))
    order.go(one.ready_back(2, None))
    order.go(three.ready_half(1))
    doubled(two)
    order.go(four.ready_half(1))
    order.go(one.ready_back(1, 2))
    order.go(three.ready_half(2))
    order.go(four.ready_half(2))
    order.go(two.ready_back(2, None))
    doubled(three)
    doubled(four)
    order.go(two.ready_back(1, 2))
    order.go(three.ready_back(2, None))
    order.go(four.ready_back(2, None))
    order.go(three.ready_back(1, 2))
    order.go(four.ready_back(1, 2))
    full = [chain.joined(1) for chain in (one, two, three, four)]
    came = [
        lax.ppermute(array, "pipe", pairs) for array, pairs in zip(full, ([(0, 1)], SWAP, [(1, 0)], [(1, 0)]))
    ]
    fc1_out, fc2_out, proj_out = run_assemble_mlp(flags, (full[0], came[0], full[1], came[1], full[2], came[2]))
    (qkv_out,) = run_assemble_qkv(flags, (full[1], came[1], full[3], came[3]))
    tail = full[3][384:392].reshape(-1).astype(F32)
    vectors = tail[:1536].reshape(6, 1, 256)
    return (
        activations,
        input_grads,
        vectors[0],
        vectors[1],
        qkv_out,
        tail[2560 : 2560 + TABLE * 8].reshape(1, TABLE, 8),
        proj_out,
        vectors[2],
        vectors[3],
        vectors[4],
        fc1_out,
        tail[1536:2560].reshape(1, 1024),
        fc2_out,
        vectors[5],
    )


def solution(mesh):
    return jax.shard_map(
        functools.partial(per_device, mesh.shape["rep"]),
        mesh=mesh,
        in_specs=(
            P(("group", "rep"), None, None),
            P(("group", "rep"), None, None),
            P(),
            P(),
            P(("group", "rep")),
            P("pipe", "group"),
            P("pipe", "group"),
            P("pipe", "group", None),
            P("pipe", None, "group"),
            P("pipe", "group", None),
            P("pipe", "group"),
            P("pipe", "group"),
            P("pipe", "group"),
            P("pipe", "group", None),
            P("pipe", "group"),
            P("pipe", "group", None),
            P("pipe", "group"),
        ),
        out_specs=(
            P("pipe", ("group", "rep"), None, None),
            P("pipe", ("group", "rep"), None, None),
            P("pipe", "group"),
            P("pipe", "group"),
            P("pipe", "group", None),
            P("pipe", None, "group"),
            P("pipe", "group", None),
            P("pipe", "group"),
            P("pipe", "group"),
            P("pipe", "group"),
            P("pipe", "group", None),
            P("pipe", "group"),
            P("pipe", "group", None),
            P("pipe", "group"),
        ),
        check_vma=False,
    )
```

```python
import functools

import jax
import jax.numpy as jnp
from jax import lax
from jax.experimental import pallas as pl
from jax.experimental.pallas import tpu as pltpu
from jax.sharding import PartitionSpec as P

D = 512
FF = 2048
HEADS = 16
WIN = 7
SIDE = 14
SHIFT = 3
HEAD_DIM = 32
TOK = 196
WINDOWS = 4
SLOTS = WIN * WIN
TABLE = 169
ROWS = 56
PAD = 64
IMG = WINDOWS * ROWS
PACK = 4
WIDE = PACK * HEAD_DIM
LANES = PACK * PAD
PACKS = HEADS // PACK
TILE = 512

EPSILON = 1e-05
ROOT_HALF = 0.7071067811865476
DENSITY = 0.3989422804014327
SCALE = HEAD_DIM ** (-0.5)
NEVER = -1e30
F32 = jnp.float32
BF16 = jnp.bfloat16
VMEM_LIMIT = 60 * 1024 * 1024

NN = (((1,), (0,)), ((), ()))
NT = (((1,), (1,)), ((), ()))
TN = (((0,), (0,)), ((), ()))


def mxu(left, right, dims=NN):
    return lax.dot_general(left, right, dims, preferred_element_type=F32)


def normalize(values):
    centre = jnp.mean(values, -1, keepdims=True)
    centred = values - centre
    inv_std = lax.rsqrt(jnp.mean(centred * centred, -1, keepdims=True) + EPSILON)
    return centred * inv_std, inv_std


def norm_back(grad_rows, unit_rows, inv_std, gain):
    scaled = grad_rows * gain
    average = jnp.mean(scaled, -1, keepdims=True)
    aligned = jnp.mean(scaled * unit_rows, -1, keepdims=True)
    return inv_std * (scaled - average - unit_rows * aligned)


def head_masks():
    lane = lax.broadcasted_iota(jnp.int32, (1, WIDE), 1) // HEAD_DIM
    return [(lane == h).astype(F32) for h in range(PACK)]


def spread(block, masks):
    return jnp.concatenate([block * m.astype(BF16) for m in masks], axis=0)


def collect(product, masks):
    total = product[:PAD] * masks[0]
    for h in range(1, PACK):
        total = total + product[h * PAD : (h + 1) * PAD] * masks[h]
    return total


def softmax_t(keys, queries_wide, bias):
    scores = mxu(keys, queries_wide, NT) * SCALE + bias
    weights = jnp.exp(scores - jnp.max(scores, axis=0, keepdims=True))
    return weights * (1.0 / jnp.sum(weights, axis=0, keepdims=True))


def copies(which, flags, refs, sems):
    own, other, x_own, y_own, x_other, y_other, base, target = refs
    side, low = flags[1], flags[3]
    pairs = []
    for b in range(BLOCKS):
        here = pl.ds((base + b) * 256, 256)
        pairs.append((own.at[here], other.at[here], target(side, b)))
    for over, over_other, half in ((x_own, x_other, low), (y_own, y_other, 1 - low)):
        for b in range(2):
            here = pl.ds(b * 256, 256)
            pairs.append((over.at[here], over_other.at[here], target(1 - side, 2 * half + b)))
    return [[(refs[m], refs[2], sems.at[k]) for m in range(2)] for k, refs in enumerate(pairs)]


def load_weights(which, flags, segments, sems):
    made = [copies(which, flags, refs, sems.at[k]) for k, refs in enumerate(segments)]

    @pl.when(flags[0] == which)
    def _():
        for segment in made:
            for copy, _ in segment:
                pltpu.make_async_copy(*copy).start()

    @pl.when(flags[0] != which)
    def _():
        for segment in made:
            for _, copy in segment:
                pltpu.make_async_copy(*copy).start()


def wait_weights(which, flags, segments, sems):
    for k, refs in enumerate(segments):
        for copy, _ in copies(which, flags, refs, sems.at[k]):
            pltpu.make_async_copy(*copy).wait()


def by_columns(ref):
    return lambda half, b: ref.at[b, pl.ds(pl.multiple_of(half * 256, 256), 256)]


def by_rows(ref):
    return lambda half, b: ref.at[half * BLOCKS + b]


def att_segments(refs, wqkv):
    return [tuple(refs) + (0, by_columns(wqkv))]


def mlp_segments(refs, wfc1, wfc2):
    own = tuple(refs[:2])
    return [own + tuple(refs[2:6]) + (4, by_columns(wfc1)), own + tuple(refs[6:10]) + (8, by_rows(wfc2))]


def vec(vecs, row, count=1):
    rows = [vecs[row + i : row + i + 1, :] for i in range(count)]
    return rows[0] if count == 1 else jnp.concatenate(rows, axis=1)


def attention_forward(mixed, bias, att):
    masks = head_masks()

    def image(n, carry):
        for w in range(WINDOWS):
            parts = []
            for g in range(PACKS):
                c = g * WIDE
                wide = spread(mixed[n, w, :, c : c + WIDE], masks)
                keys = mixed[n, w, :, D + c : D + c + WIDE]
                values = mixed[n, w, :, 2 * D + c : 2 * D + c + WIDE]
                probs = softmax_t(keys, wide, bias[w, :, g * LANES : (g + 1) * LANES]).astype(BF16)
                parts.append(collect(mxu(probs, values, TN), masks)[:ROWS])
            att[n, w] = jnp.concatenate(parts, axis=1)
        return carry

    lax.fori_loop(0, mixed.shape[0], image, 0)


def attention_backward(mixed, bias, datt, dmix, dscore):
    masks = head_masks()

    def image(n, carry):
        for w in range(WINDOWS):
            units = [slice(g * WIDE, (g + 1) * WIDE) for g in range(PACKS)]
            keys = [mixed[n, w, :, D + u.start : D + u.stop] for u in units]
            values = [mixed[n, w, :, 2 * D + u.start : 2 * D + u.stop] for u in units]
            wide = [spread(mixed[n, w, :, u], masks) for u in units]
            dwide = [spread(datt[n, w, :, u], masks) for u in units]
            probs = [softmax_t(k, q, bias[w, :, g * LANES : (g + 1) * LANES]) for g, (k, q) in enumerate(zip(keys, wide))]
            dprobs = [mxu(v, q, NT) for v, q in zip(values, dwide)]
            ds = []
            for p, d in zip(probs, dprobs):
                inner = jnp.sum(d * p, axis=0, keepdims=True)
                ds.append((p * (d - inner)).astype(BF16))
            dv = [mxu(p.astype(BF16), q)[:ROWS] for p, q in zip(probs, dwide)]
            dk = [mxu(s, q)[:ROWS] * SCALE for s, q in zip(ds, wide)]
            dq = [collect(mxu(s, k, TN), masks)[:ROWS] * SCALE for s, k in zip(ds, keys)]
            for g in range(PACKS):
                dscore[:, g * LANES : (g + 1) * LANES] += ds[g].astype(F32)
            dmix[n, w] = jnp.concatenate(dq + dk + dv, axis=1)
        return carry

    lax.fori_loop(0, mixed.shape[0], image, 0)


def tall(values):
    width = values.shape[-1]
    split = values.reshape(-1, ROWS, width)
    blank = jnp.zeros((split.shape[0], PAD - ROWS, width), F32)
    made = jnp.concatenate([split, blank], axis=1).astype(BF16)
    return made.reshape(-1, WINDOWS, PAD, width)


def place(perm, x):
    return jnp.concatenate([mxu(perm[...], x[n]) for n in range(x.shape[0])], axis=0)


def unplace(perm_back, rows, out, alive=None):
    for n in range(out.shape[0]):
        image = mxu(perm_back[...], rows[n * IMG : (n + 1) * IMG])
        out[n] = (image if alive is None else image * alive(n)).astype(BF16)


def flat(ref):
    return ref[...].reshape(-1, ref.shape[-1])


def attention_part(which, flags, x, perm, bias, vecs, *rest):
    residual_out, mixed, att_out, weights, att, sems = rest[6:]
    segments = att_segments(rest[:6], weights)
    first = pl.program_id(0) == 0

    @pl.when(first)
    def _():
        load_weights(which, flags, segments, sems)

    windowed = place(perm, x)
    unit, _ = normalize(windowed)
    low = (unit * vec(vecs, 0) + vec(vecs, 1)).astype(BF16)

    @pl.when(first)
    def _():
        wait_weights(which, flags, segments, sems)

    for j in range(3):
        cols = slice(j * D, (j + 1) * D)
        mixed[:, :, :, cols] = tall(mxu(low, weights[j]))
    attention_forward(mixed, bias, att)
    attended = att[...].reshape(-1, D).astype(BF16)
    att_out[...] = attended.reshape(att_out.shape)
    residual = windowed + mxu(attended, weights[3]) + vec(vecs, 2)
    residual_out[...] = residual.reshape(residual_out.shape)


def hidden_part(which, images, flags, residual_in, perm_back, vecs, *rest):
    out, act, slope, wfc1, wfc2, sems = rest[10:]
    segments = mlp_segments(rest[:10], wfc1, wfc2)
    i = pl.program_id(0)

    @pl.when(i == 0)
    def _():
        load_weights(which, flags, segments, sems)

    residual = flat(residual_in)
    unit, _ = normalize(residual)
    low = (unit * vec(vecs, 3) + vec(vecs, 4)).astype(BF16)

    @pl.when(i == 0)
    def _():
        wait_weights(which, flags, segments, sems)

    step = out.shape[0]

    def alive(n):
        return (flags[0] * images + i * step + n < flags[2]).astype(F32)

    result = hidden_forward(residual, low, vecs, wfc1, wfc2, act, slope)
    unplace(perm_back, result.astype(BF16), out, alive)


def hidden_forward(residual, low, vecs, wfc1, wfc2, act, slope):
    result = residual + vec(vecs, 5)
    shape = act.shape[:-1] + (TILE,)
    for j in range(FF // TILE):
        cols = slice(j * TILE, (j + 1) * TILE)
        hidden = mxu(low, wfc1[j]) + vec(vecs, 6 + j)
        below = 0.5 * (1.0 + lax.erf(hidden * ROOT_HALF))
        low_act = (hidden * below).astype(BF16)
        act[..., cols] = low_act.reshape(shape)
        steep = below + hidden * jnp.exp(-0.5 * hidden * hidden) * DENSITY
        slope[..., cols] = steep.astype(BF16).reshape(shape)
        result = result + mxu(low_act, wfc2[2 * j : 2 * j + 2].reshape(TILE, D))
    return result


def split_grads(part, left, right, outs, row):
    low = left[:, pl.ds(pl.multiple_of(part * 128, 128), 128)]
    high = left[:, pl.ds(pl.multiple_of(256 + part * 128, 128), 128)]
    both = jnp.concatenate([low, high], axis=1).T
    for j in range(right.shape[1] // TILE):
        product = mxu(both, right[:, j * TILE : (j + 1) * TILE]).astype(BF16)
        outs[0, row : row + 128, :] = product[:128]
        outs[1, row : row + 128, :] = product[128:]
        row += 128


def hidden_gradients(flags, rows, grad_out, unit, inv_std, slope, att, vecs, wfc1, wfc2, keep, dres, outs, sums):
    k_two, k_act, k_go, k_dh, k_att, k_dp = keep
    go = grad_out.astype(BF16)
    k_go[rows, :] = go
    grad_two = jnp.zeros(grad_out.shape, F32)
    for j in range(FF // TILE):
        cols = slice(j * TILE, (j + 1) * TILE)
        steep = slope[..., cols].reshape(-1, TILE).astype(F32)
        dh = (mxu(go, wfc2[2 * j : 2 * j + 2].reshape(TILE, D), NT) * steep).astype(BF16)
        k_dh[rows, cols] = dh
        sums[6 + j : 7 + j, :] += jnp.sum(dh.astype(F32), axis=0, keepdims=True)
        grad_two = grad_two + mxu(dh, wfc1[j], NT)
    sums[5:6, :] += jnp.sum(grad_out, axis=0, keepdims=True)
    sums[3:4, :] += jnp.sum(grad_two * unit, axis=0, keepdims=True)
    sums[4:5, :] += jnp.sum(grad_two, axis=0, keepdims=True)
    grad = grad_out + norm_back(grad_two, unit, inv_std, vec(vecs, 3))
    dres[...] = grad.reshape(dres.shape)
    dp = grad.astype(BF16)
    sums[2:3, :] += jnp.sum(dp.astype(F32), axis=0, keepdims=True)
    k_dp[rows, :] = dp
    k_att[rows, :] = flat(att)

    @pl.when(pl.program_id(0) == pl.num_programs(0) - 1)
    def _():
        two_keep, two_send, one_keep, one_send = outs
        for slot, (two, one) in enumerate(((two_keep, one_keep), (two_send, one_send))):
            part = flags[0] if slot == 0 else 1 - flags[0]
            for half in range(2):
                for q in range(2):
                    left = k_act[:, pl.ds(pl.multiple_of(half * 1024 + part * 512 + q * 256, 256), 256)]
                    two[half, q * 256 : (q + 1) * 256, :] = mxu(left, k_go[...], TN).astype(BF16)
            split_grads(part, k_two, k_dh, one, 0)
            split_grads(part, k_att, k_dp, one, 512)


def hidden_back(which, images, flags, residual_in, act, slope, att, og, perm, vecs, *rest):
    dres, outs, sums, wfc1, wfc2, keep, sems = rest[10], rest[11:15], *rest[15:18], rest[18:24], rest[24]
    segments = mlp_segments(rest[:10], wfc1, wfc2)
    i = pl.program_id(0)
    step = og.shape[0]

    @pl.when(i == 0)
    def _():
        load_weights(which, flags, segments, sems)
        sums[...] = jnp.zeros(sums.shape, F32)

    rows = pl.ds(pl.multiple_of(i * step * IMG, step * IMG), step * IMG)
    unit, inv_std = normalize(flat(residual_in))
    keep[0][rows, :] = (unit * vec(vecs, 3) + vec(vecs, 4)).astype(BF16)
    keep[1][rows, :] = flat(act)
    grad_out = place(perm, og)

    @pl.when(i == 0)
    def _():
        wait_weights(which, flags, segments, sems)

    hidden_gradients(flags, rows, grad_out, unit, inv_std, slope, att, vecs, wfc1, wfc2, keep, dres, outs, sums)


def hidden_both(which, images, flags, residual_in, att, og, perm, perm_back, vecs, *rest):
    out, dres, outs, sums, wfc1, wfc2 = *rest[10:12], rest[12:16], *rest[16:19]
    keep, slope, sems = rest[19:25], *rest[25:27]
    segments = mlp_segments(rest[:10], wfc1, wfc2)
    i = pl.program_id(0)
    step = og.shape[0]

    @pl.when(i == 0)
    def _():
        load_weights(which, flags, segments, sems)
        sums[...] = jnp.zeros(sums.shape, F32)

    def alive(n):
        return (flags[0] * images + i * step + n < flags[2]).astype(F32)

    rows = pl.ds(pl.multiple_of(i * step * IMG, step * IMG), step * IMG)
    residual = flat(residual_in)
    unit, inv_std = normalize(residual)
    low = (unit * vec(vecs, 3) + vec(vecs, 4)).astype(BF16)
    keep[0][rows, :] = low
    grad_out = jnp.concatenate([mxu(perm[...], og[n]) * alive(n) for n in range(step)], axis=0)

    @pl.when(i == 0)
    def _():
        wait_weights(which, flags, segments, sems)

    result = hidden_forward(residual, low, vecs, wfc1, wfc2, keep[1].at[rows], slope)
    unplace(perm_back, result.astype(BF16), out, alive)
    hidden_gradients(flags, rows, grad_out, unit, inv_std, slope, att, vecs, wfc1, wfc2, keep, dres, outs, sums)


def attention_back(which, flags, x, mixed, dres, perm, perm_back, bias, vecs, *rest):
    dx, grads_keep, grads_send, sums, dscore, weights, datt, dmix, k_one, k_dm, sems = rest[6:]
    segments = att_segments(rest[:6], weights)
    i = pl.program_id(0)
    step = x.shape[0]

    @pl.when(i == 0)
    def _():
        load_weights(which, flags, segments, sems)
        sums[...] = jnp.zeros(sums.shape, F32)
        dscore[...] = jnp.zeros(dscore.shape, F32)

    rows = pl.ds(pl.multiple_of(i * step * IMG, step * IMG), step * IMG)
    unit, inv_std = normalize(place(perm, x))
    k_one[rows, :] = (unit * vec(vecs, 0) + vec(vecs, 1)).astype(BF16)
    dp = flat(dres).astype(BF16)

    @pl.when(i == 0)
    def _():
        wait_weights(which, flags, segments, sems)

    datt[...] = tall(mxu(dp, weights[3], NT))
    attention_backward(mixed, bias, datt, dmix, dscore)
    dm = dmix[...].reshape(-1, 3 * D).astype(BF16)
    k_dm[rows, :] = dm
    grad_one = sum(mxu(dm[:, j * D : (j + 1) * D], weights[j], NT) for j in range(3))
    sums[0:1, :] += jnp.sum(grad_one * unit, axis=0, keepdims=True)
    sums[1:2, :] += jnp.sum(grad_one, axis=0, keepdims=True)
    grad = flat(dres) + norm_back(grad_one, unit, inv_std, vec(vecs, 0))
    unplace(perm_back, grad.astype(BF16), dx)

    @pl.when(i == pl.num_programs(0) - 1)
    def _():
        for slot, out in enumerate((grads_keep, grads_send)):
            part = flags[0] if slot == 0 else 1 - flags[0]
            split_grads(part, k_one, k_dm, out, 0)


ANY = pl.BlockSpec(memory_space=pl.ANY)
BLOCKS = 4
W_ATT = [pltpu.VMEM((BLOCKS, D, D), BF16)]
W_MLP = [pltpu.VMEM((BLOCKS, D, D), BF16), pltpu.VMEM((2 * BLOCKS, 256, D), BF16)]
SEMS = [pltpu.SemaphoreType.DMA((2, 8))]
STEPS = {"attention": 4, "hidden": 2, "hidden_back": 4, "hidden_both": 4, "attention_back": 4}


def whole(*shape):
    return pl.BlockSpec(shape, lambda i, flags: (0,) * len(shape), pipeline_mode=pl.Buffered(1))


def block(step, *shape):
    return pl.BlockSpec((step,) + shape, lambda i, flags: (i,) + (0,) * len(shape))


def core_block(step, count):
    return pl.BlockSpec((step, TOK, D), lambda i, flags: (flags[0] * (count // step) + i, 0, 0))


def struct(kind, *shape):
    return jax.ShapeDtypeStruct(shape, kind)


def call(body, images, step, in_specs, outs, scratch, flops, name):
    return pl.pallas_call(
        body,
        grid_spec=pltpu.PrefetchScalarGridSpec(
            num_scalar_prefetch=1,
            grid=(images // step,),
            in_specs=in_specs,
            out_specs=[spec for spec, _ in outs],
            scratch_shapes=scratch,
        ),
        out_shape=[shape for _, shape in outs],
        compiler_params=pltpu.CompilerParams(vmem_limit_bytes=VMEM_LIMIT, dimension_semantics=("arbitrary",)),
        cost_estimate=pl.CostEstimate(flops=flops * images, bytes_accessed=20_000_000, transcendentals=0),
        name=name,
    )


def step_of(name, images):
    step = STEPS[name]
    return step if images % step == 0 else 1


BIAS = (WINDOWS, PAD, HEADS * PAD)
MIXED = (WINDOWS, PAD, 3 * D)


def run_attention(which, flags, x, shared, weights, images):
    step = step_of("attention", images)
    perm, _, bias, vecs = shared
    entry = core_block(step, images) if which == 0 else block(step, TOK, D)
    return call(
        functools.partial(attention_part, which),
        images,
        step,
        [entry, whole(IMG, TOK), whole(*BIAS), whole(16, D)] + [ANY] * 6,
        [
            (block(step, IMG, D), struct(F32, images, IMG, D)),
            (block(step, *MIXED), struct(BF16, images, *MIXED)),
            (block(step, IMG, D), struct(BF16, images, IMG, D)),
        ],
        W_ATT + [pltpu.VMEM((step, WINDOWS, ROWS, D), F32)] + SEMS,
        800_000_000,
        "layer%d_attention" % which,
    )(flags, x, perm, bias, vecs, *weights)


def run_hidden(which, flags, residual, shared, weights, images):
    step = step_of("hidden", images)
    _, perm_back, _, vecs = shared
    return call(
        functools.partial(hidden_part, which, images),
        images,
        step,
        [block(step, IMG, D), whole(TOK, IMG), whole(16, D)] + [ANY] * 10,
        [
            (block(step, TOK, D), struct(BF16, images, TOK, D)),
            (block(step, IMG, FF), struct(BF16, images, IMG, FF)),
            (block(step, IMG, FF), struct(BF16, images, IMG, FF)),
        ],
        W_MLP + SEMS,
        1_000_000_000,
        "layer%d_hidden" % which,
    )(flags, residual, perm_back, vecs, *weights)


def hidden_outs(step, images):
    return [
        (block(step, IMG, D), struct(F32, images, IMG, D)),
        (whole(2, 512, D), struct(BF16, 2, 512, D)),
        (whole(2, 512, D), struct(BF16, 2, 512, D)),
        (whole(2, 640, D), struct(BF16, 2, 640, D)),
        (whole(2, 640, D), struct(BF16, 2, 640, D)),
        (whole(16, D), struct(F32, 16, D)),
    ]


def hidden_keep(images):
    return [pltpu.VMEM((images * IMG, width), BF16) for width in (D, FF, D, FF, D, D)]


def run_hidden_back(which, flags, residual, act, slope, att, og, shared, weights, images):
    step = step_of("hidden_back", images)
    perm, _, _, vecs = shared
    return call(
        functools.partial(hidden_back, which, images),
        images,
        step,
        [block(step, IMG, D), block(step, IMG, FF), block(step, IMG, FF), block(step, IMG, D), block(step, TOK, D)]
        + [whole(IMG, TOK), whole(16, D)]
        + [ANY] * 10,
        hidden_outs(step, images),
        W_MLP + hidden_keep(images) + SEMS,
        2_000_000_000,
        "layer%d_hidden_back" % which,
    )(flags, residual, act, slope, att, og, perm, vecs, *weights)


def run_hidden_both(which, flags, residual, att, og, shared, weights, images):
    step = step_of("hidden_both", images)
    perm, perm_back, _, vecs = shared
    return call(
        functools.partial(hidden_both, which, images),
        images,
        step,
        [block(step, IMG, D), block(step, IMG, D), core_block(step, images)]
        + [whole(IMG, TOK), whole(TOK, IMG), whole(16, D)]
        + [ANY] * 10,
        [(block(step, TOK, D), struct(BF16, images, TOK, D))] + hidden_outs(step, images),
        W_MLP + hidden_keep(images) + [pltpu.VMEM((step * IMG, FF), BF16)] + SEMS,
        3_000_000_000,
        "layer%d_hidden_both" % which,
    )(flags, residual, att, og, perm, perm_back, vecs, *weights)


def run_attention_back(which, flags, x, mixed, dres, shared, weights, images):
    step = step_of("attention_back", images)
    perm, perm_back, bias, vecs = shared
    rows = images * IMG
    entry = core_block(step, images) if which == 0 else block(step, TOK, D)
    return call(
        functools.partial(attention_back, which),
        images,
        step,
        [entry, block(step, *MIXED), block(step, IMG, D)]
        + [whole(IMG, TOK), whole(TOK, IMG), whole(*BIAS), whole(16, D)]
        + [ANY] * 6,
        [
            (block(step, TOK, D), struct(BF16, images, TOK, D)),
            (whole(2, 384, D), struct(BF16, 2, 384, D)),
            (whole(2, 384, D), struct(BF16, 2, 384, D)),
            (whole(16, D), struct(F32, 16, D)),
            (whole(PAD, HEADS * PAD), struct(F32, PAD, HEADS * PAD)),
        ],
        W_ATT
        + [pltpu.VMEM((step, WINDOWS, PAD, D), BF16), pltpu.VMEM((step, WINDOWS, ROWS, 3 * D), F32)]
        + [pltpu.VMEM((rows, width), BF16) for width in (D, 3 * D)]
        + SEMS,
        2_000_000_000,
        "layer%d_attention_back" % which,
    )(flags, x, mixed, dres, perm, perm_back, bias, vecs, *weights)


def choose(flags, zero, one, target, sems):
    rows = target.shape[1]

    def start(refs, order):
        for m in range(2):
            pltpu.make_async_copy(refs[m].at[pl.ds(refs[2], rows)], target.at[order[m]], sems.at[m]).start()

    @pl.when(flags[0] == 0)
    def _():
        start(zero, (0, 1))

    @pl.when(flags[0] != 0)
    def _():
        start(one, (1, 0))


def arrived(zero, target, sems):
    rows = target.shape[1]
    for m in range(2):
        pltpu.make_async_copy(zero[m].at[pl.ds(zero[2], rows)], target.at[m], sems.at[m]).wait()


def assemble_mlp(flags, *refs):
    first, second, third = (refs[2 * k : 2 * k + 2] for k in range(3))
    fc1_out, fc2_out, proj_out, two, one, sems = refs[6:]
    choose(flags, second + (384,), first + (0,), two, sems.at[0])
    choose(flags, third + (0,), first + (512,), one, sems.at[1])
    arrived(second + (384,), two, sems.at[0])
    fc2_out[0] = two[...].reshape(1024, D).astype(F32)
    arrived(third + (0,), one, sems.at[1])
    for part in range(2):
        rows = slice(part * 128, (part + 1) * 128)
        for j in range(FF // TILE):
            fc1_out[0, rows, j * TILE : (j + 1) * TILE] = one[part, j * 128 : (j + 1) * 128, :].astype(F32)
        proj_out[0, rows, :] = one[part, 512:640, :].astype(F32)


def assemble_qkv(flags, *refs):
    second, fourth = refs[:2], refs[2:4]
    out, parts, sems = refs[4:]
    choose(flags, fourth + (0,), second + (0,), parts, sems)
    arrived(fourth + (0,), parts, sems)
    for part in range(2):
        for j in range(3):
            out[0, part * 128 : (part + 1) * 128, j * D : (j + 1) * D] = parts[part, j * 128 : (j + 1) * 128, :].astype(F32)


def assemble(body, flags, arrays, shapes, scratch, name):
    return pl.pallas_call(
        body,
        grid_spec=pltpu.PrefetchScalarGridSpec(
            num_scalar_prefetch=1,
            grid=(1,),
            in_specs=[ANY] * len(arrays),
            out_specs=[whole(*shape) for shape in shapes],
            scratch_shapes=scratch,
        ),
        out_shape=[struct(F32, *shape) for shape in shapes],
        compiler_params=pltpu.CompilerParams(vmem_limit_bytes=VMEM_LIMIT),
        cost_estimate=pl.CostEstimate(flops=0, bytes_accessed=8_000_000, transcendentals=0),
        name=name,
    )(flags, *arrays)


def run_assemble_mlp(flags, arrays):
    shapes = [(1, 256, FF), (1, 1024, D), (1, 256, D)]
    scratch = [pltpu.VMEM((2, 512, D), BF16), pltpu.VMEM((2, 640, D), BF16), pltpu.SemaphoreType.DMA((2, 2))]
    return assemble(assemble_mlp, flags, arrays, shapes, scratch, "assemble_mlp")


def run_assemble_qkv(flags, arrays):
    scratch = [pltpu.VMEM((2, 384, D), BF16), pltpu.SemaphoreType.DMA((2,))]
    return assemble(assemble_qkv, flags, arrays, [(1, 256, 3 * D)], scratch, "assemble_qkv")


SWAP = [(0, 1), (1, 0)]


def swap(array, axis):
    return lax.ppermute(array, axis, SWAP)


def relative_onehot():
    t = jnp.arange(PAD, dtype=jnp.int32)[:, None]
    s = jnp.arange(PAD, dtype=jnp.int32)[None, :]
    relative = (s // WIN - t // WIN + WIN - 1) * (2 * WIN - 1) + s % WIN - t % WIN + WIN - 1
    relative = jnp.where((t < SLOTS) & (s < SLOTS), relative, -1).reshape(-1)
    return relative[None, :] == jnp.arange(TABLE, dtype=jnp.int32)[:, None]


def geometry(window_order, regions, layer):
    offset = layer * SHIFT
    source = (window_order // SIDE + offset) % SIDE * SIDE + (window_order % SIDE + offset) % SIDE
    padded = jnp.pad(source.reshape(WINDOWS, SLOTS), ((0, 0), (0, ROWS - SLOTS)), constant_values=-1).reshape(-1)
    places = jnp.arange(TOK, dtype=jnp.int32)
    perm = (padded[:, None] == places[None, :]).astype(BF16)
    perm_back = (places[:, None] == padded[None, :]).astype(BF16)
    masking = jnp.zeros((WINDOWS, PAD, PAD), F32)
    if layer:
        hits = window_order[:, None] == places[None, :]
        region = jnp.sum(jnp.where(hits, regions[None, :], 0), axis=1).reshape(WINDOWS, SLOTS)
        region = jnp.pad(region, ((0, 0), (0, PAD - SLOTS)))
        masking = jnp.where(region[:, :, None] != region[:, None, :], -100.0 * layer, 0.0)
    masking = jnp.where(jnp.arange(PAD)[None, :, None] < SLOTS, masking, NEVER)
    return perm, perm_back, masking.astype(F32)


def bias_of(table, masking):
    spread_bias = jnp.dot(table.T, relative_onehot().astype(BF16), preferred_element_type=F32)
    spread_bias = spread_bias.reshape(HEADS, PAD, PAD).transpose(1, 0, 2)
    return (spread_bias[None] + masking[:, :, None, :]).reshape(WINDOWS, PAD, HEADS * PAD)


def pick(array, index):
    return lax.dynamic_index_in_dim(array, index, 0, keepdims=False)


def after(values, *others):
    return lax.optimization_barrier((values, others))[0]


class Place:
    def __init__(self, replicas):
        self.replicas = replicas
        self.core = lax.axis_index("pipe")
        self.side = lax.axis_index("group")
        self.rep = lax.axis_index("rep")
        self.low = self.rep % 2

    def trade(self, array, bit):
        return lax.ppermute(array, "rep", [(r, r ^ bit) for r in range(self.replicas)])


def in_order(flag, mine, other):
    return jnp.where(flag == 0, jnp.concatenate([mine, other]), jnp.concatenate([other, mine]))


class Chain:
    def __init__(self, place):
        self.place, self.parts, self.ways = place, [], []

    def add(self, keep, send):
        self.parts.append((keep, swap(send, "pipe")))

    def half_of(self, side):
        sums = [pick(keep, side).astype(F32) + pick(got, side) for keep, got in self.parts]
        return sums[0] if len(sums) == 1 else jnp.concatenate(sums, axis=0)

    def ready_x(self):
        side = self.place.side
        self.sent, self.here = self.half_of(1 - side).astype(BF16), self.half_of(side)
        self.move = lambda array: swap(array, "group")
        return self

    def total(self):
        return self.here.astype(F32) + self.arrived.astype(F32)

    def ready_half(self, bit):
        way = (self.place.rep // bit) % 2
        total = self.total()
        total = total.reshape(2, total.shape[0] // 2, D)
        self.sent, self.here = pick(total, 1 - way).astype(BF16), pick(total, way)
        self.move = lambda array: self.place.trade(array, bit)
        return self

    def ready_double(self, bit):
        self.sent = self.here = self.total().astype(BF16)
        self.move = lambda array: self.place.trade(array, bit)
        return self

    def ready_back(self, bit, last):
        way = (self.place.rep // bit) % 2
        if last is None:
            self.sent = self.total().astype(BF16)
        else:
            self.sent = self.joined(last)
        self.move = lambda array: self.place.trade(array, bit)
        return self

    def joined(self, bit):
        return in_order((self.place.rep // bit) % 2, self.sent, self.arrived)

    def send(self):
        self.arrived = self.move(self.sent)


def send_before(flags, *chains):
    flags, sent = lax.optimization_barrier((flags, [chain.sent for chain in chains]))
    for chain, array in zip(chains, sent):
        chain.sent = array
        chain.send()
    return flags


class Order:
    def __init__(self):
        self.last = None

    def go(self, chain):
        if self.last is not None:
            chain.sent = after(chain.sent, self.last)
        self.last = chain.sent
        chain.send()


def blocks_of(array):
    return jnp.concatenate([array[:, c : c + D] for c in range(0, array.shape[1], D)], axis=0)


def per_device(replicas, images, out_grad, window_order, regions, counts, *params):
    place = Place(replicas)
    core, side = place.core, place.side
    count = images.shape[0] // 2
    flags = jnp.stack([core, side, counts[0], place.low]).astype(jnp.int32)
    (gain_one, shift_one, qkv, table, proj, proj_shift, gain_two, shift_two, fc1, fc1_shift, fc2, fc2_shift) = params

    parts = [jnp.concatenate([blocks_of(qkv[0]), proj[0]], axis=0), blocks_of(fc1[0]), fc2[0]]
    halves = [lax.dynamic_slice_in_dim(part, place.low * 512, 512, 0) for part in parts]
    over_x = [swap(halves[0], "group")]
    vectors = [gain_one, shift_one, proj_shift, gain_two, shift_two, fc2_shift, fc1_shift, table]
    parts, vectors = after((parts, vectors), over_x[0])
    own = jnp.concatenate(parts, axis=0)
    small = jnp.concatenate([v.reshape(-1) for v in vectors])
    small = jnp.pad(small, (0, 16 * D - small.shape[0])).reshape(16, D)
    own_other = swap(own, "pipe")
    small_x = swap(small, "group")
    small_both = jnp.concatenate([small, small_x], axis=0)
    small_other = swap(small_both, "pipe")
    over_x.append(swap(after(halves[1], over_x[0]), "group"))
    over_x.append(swap(after(halves[2], over_x[1]), "group"))
    over_y = [place.trade(over_x[0], 1), place.trade(over_x[1], 1)]
    att_weights = (own, own_other, over_x[0], over_y[0], swap(over_x[0], "pipe"), swap(over_y[0], "pipe"))

    shared = []
    for layer in range(2):
        chosen = jnp.where(core == layer, small_both, small_other).reshape(2, -1)
        pair = jnp.where(side == 0, chosen, jnp.concatenate([chosen[1:], chosen[:1]]))
        six = pair[:, :1536].reshape(2, 6, 256).transpose(1, 0, 2).reshape(6, D)
        vecs = jnp.concatenate([six, pair[:, 1536:2560].reshape(4, D), jnp.zeros((6, D), BF16)]).astype(F32)
        joined = pair[:, 2560 : 2560 + TABLE * 8].reshape(2, TABLE, 8).transpose(1, 0, 2).reshape(TABLE, HEADS)
        perm, perm_back, masking = geometry(window_order, regions, layer)
        shared.append((perm, perm_back, bias_of(joined, masking), vecs))

    residual_zero, mixed_zero, attended_zero = run_attention(
        0, after(flags, over_x[1]), images, shared[0], att_weights, count
    )
    over_y.append(place.trade(after(over_x[2], residual_zero), 1))
    mlp_weights = (own, own_other)
    for k in (1, 2):
        mlp_weights += (over_x[k], over_y[k], swap(after(over_x[k], residual_zero), "pipe"), swap(after(over_y[k], residual_zero), "pipe"))
    out_zero, act_zero, slope_zero = run_hidden(0, flags, residual_zero, shared[0], mlp_weights, count)
    residual_one, mixed_one, attended_one = run_attention(1, flags, out_zero, shared[1], att_weights, count)
    out_one, dres_one, two_keep, two_send, one_keep, one_send, sums_mlp_one = run_hidden_both(
        1, flags, residual_one, attended_one, out_grad, shared[1], mlp_weights, count
    )
    one = Chain(place)
    one.add(two_keep, two_send)
    one.add(one_keep, one_send)
    tied = send_before(flags, one.ready_x())
    outs = run_attention_back(1, tied, out_zero, mixed_one, dres_one, shared[1], att_weights, count)
    grad_one, keep, send, sums_att_one, score_one = after(outs, one.arrived)
    two = Chain(place)
    two.add(keep, send)
    tied = send_before(flags, one.ready_half(1))
    outs = run_hidden_back(
        0, tied, residual_zero, act_zero, slope_zero, attended_zero, grad_one, shared[0], mlp_weights, count
    )
    dres_zero, two_keep, two_send, one_keep, one_send, sums_mlp_zero = after(outs, one.arrived)
    two.add(two_keep, two_send)
    three = Chain(place)
    three.add(one_keep, one_send)
    tied = send_before(flags, one.ready_half(2), two.ready_x())
    outs = run_attention_back(0, tied, images, mixed_zero, dres_zero, shared[0], att_weights, count)
    grad_zero, keep, send, sums_att_zero, score_zero = after(outs, one.arrived, two.arrived)

    def packed(sums, score):
        lookup = relative_onehot().astype(F32)
        flat_score = score.reshape(PAD, HEADS, PAD).transpose(1, 0, 2).reshape(HEADS, PAD * PAD)
        grad_table = lax.dot_general(lookup, flat_score, NT, precision=lax.Precision.HIGHEST)
        halves = [
            sums[:6].reshape(6, 2, 256).transpose(1, 0, 2).reshape(2, 1536),
            sums[6:10].reshape(2, 1024),
            grad_table.reshape(TABLE, 2, 8).transpose(1, 0, 2).reshape(2, TABLE * 8),
            jnp.zeros((2, 8 * D - 1536 - 1024 - TABLE * 8), F32),
        ]
        return jnp.concatenate(halves, axis=1).astype(BF16).reshape(2, 8, D)

    pack_zero = packed(sums_mlp_zero + sums_att_zero, score_zero)
    pack_one = packed(sums_mlp_one + sums_att_one, score_one)
    pack_keep = jnp.where(core == 0, pack_zero, pack_one)
    pack_send = jnp.where(core == 0, pack_one, pack_zero)
    four = Chain(place)
    four.add(jnp.concatenate([keep, pack_keep], axis=1), jnp.concatenate([send, pack_send], axis=1))

    def both(first_array, second_array):
        mine = jnp.where(core == 0, first_array, second_array)
        other = swap(jnp.where(core == 0, second_array, first_array), "pipe")
        return in_order(core, mine, other)[None]

    activations = both(*after((out_zero, out_one), score_zero))
    input_grads = both(grad_zero, grad_one)

    order = Order()
    far = [bit for bit in (4, 8, 16, 32, 64, 128, 256) if bit < replicas]

    def doubled(chain):
        for bit in far:
            order.go(chain.ready_double(bit))

    order.go(two.ready_half(1))
    doubled(one)
    order.go(three.ready_x())
    order.go(four.ready_x())
    order.go(two.ready_half(2))
    one.arrived = after(one.arrived, three.arrived)
    order.go(one.ready_back(2, None))
    order.go(three.ready_half(1))
    doubled(two)
    order.go(four.ready_half(1))
    order.go(one.ready_back(1, 2))
    order.go(three.ready_half(2))
    order.go(four.ready_half(2))
    order.go(two.ready_back(2, None))
    doubled(three)
    doubled(four)
    order.go(two.ready_back(1, 2))
    order.go(three.ready_back(2, None))
    order.go(four.ready_back(2, None))
    order.go(three.ready_back(1, 2))
    order.go(four.ready_back(1, 2))
    full = [chain.joined(1) for chain in (one, two, three, four)]
    came = [
        lax.ppermute(array, "pipe", pairs) for array, pairs in zip(full, ([(0, 1)], SWAP, [(1, 0)], [(1, 0)]))
    ]
    fc1_out, fc2_out, proj_out = run_assemble_mlp(flags, (full[0], came[0], full[1], came[1], full[2], came[2]))
    (qkv_out,) = run_assemble_qkv(flags, (full[1], came[1], full[3], came[3]))
    tail = full[3][384:392].reshape(-1).astype(F32)
    vectors = tail[:1536].reshape(6, 1, 256)
    return (
        activations,
        input_grads,
        vectors[0],
        vectors[1],
        qkv_out,
        tail[2560 : 2560 + TABLE * 8].reshape(1, TABLE, 8),
        proj_out,
        vectors[2],
        vectors[3],
        vectors[4],
        fc1_out,
        tail[1536:2560].reshape(1, 1024),
        fc2_out,
        vectors[5],
    )


def solution(mesh):
    return jax.shard_map(
        functools.partial(per_device, mesh.shape["rep"]),
        mesh=mesh,
        in_specs=(
            P(("group", "rep"), None, None),
            P(("group", "rep"), None, None),
            P(),
            P(),
            P(("group", "rep")),
            P("pipe", "group"),
            P("pipe", "group"),
            P("pipe", "group", None),
            P("pipe", None, "group"),
            P("pipe", "group", None),
            P("pipe", "group"),
            P("pipe", "group"),
            P("pipe", "group"),
            P("pipe", "group", None),
            P("pipe", "group"),
            P("pipe", "group", None),
            P("pipe", "group"),
        ),
        out_specs=(
            P("pipe", ("group", "rep"), None, None),
            P("pipe", ("group", "rep"), None, None),
            P("pipe", "group"),
            P("pipe", "group"),
            P("pipe", "group", None),
            P("pipe", None, "group"),
            P("pipe", "group", None),
            P("pipe", "group"),
            P("pipe", "group"),
            P("pipe", "group"),
            P("pipe", "group", None),
            P("pipe", "group"),
            P("pipe", "group", None),
            P("pipe", "group"),
        ),
        check_vma=False,
    )
```

```python
import functools

import jax
import jax.numpy as jnp
from jax import lax
from jax.experimental import pallas as pl
from jax.experimental.pallas import tpu as pltpu
from jax.sharding import PartitionSpec as P

D = 512
FF = 2048
HEADS = 16
WIN = 7
SIDE = 14
SHIFT = 3
HEAD_DIM = 32
TOK = 196
WINDOWS = 4
SLOTS = WIN * WIN
TABLE = 169
ROWS = 56
PAD = 64
IMG = WINDOWS * ROWS
PACK = 4
WIDE = PACK * HEAD_DIM
LANES = PACK * PAD
PACKS = HEADS // PACK
TILE = 512

EPSILON = 1e-05
ROOT_HALF = 0.7071067811865476
DENSITY = 0.3989422804014327
SCALE = HEAD_DIM ** (-0.5)
NEVER = -1e30
F32 = jnp.float32
BF16 = jnp.bfloat16
VMEM_LIMIT = 60 * 1024 * 1024

NN = (((1,), (0,)), ((), ()))
NT = (((1,), (1,)), ((), ()))
TN = (((0,), (0,)), ((), ()))


def mxu(left, right, dims=NN):
    return lax.dot_general(left, right, dims, preferred_element_type=F32)


def normalize(values):
    centre = jnp.mean(values, -1, keepdims=True)
    centred = values - centre
    inv_std = lax.rsqrt(jnp.mean(centred * centred, -1, keepdims=True) + EPSILON)
    return centred * inv_std, inv_std


def norm_back(grad_rows, unit_rows, inv_std, gain):
    scaled = grad_rows * gain
    average = jnp.mean(scaled, -1, keepdims=True)
    aligned = jnp.mean(scaled * unit_rows, -1, keepdims=True)
    return inv_std * (scaled - average - unit_rows * aligned)


def head_masks():
    lane = lax.broadcasted_iota(jnp.int32, (1, WIDE), 1) // HEAD_DIM
    return [(lane == h).astype(F32) for h in range(PACK)]


def spread(block, masks):
    return jnp.concatenate([block * m.astype(BF16) for m in masks], axis=0)


def collect(product, masks):
    total = product[:PAD] * masks[0]
    for h in range(1, PACK):
        total = total + product[h * PAD : (h + 1) * PAD] * masks[h]
    return total


def softmax_t(keys, queries_wide, bias):
    scores = mxu(keys, queries_wide, NT) * SCALE + bias
    weights = jnp.exp(scores - jnp.max(scores, axis=0, keepdims=True))
    return weights * (1.0 / jnp.sum(weights, axis=0, keepdims=True))


def copies(which, flags, refs, sems):
    own, other, x_own, y_own, x_other, y_other, base, target = refs
    side, low = flags[1], flags[3]
    pairs = []
    for b in range(BLOCKS):
        here = pl.ds((base + b) * 256, 256)
        pairs.append((own.at[here], other.at[here], target(side, b)))
    for over, over_other, half in ((x_own, x_other, low), (y_own, y_other, 1 - low)):
        for b in range(2):
            here = pl.ds(b * 256, 256)
            pairs.append((over.at[here], over_other.at[here], target(1 - side, 2 * half + b)))
    return [[(refs[m], refs[2], sems.at[k]) for m in range(2)] for k, refs in enumerate(pairs)]


def load_weights(which, flags, segments, sems):
    made = [copies(which, flags, refs, sems.at[k]) for k, refs in enumerate(segments)]

    @pl.when(flags[0] == which)
    def _():
        for segment in made:
            for copy, _ in segment:
                pltpu.make_async_copy(*copy).start()

    @pl.when(flags[0] != which)
    def _():
        for segment in made:
            for _, copy in segment:
                pltpu.make_async_copy(*copy).start()


def wait_weights(which, flags, segments, sems):
    for k, refs in enumerate(segments):
        for copy, _ in copies(which, flags, refs, sems.at[k]):
            pltpu.make_async_copy(*copy).wait()


def by_columns(ref):
    return lambda half, b: ref.at[b, pl.ds(pl.multiple_of(half * 256, 256), 256)]


def by_rows(ref):
    return lambda half, b: ref.at[half * BLOCKS + b]


def att_segments(refs, wqkv):
    return [tuple(refs) + (0, by_columns(wqkv))]


def mlp_segments(refs, wfc1, wfc2):
    own = tuple(refs[:2])
    return [own + tuple(refs[2:6]) + (4, by_columns(wfc1)), own + tuple(refs[6:10]) + (8, by_rows(wfc2))]


def vec(vecs, row, count=1):
    rows = [vecs[row + i : row + i + 1, :] for i in range(count)]
    return rows[0] if count == 1 else jnp.concatenate(rows, axis=1)


def attention_forward(mixed, bias, att):
    masks = head_masks()

    def image(n, carry):
        for w in range(WINDOWS):
            parts = []
            for g in range(PACKS):
                c = g * WIDE
                wide = spread(mixed[n, w, :, c : c + WIDE], masks)
                keys = mixed[n, w, :, D + c : D + c + WIDE]
                values = mixed[n, w, :, 2 * D + c : 2 * D + c + WIDE]
                probs = softmax_t(keys, wide, bias[w, :, g * LANES : (g + 1) * LANES]).astype(BF16)
                parts.append(collect(mxu(probs, values, TN), masks)[:ROWS])
            att[n, w] = jnp.concatenate(parts, axis=1)
        return carry

    lax.fori_loop(0, mixed.shape[0], image, 0)


def attention_backward(mixed, bias, datt, dmix, dscore):
    masks = head_masks()

    def image(n, carry):
        for w in range(WINDOWS):
            units = [slice(g * WIDE, (g + 1) * WIDE) for g in range(PACKS)]
            keys = [mixed[n, w, :, D + u.start : D + u.stop] for u in units]
            values = [mixed[n, w, :, 2 * D + u.start : 2 * D + u.stop] for u in units]
            wide = [spread(mixed[n, w, :, u], masks) for u in units]
            dwide = [spread(datt[n, w, :, u], masks) for u in units]
            probs = [softmax_t(k, q, bias[w, :, g * LANES : (g + 1) * LANES]) for g, (k, q) in enumerate(zip(keys, wide))]
            dprobs = [mxu(v, q, NT) for v, q in zip(values, dwide)]
            ds = []
            for p, d in zip(probs, dprobs):
                inner = jnp.sum(d * p, axis=0, keepdims=True)
                ds.append((p * (d - inner)).astype(BF16))
            dv = [mxu(p.astype(BF16), q)[:ROWS] for p, q in zip(probs, dwide)]
            dk = [mxu(s, q)[:ROWS] * SCALE for s, q in zip(ds, wide)]
            dq = [collect(mxu(s, k, TN), masks)[:ROWS] * SCALE for s, k in zip(ds, keys)]
            for g in range(PACKS):
                dscore[:, g * LANES : (g + 1) * LANES] += ds[g].astype(F32)
            dmix[n, w] = jnp.concatenate(dq + dk + dv, axis=1)
        return carry

    lax.fori_loop(0, mixed.shape[0], image, 0)


def tall(values):
    width = values.shape[-1]
    split = values.reshape(-1, ROWS, width)
    blank = jnp.zeros((split.shape[0], PAD - ROWS, width), F32)
    made = jnp.concatenate([split, blank], axis=1).astype(BF16)
    return made.reshape(-1, WINDOWS, PAD, width)


def place(perm, x):
    return jnp.concatenate([mxu(perm[...], x[n]) for n in range(x.shape[0])], axis=0)


def unplace(perm_back, rows, out, alive=None):
    for n in range(out.shape[0]):
        image = mxu(perm_back[...], rows[n * IMG : (n + 1) * IMG])
        out[n] = (image if alive is None else image * alive(n)).astype(BF16)


def flat(ref):
    return ref[...].reshape(-1, ref.shape[-1])


def attention_part(which, flags, x, perm, bias, vecs, *rest):
    residual_out, mixed, att_out, weights, att, sems = rest[6:]
    segments = att_segments(rest[:6], weights)
    first = pl.program_id(0) == 0

    @pl.when(first)
    def _():
        load_weights(which, flags, segments, sems)

    windowed = place(perm, x)
    unit, _ = normalize(windowed)
    low = (unit * vec(vecs, 0) + vec(vecs, 1)).astype(BF16)

    @pl.when(first)
    def _():
        wait_weights(which, flags, segments, sems)

    for j in range(3):
        cols = slice(j * D, (j + 1) * D)
        mixed[:, :, :, cols] = tall(mxu(low, weights[j]))
    attention_forward(mixed, bias, att)
    attended = att[...].reshape(-1, D).astype(BF16)
    att_out[...] = attended.reshape(att_out.shape)
    residual = windowed + mxu(attended, weights[3]) + vec(vecs, 2)
    residual_out[...] = residual.reshape(residual_out.shape)


def hidden_part(which, images, flags, residual_in, perm_back, vecs, *rest):
    out, act, slope, wfc1, wfc2, sems = rest[10:]
    segments = mlp_segments(rest[:10], wfc1, wfc2)
    i = pl.program_id(0)

    @pl.when(i == 0)
    def _():
        load_weights(which, flags, segments, sems)

    residual = flat(residual_in)
    unit, _ = normalize(residual)
    low = (unit * vec(vecs, 3) + vec(vecs, 4)).astype(BF16)

    @pl.when(i == 0)
    def _():
        wait_weights(which, flags, segments, sems)

    result = residual + vec(vecs, 5)
    block = act.shape[:2]
    for j in range(FF // TILE):
        cols = slice(j * TILE, (j + 1) * TILE)
        hidden = mxu(low, wfc1[j]) + vec(vecs, 6 + j)
        below = 0.5 * (1.0 + lax.erf(hidden * ROOT_HALF))
        low_act = (hidden * below).astype(BF16)
        act[:, :, cols] = low_act.reshape(block + (TILE,))
        steep = below + hidden * jnp.exp(-0.5 * hidden * hidden) * DENSITY
        slope[:, :, cols] = steep.astype(BF16).reshape(block + (TILE,))
        result = result + mxu(low_act, wfc2[2 * j : 2 * j + 2].reshape(TILE, D))
    step = out.shape[0]

    def alive(n):
        return (flags[0] * images + i * step + n < flags[2]).astype(F32)

    unplace(perm_back, result.astype(BF16), out, alive)


def hidden_forward(residual, low, vecs, wfc1, wfc2, act, slope):
    result = residual + vec(vecs, 5)
    shape = act.shape[:-1] + (TILE,)
    for j in range(FF // TILE):
        cols = slice(j * TILE, (j + 1) * TILE)
        hidden = mxu(low, wfc1[j]) + vec(vecs, 6 + j)
        below = 0.5 * (1.0 + lax.erf(hidden * ROOT_HALF))
        low_act = (hidden * below).astype(BF16)
        act[..., cols] = low_act.reshape(shape)
        steep = below + hidden * jnp.exp(-0.5 * hidden * hidden) * DENSITY
        slope[..., cols] = steep.astype(BF16).reshape(shape)
        result = result + mxu(low_act, wfc2[2 * j : 2 * j + 2].reshape(TILE, D))
    return result


def split_grads(part, left, right, outs, row):
    low = left[:, pl.ds(pl.multiple_of(part * 128, 128), 128)]
    high = left[:, pl.ds(pl.multiple_of(256 + part * 128, 128), 128)]
    both = jnp.concatenate([low, high], axis=1).T
    for j in range(right.shape[1] // TILE):
        product = mxu(both, right[:, j * TILE : (j + 1) * TILE]).astype(BF16)
        outs[0, row : row + 128, :] = product[:128]
        outs[1, row : row + 128, :] = product[128:]
        row += 128


def hidden_gradients(flags, rows, grad_out, unit, inv_std, slope, att, vecs, wfc1, wfc2, keep, dres, outs, sums):
    k_two, k_act, k_go, k_dh, k_att, k_dp = keep
    go = grad_out.astype(BF16)
    k_go[rows, :] = go
    grad_two = jnp.zeros(grad_out.shape, F32)
    for j in range(FF // TILE):
        cols = slice(j * TILE, (j + 1) * TILE)
        steep = slope[..., cols].reshape(-1, TILE).astype(F32)
        dh = (mxu(go, wfc2[2 * j : 2 * j + 2].reshape(TILE, D), NT) * steep).astype(BF16)
        k_dh[rows, cols] = dh
        sums[6 + j : 7 + j, :] += jnp.sum(dh.astype(F32), axis=0, keepdims=True)
        grad_two = grad_two + mxu(dh, wfc1[j], NT)
    sums[5:6, :] += jnp.sum(grad_out, axis=0, keepdims=True)
    sums[3:4, :] += jnp.sum(grad_two * unit, axis=0, keepdims=True)
    sums[4:5, :] += jnp.sum(grad_two, axis=0, keepdims=True)
    grad = grad_out + norm_back(grad_two, unit, inv_std, vec(vecs, 3))
    dres[...] = grad.reshape(dres.shape)
    dp = grad.astype(BF16)
    sums[2:3, :] += jnp.sum(dp.astype(F32), axis=0, keepdims=True)
    k_dp[rows, :] = dp
    k_att[rows, :] = flat(att)

    @pl.when(pl.program_id(0) == pl.num_programs(0) - 1)
    def _():
        two_keep, two_send, one_keep, one_send = outs
        for slot, (two, one) in enumerate(((two_keep, one_keep), (two_send, one_send))):
            part = flags[0] if slot == 0 else 1 - flags[0]
            for half in range(2):
                for q in range(2):
                    left = k_act[:, pl.ds(pl.multiple_of(half * 1024 + part * 512 + q * 256, 256), 256)]
                    two[half, q * 256 : (q + 1) * 256, :] = mxu(left, k_go[...], TN).astype(BF16)
            split_grads(part, k_two, k_dh, one, 0)
            split_grads(part, k_att, k_dp, one, 512)


def hidden_back(which, images, flags, residual_in, act, slope, att, og, perm, vecs, *rest):
    dres, outs, sums, wfc1, wfc2, keep, sems = rest[10], rest[11:15], *rest[15:18], rest[18:24], rest[24]
    segments = mlp_segments(rest[:10], wfc1, wfc2)
    i = pl.program_id(0)
    step = og.shape[0]

    @pl.when(i == 0)
    def _():
        load_weights(which, flags, segments, sems)
        sums[...] = jnp.zeros(sums.shape, F32)

    rows = pl.ds(pl.multiple_of(i * step * IMG, step * IMG), step * IMG)
    unit, inv_std = normalize(flat(residual_in))
    keep[0][rows, :] = (unit * vec(vecs, 3) + vec(vecs, 4)).astype(BF16)
    keep[1][rows, :] = flat(act)
    grad_out = place(perm, og)

    @pl.when(i == 0)
    def _():
        wait_weights(which, flags, segments, sems)

    hidden_gradients(flags, rows, grad_out, unit, inv_std, slope, att, vecs, wfc1, wfc2, keep, dres, outs, sums)


def hidden_both(which, images, flags, residual_in, att, og, perm, perm_back, vecs, *rest):
    out, dres, outs, sums, wfc1, wfc2 = *rest[10:12], rest[12:16], *rest[16:19]
    keep, slope, sems = rest[19:25], *rest[25:27]
    segments = mlp_segments(rest[:10], wfc1, wfc2)
    i = pl.program_id(0)
    step = og.shape[0]

    @pl.when(i == 0)
    def _():
        load_weights(which, flags, segments, sems)
        sums[...] = jnp.zeros(sums.shape, F32)

    def alive(n):
        return (flags[0] * images + i * step + n < flags[2]).astype(F32)

    rows = pl.ds(pl.multiple_of(i * step * IMG, step * IMG), step * IMG)
    residual = flat(residual_in)
    unit, inv_std = normalize(residual)
    low = (unit * vec(vecs, 3) + vec(vecs, 4)).astype(BF16)
    keep[0][rows, :] = low
    grad_out = jnp.concatenate([mxu(perm[...], og[n]) * alive(n) for n in range(step)], axis=0)

    @pl.when(i == 0)
    def _():
        wait_weights(which, flags, segments, sems)

    result = hidden_forward(residual, low, vecs, wfc1, wfc2, keep[1].at[rows], slope)
    unplace(perm_back, result.astype(BF16), out, alive)
    hidden_gradients(flags, rows, grad_out, unit, inv_std, slope, att, vecs, wfc1, wfc2, keep, dres, outs, sums)


def attention_back(which, flags, x, mixed, dres, perm, perm_back, bias, vecs, *rest):
    dx, grads_keep, grads_send, sums, dscore, weights, datt, dmix, k_one, k_dm, sems = rest[6:]
    segments = att_segments(rest[:6], weights)
    i = pl.program_id(0)
    step = x.shape[0]

    @pl.when(i == 0)
    def _():
        load_weights(which, flags, segments, sems)
        sums[...] = jnp.zeros(sums.shape, F32)
        dscore[...] = jnp.zeros(dscore.shape, F32)

    rows = pl.ds(pl.multiple_of(i * step * IMG, step * IMG), step * IMG)
    unit, inv_std = normalize(place(perm, x))
    k_one[rows, :] = (unit * vec(vecs, 0) + vec(vecs, 1)).astype(BF16)
    dp = flat(dres).astype(BF16)

    @pl.when(i == 0)
    def _():
        wait_weights(which, flags, segments, sems)

    datt[...] = tall(mxu(dp, weights[3], NT))
    attention_backward(mixed, bias, datt, dmix, dscore)
    dm = dmix[...].reshape(-1, 3 * D).astype(BF16)
    k_dm[rows, :] = dm
    grad_one = sum(mxu(dm[:, j * D : (j + 1) * D], weights[j], NT) for j in range(3))
    sums[0:1, :] += jnp.sum(grad_one * unit, axis=0, keepdims=True)
    sums[1:2, :] += jnp.sum(grad_one, axis=0, keepdims=True)
    grad = flat(dres) + norm_back(grad_one, unit, inv_std, vec(vecs, 0))
    unplace(perm_back, grad.astype(BF16), dx)

    @pl.when(i == pl.num_programs(0) - 1)
    def _():
        for slot, out in enumerate((grads_keep, grads_send)):
            part = flags[0] if slot == 0 else 1 - flags[0]
            split_grads(part, k_one, k_dm, out, 0)


ANY = pl.BlockSpec(memory_space=pl.ANY)
BLOCKS = 4
W_ATT = [pltpu.VMEM((BLOCKS, D, D), BF16)]
W_MLP = [pltpu.VMEM((BLOCKS, D, D), BF16), pltpu.VMEM((2 * BLOCKS, 256, D), BF16)]
SEMS = [pltpu.SemaphoreType.DMA((2, 8))]
STEPS = {"attention": 4, "hidden": 2, "hidden_back": 4, "hidden_both": 4, "attention_back": 4}


def whole(*shape):
    return pl.BlockSpec(shape, lambda i, flags: (0,) * len(shape), pipeline_mode=pl.Buffered(1))


def block(step, *shape):
    return pl.BlockSpec((step,) + shape, lambda i, flags: (i,) + (0,) * len(shape))


def core_block(step, count):
    return pl.BlockSpec((step, TOK, D), lambda i, flags: (flags[0] * (count // step) + i, 0, 0))


def struct(kind, *shape):
    return jax.ShapeDtypeStruct(shape, kind)


def call(body, images, step, in_specs, outs, scratch, flops, name):
    return pl.pallas_call(
        body,
        grid_spec=pltpu.PrefetchScalarGridSpec(
            num_scalar_prefetch=1,
            grid=(images // step,),
            in_specs=in_specs,
            out_specs=[spec for spec, _ in outs],
            scratch_shapes=scratch,
        ),
        out_shape=[shape for _, shape in outs],
        compiler_params=pltpu.CompilerParams(vmem_limit_bytes=VMEM_LIMIT, dimension_semantics=("arbitrary",)),
        cost_estimate=pl.CostEstimate(flops=flops * images, bytes_accessed=20_000_000, transcendentals=0),
        name=name,
    )


def step_of(name, images):
    step = STEPS[name]
    return step if images % step == 0 else 1


BIAS = (WINDOWS, PAD, HEADS * PAD)
MIXED = (WINDOWS, PAD, 3 * D)


def run_attention(which, flags, x, shared, weights, images):
    step = step_of("attention", images)
    perm, _, bias, vecs = shared
    entry = core_block(step, images) if which == 0 else block(step, TOK, D)
    return call(
        functools.partial(attention_part, which),
        images,
        step,
        [entry, whole(IMG, TOK), whole(*BIAS), whole(16, D)] + [ANY] * 6,
        [
            (block(step, IMG, D), struct(F32, images, IMG, D)),
            (block(step, *MIXED), struct(BF16, images, *MIXED)),
            (block(step, IMG, D), struct(BF16, images, IMG, D)),
        ],
        W_ATT + [pltpu.VMEM((step, WINDOWS, ROWS, D), F32)] + SEMS,
        800_000_000,
        "layer%d_attention" % which,
    )(flags, x, perm, bias, vecs, *weights)


def run_hidden(which, flags, residual, shared, weights, images):
    step = step_of("hidden", images)
    _, perm_back, _, vecs = shared
    return call(
        functools.partial(hidden_part, which, images),
        images,
        step,
        [block(step, IMG, D), whole(TOK, IMG), whole(16, D)] + [ANY] * 10,
        [
            (block(step, TOK, D), struct(BF16, images, TOK, D)),
            (block(step, IMG, FF), struct(BF16, images, IMG, FF)),
            (block(step, IMG, FF), struct(BF16, images, IMG, FF)),
        ],
        W_MLP + SEMS,
        1_000_000_000,
        "layer%d_hidden" % which,
    )(flags, residual, perm_back, vecs, *weights)


def hidden_outs(step, images):
    return [
        (block(step, IMG, D), struct(F32, images, IMG, D)),
        (whole(2, 512, D), struct(BF16, 2, 512, D)),
        (whole(2, 512, D), struct(BF16, 2, 512, D)),
        (whole(2, 640, D), struct(BF16, 2, 640, D)),
        (whole(2, 640, D), struct(BF16, 2, 640, D)),
        (whole(16, D), struct(F32, 16, D)),
    ]


def hidden_keep(images):
    return [pltpu.VMEM((images * IMG, width), BF16) for width in (D, FF, D, FF, D, D)]


def run_hidden_back(which, flags, residual, act, slope, att, og, shared, weights, images):
    step = step_of("hidden_back", images)
    perm, _, _, vecs = shared
    return call(
        functools.partial(hidden_back, which, images),
        images,
        step,
        [block(step, IMG, D), block(step, IMG, FF), block(step, IMG, FF), block(step, IMG, D), block(step, TOK, D)]
        + [whole(IMG, TOK), whole(16, D)]
        + [ANY] * 10,
        hidden_outs(step, images),
        W_MLP + hidden_keep(images) + SEMS,
        2_000_000_000,
        "layer%d_hidden_back" % which,
    )(flags, residual, act, slope, att, og, perm, vecs, *weights)


def run_hidden_both(which, flags, residual, att, og, shared, weights, images):
    step = step_of("hidden_both", images)
    perm, perm_back, _, vecs = shared
    return call(
        functools.partial(hidden_both, which, images),
        images,
        step,
        [block(step, IMG, D), block(step, IMG, D), core_block(step, images)]
        + [whole(IMG, TOK), whole(TOK, IMG), whole(16, D)]
        + [ANY] * 10,
        [(block(step, TOK, D), struct(BF16, images, TOK, D))] + hidden_outs(step, images),
        W_MLP + hidden_keep(images) + [pltpu.VMEM((step * IMG, FF), BF16)] + SEMS,
        3_000_000_000,
        "layer%d_hidden_both" % which,
    )(flags, residual, att, og, perm, perm_back, vecs, *weights)


def run_attention_back(which, flags, x, mixed, dres, shared, weights, images):
    step = step_of("attention_back", images)
    perm, perm_back, bias, vecs = shared
    rows = images * IMG
    entry = core_block(step, images) if which == 0 else block(step, TOK, D)
    return call(
        functools.partial(attention_back, which),
        images,
        step,
        [entry, block(step, *MIXED), block(step, IMG, D)]
        + [whole(IMG, TOK), whole(TOK, IMG), whole(*BIAS), whole(16, D)]
        + [ANY] * 6,
        [
            (block(step, TOK, D), struct(BF16, images, TOK, D)),
            (whole(2, 384, D), struct(BF16, 2, 384, D)),
            (whole(2, 384, D), struct(BF16, 2, 384, D)),
            (whole(16, D), struct(F32, 16, D)),
            (whole(PAD, HEADS * PAD), struct(F32, PAD, HEADS * PAD)),
        ],
        W_ATT
        + [pltpu.VMEM((step, WINDOWS, PAD, D), BF16), pltpu.VMEM((step, WINDOWS, ROWS, 3 * D), F32)]
        + [pltpu.VMEM((rows, width), BF16) for width in (D, 3 * D)]
        + SEMS,
        2_000_000_000,
        "layer%d_attention_back" % which,
    )(flags, x, mixed, dres, perm, perm_back, bias, vecs, *weights)


def choose(flags, zero, one, target, sems):
    rows = target.shape[1]

    def start(refs, order):
        for m in range(2):
            pltpu.make_async_copy(refs[m].at[pl.ds(refs[2], rows)], target.at[order[m]], sems.at[m]).start()

    @pl.when(flags[0] == 0)
    def _():
        start(zero, (0, 1))

    @pl.when(flags[0] != 0)
    def _():
        start(one, (1, 0))


def arrived(zero, target, sems):
    rows = target.shape[1]
    for m in range(2):
        pltpu.make_async_copy(zero[m].at[pl.ds(zero[2], rows)], target.at[m], sems.at[m]).wait()


def assemble_mlp(flags, *refs):
    first, second, third = (refs[2 * k : 2 * k + 2] for k in range(3))
    fc1_out, fc2_out, proj_out, two, one, sems = refs[6:]
    choose(flags, second + (384,), first + (0,), two, sems.at[0])
    choose(flags, third + (0,), first + (512,), one, sems.at[1])
    arrived(second + (384,), two, sems.at[0])
    fc2_out[0] = two[...].reshape(1024, D).astype(F32)
    arrived(third + (0,), one, sems.at[1])
    for part in range(2):
        rows = slice(part * 128, (part + 1) * 128)
        for j in range(FF // TILE):
            fc1_out[0, rows, j * TILE : (j + 1) * TILE] = one[part, j * 128 : (j + 1) * 128, :].astype(F32)
        proj_out[0, rows, :] = one[part, 512:640, :].astype(F32)


def assemble_qkv(flags, *refs):
    second, fourth = refs[:2], refs[2:4]
    out, parts, sems = refs[4:]
    choose(flags, fourth + (0,), second + (0,), parts, sems)
    arrived(fourth + (0,), parts, sems)
    for part in range(2):
        for j in range(3):
            out[0, part * 128 : (part + 1) * 128, j * D : (j + 1) * D] = parts[part, j * 128 : (j + 1) * 128, :].astype(F32)


def assemble(body, flags, arrays, shapes, scratch, name):
    return pl.pallas_call(
        body,
        grid_spec=pltpu.PrefetchScalarGridSpec(
            num_scalar_prefetch=1,
            grid=(1,),
            in_specs=[ANY] * len(arrays),
            out_specs=[whole(*shape) for shape in shapes],
            scratch_shapes=scratch,
        ),
        out_shape=[struct(F32, *shape) for shape in shapes],
        compiler_params=pltpu.CompilerParams(vmem_limit_bytes=VMEM_LIMIT),
        cost_estimate=pl.CostEstimate(flops=0, bytes_accessed=8_000_000, transcendentals=0),
        name=name,
    )(flags, *arrays)


def run_assemble_mlp(flags, arrays):
    shapes = [(1, 256, FF), (1, 1024, D), (1, 256, D)]
    scratch = [pltpu.VMEM((2, 512, D), BF16), pltpu.VMEM((2, 640, D), BF16), pltpu.SemaphoreType.DMA((2, 2))]
    return assemble(assemble_mlp, flags, arrays, shapes, scratch, "assemble_mlp")


def run_assemble_qkv(flags, arrays):
    scratch = [pltpu.VMEM((2, 384, D), BF16), pltpu.SemaphoreType.DMA((2,))]
    return assemble(assemble_qkv, flags, arrays, [(1, 256, 3 * D)], scratch, "assemble_qkv")


SWAP = [(0, 1), (1, 0)]


def swap(array, axis):
    return lax.ppermute(array, axis, SWAP)


def relative_onehot():
    t = jnp.arange(PAD, dtype=jnp.int32)[:, None]
    s = jnp.arange(PAD, dtype=jnp.int32)[None, :]
    relative = (s // WIN - t // WIN + WIN - 1) * (2 * WIN - 1) + s % WIN - t % WIN + WIN - 1
    relative = jnp.where((t < SLOTS) & (s < SLOTS), relative, -1).reshape(-1)
    return relative[None, :] == jnp.arange(TABLE, dtype=jnp.int32)[:, None]


def geometry(window_order, regions, layer):
    offset = layer * SHIFT
    source = (window_order // SIDE + offset) % SIDE * SIDE + (window_order % SIDE + offset) % SIDE
    padded = jnp.pad(source.reshape(WINDOWS, SLOTS), ((0, 0), (0, ROWS - SLOTS)), constant_values=-1).reshape(-1)
    places = jnp.arange(TOK, dtype=jnp.int32)
    perm = (padded[:, None] == places[None, :]).astype(BF16)
    perm_back = (places[:, None] == padded[None, :]).astype(BF16)
    masking = jnp.zeros((WINDOWS, PAD, PAD), F32)
    if layer:
        hits = window_order[:, None] == places[None, :]
        region = jnp.sum(jnp.where(hits, regions[None, :], 0), axis=1).reshape(WINDOWS, SLOTS)
        region = jnp.pad(region, ((0, 0), (0, PAD - SLOTS)))
        masking = jnp.where(region[:, :, None] != region[:, None, :], -100.0 * layer, 0.0)
    masking = jnp.where(jnp.arange(PAD)[None, :, None] < SLOTS, masking, NEVER)
    return perm, perm_back, masking.astype(F32)


def bias_of(table, masking):
    spread_bias = jnp.dot(table.T, relative_onehot().astype(BF16), preferred_element_type=F32)
    spread_bias = spread_bias.reshape(HEADS, PAD, PAD).transpose(1, 0, 2)
    return (spread_bias[None] + masking[:, :, None, :]).reshape(WINDOWS, PAD, HEADS * PAD)


def pick(array, index):
    return lax.dynamic_index_in_dim(array, index, 0, keepdims=False)


def after(values, *others):
    return lax.optimization_barrier((values, others))[0]


class Place:
    def __init__(self, replicas):
        self.replicas = replicas
        self.core = lax.axis_index("pipe")
        self.side = lax.axis_index("group")
        self.rep = lax.axis_index("rep")
        self.low = self.rep % 2

    def trade(self, array, bit):
        return lax.ppermute(array, "rep", [(r, r ^ bit) for r in range(self.replicas)])


def in_order(flag, mine, other):
    return jnp.where(flag == 0, jnp.concatenate([mine, other]), jnp.concatenate([other, mine]))


class Chain:
    def __init__(self, place):
        self.place, self.parts, self.ways = place, [], []

    def add(self, keep, send):
        self.parts.append((keep, swap(send, "pipe")))

    def half_of(self, side):
        sums = [pick(keep, side).astype(F32) + pick(got, side) for keep, got in self.parts]
        return sums[0] if len(sums) == 1 else jnp.concatenate(sums, axis=0)

    def ready_x(self):
        side = self.place.side
        self.sent, self.here = self.half_of(1 - side).astype(BF16), self.half_of(side)
        self.move = lambda array: swap(array, "group")
        return self

    def take(self, other):
        self.here = jnp.concatenate([self.here, other.here], axis=0)
        self.arrived = jnp.concatenate([self.arrived, other.arrived], axis=0)

    def total(self):
        return self.here.astype(F32) + self.arrived.astype(F32)

    def ready_half(self, bit):
        way = (self.place.rep // bit) % 2
        total = self.total()
        total = total.reshape(2, total.shape[0] // 2, D)
        self.sent, self.here = pick(total, 1 - way).astype(BF16), pick(total, way)
        self.move = lambda array: self.place.trade(array, bit)
        return self

    def ready_double(self, bit):
        self.sent = self.here = self.total().astype(BF16)
        self.move = lambda array: self.place.trade(array, bit)
        return self

    def ready_back(self, bit, last):
        way = (self.place.rep // bit) % 2
        if last is None:
            self.sent = self.total().astype(BF16)
        else:
            self.sent = self.joined(last)
        self.move = lambda array: self.place.trade(array, bit)
        return self

    def joined(self, bit):
        return in_order((self.place.rep // bit) % 2, self.sent, self.arrived)

    def send(self):
        self.arrived = self.move(self.sent)


def send_before(flags, *chains):
    flags, sent = lax.optimization_barrier((flags, [chain.sent for chain in chains]))
    for chain, array in zip(chains, sent):
        chain.sent = array
        chain.send()
    return flags


class Order:
    def __init__(self):
        self.last = None

    def go(self, chain):
        if self.last is not None:
            chain.sent = after(chain.sent, self.last)
        self.last = chain.sent
        chain.send()


def blocks_of(array):
    return jnp.concatenate([array[:, c : c + D] for c in range(0, array.shape[1], D)], axis=0)


def per_device(replicas, images, out_grad, window_order, regions, counts, *params):
    place = Place(replicas)
    core, side = place.core, place.side
    count = images.shape[0] // 2
    flags = jnp.stack([core, side, counts[0], place.low]).astype(jnp.int32)
    (gain_one, shift_one, qkv, table, proj, proj_shift, gain_two, shift_two, fc1, fc1_shift, fc2, fc2_shift) = params

    parts = [jnp.concatenate([blocks_of(qkv[0]), proj[0]], axis=0), blocks_of(fc1[0]), fc2[0]]
    first = place.low == 0
    halves = [
        jnp.where(first, blocks_of(qkv[0, :, : 2 * D]), jnp.concatenate([qkv[0, :, 2 * D :], proj[0]], axis=0)),
        jnp.where(first, blocks_of(fc1[0, :, : 2 * D]), blocks_of(fc1[0, :, 2 * D :])),
        lax.dynamic_slice_in_dim(fc2[0], place.low * 512, 512, 0),
    ]
    over_x = [swap(halves[0], "group")]
    vectors = [gain_one, shift_one, proj_shift, gain_two, shift_two, fc2_shift, fc1_shift, table]
    vectors = after(vectors, halves[0])
    parts = after(parts, over_x[0])
    own = jnp.concatenate(parts, axis=0)
    small = jnp.concatenate([v.reshape(-1) for v in vectors])
    small = jnp.pad(small, (0, 16 * D - small.shape[0])).reshape(16, D)
    own_other = swap(own, "pipe")
    small_x = swap(small, "group")
    small_both = jnp.concatenate([small, small_x], axis=0)
    small_other = swap(small_both, "pipe")
    over_x.append(swap(after(halves[1], over_x[0]), "group"))
    over_x.append(swap(after(halves[2], over_x[1]), "group"))
    over_y = [place.trade(over_x[0], 1), place.trade(over_x[1], 1)]
    att_weights = (own, own_other, over_x[0], over_y[0], swap(over_x[0], "pipe"), swap(over_y[0], "pipe"))

    shared = []
    for layer in range(2):
        chosen = jnp.where(core == layer, small_both, small_other).reshape(2, -1)
        pair = jnp.where(side == 0, chosen, jnp.concatenate([chosen[1:], chosen[:1]]))
        six = pair[:, :1536].reshape(2, 6, 256).transpose(1, 0, 2).reshape(6, D)
        vecs = jnp.concatenate([six, pair[:, 1536:2560].reshape(4, D), jnp.zeros((6, D), BF16)]).astype(F32)
        joined = pair[:, 2560 : 2560 + TABLE * 8].reshape(2, TABLE, 8).transpose(1, 0, 2).reshape(TABLE, HEADS)
        perm, perm_back, masking = geometry(window_order, regions, layer)
        shared.append((perm, perm_back, bias_of(joined, masking), vecs))

    residual_zero, mixed_zero, attended_zero = run_attention(
        0, after(flags, over_x[1]), images, shared[0], att_weights, count
    )
    over_y.append(place.trade(after(over_x[2], residual_zero), 1))
    mlp_weights = (own, own_other)
    for k in (1, 2):
        mlp_weights += (over_x[k], over_y[k], swap(after(over_x[k], residual_zero), "pipe"), swap(after(over_y[k], residual_zero), "pipe"))
    out_zero, act_zero, slope_zero = run_hidden(0, flags, residual_zero, shared[0], mlp_weights, count)
    residual_one, mixed_one, attended_one = run_attention(1, flags, out_zero, shared[1], att_weights, count)
    out_one, dres_one, two_keep, two_send, one_keep, one_send, sums_mlp_one = run_hidden_both(
        1, flags, residual_one, attended_one, out_grad, shared[1], mlp_weights, count
    )
    one, more = Chain(place), Chain(place)
    one.add(two_keep, two_send)
    more.add(one_keep, one_send)
    tied = send_before(flags, one.ready_x())
    outs = run_attention_back(1, tied, out_zero, mixed_one, dres_one, shared[1], att_weights, count)
    grad_one, keep, send, sums_att_one, score_one = after(outs, one.arrived)
    two = Chain(place)
    two.add(keep, send)
    tied = send_before(flags, more.ready_x())
    outs = run_hidden_back(
        0, tied, residual_zero, act_zero, slope_zero, attended_zero, grad_one, shared[0], mlp_weights, count
    )
    dres_zero, two_keep, two_send, one_keep, one_send, sums_mlp_zero = after(outs, more.arrived)
    one.take(more)
    two.add(two_keep, two_send)
    three = Chain(place)
    three.add(one_keep, one_send)
    tied = send_before(flags, one.ready_half(1), two.ready_x())
    outs = run_attention_back(0, tied, images, mixed_zero, dres_zero, shared[0], att_weights, count)
    grad_zero, keep, send, sums_att_zero, score_zero = after(outs, one.arrived, two.arrived)

    def packed(sums, score):
        lookup = relative_onehot().astype(F32)
        flat_score = score.reshape(PAD, HEADS, PAD).transpose(1, 0, 2).reshape(HEADS, PAD * PAD)
        grad_table = lax.dot_general(lookup, flat_score, NT, precision=lax.Precision.HIGHEST)
        halves = [
            sums[:6].reshape(6, 2, 256).transpose(1, 0, 2).reshape(2, 1536),
            sums[6:10].reshape(2, 1024),
            grad_table.reshape(TABLE, 2, 8).transpose(1, 0, 2).reshape(2, TABLE * 8),
            jnp.zeros((2, 8 * D - 1536 - 1024 - TABLE * 8), F32),
        ]
        return jnp.concatenate(halves, axis=1).astype(BF16).reshape(2, 8, D)

    pack_zero = packed(sums_mlp_zero + sums_att_zero, score_zero)
    pack_one = packed(sums_mlp_one + sums_att_one, score_one)
    pack_keep = jnp.where(core == 0, pack_zero, pack_one)
    pack_send = jnp.where(core == 0, pack_one, pack_zero)
    four = Chain(place)
    four.add(jnp.concatenate([keep, pack_keep], axis=1), jnp.concatenate([send, pack_send], axis=1))

    def both(first_array, second_array):
        mine = jnp.where(core == 0, first_array, second_array)
        other = swap(jnp.where(core == 0, second_array, first_array), "pipe")
        return in_order(core, mine, other)[None]

    activations = both(*after((out_zero, out_one), score_zero))
    input_grads = both(grad_zero, grad_one)

    order = Order()
    far = [bit for bit in (4, 8, 16, 32, 64, 128, 256) if bit < replicas]

    def doubled(chain):
        for bit in far:
            order.go(chain.ready_double(bit))

    order.go(three.ready_x())
    order.go(two.ready_half(1))
    order.go(one.ready_half(2))
    order.go(four.ready_x())
    order.go(two.ready_half(2))
    doubled(one)
    order.go(three.ready_half(1))
    doubled(two)
    order.go(four.ready_half(1))
    order.go(one.ready_back(2, None))
    order.go(three.ready_half(2))
    order.go(four.ready_half(2))
    order.go(one.ready_back(1, 2))
    order.go(two.ready_back(2, None))
    doubled(three)
    doubled(four)
    order.go(two.ready_back(1, 2))
    order.go(three.ready_back(2, None))
    order.go(four.ready_back(2, None))
    order.go(three.ready_back(1, 2))
    order.go(four.ready_back(1, 2))
    full = [chain.joined(1) for chain in (one, two, three, four)]
    came = [
        lax.ppermute(array, "pipe", pairs) for array, pairs in zip(full, ([(0, 1)], SWAP, [(1, 0)], [(1, 0)]))
    ]
    fc1_out, fc2_out, proj_out = run_assemble_mlp(flags, (full[0], came[0], full[1], came[1], full[2], came[2]))
    (qkv_out,) = run_assemble_qkv(flags, (full[1], came[1], full[3], came[3]))
    tail = full[3][384:392].reshape(-1).astype(F32)
    vectors = tail[:1536].reshape(6, 1, 256)
    return (
        activations,
        input_grads,
        vectors[0],
        vectors[1],
        qkv_out,
        tail[2560 : 2560 + TABLE * 8].reshape(1, TABLE, 8),
        proj_out,
        vectors[2],
        vectors[3],
        vectors[4],
        fc1_out,
        tail[1536:2560].reshape(1, 1024),
        fc2_out,
        vectors[5],
    )


def solution(mesh):
    return jax.shard_map(
        functools.partial(per_device, mesh.shape["rep"]),
        mesh=mesh,
        in_specs=(
            P(("group", "rep"), None, None),
            P(("group", "rep"), None, None),
            P(),
            P(),
            P(("group", "rep")),
            P("pipe", "group"),
            P("pipe", "group"),
            P("pipe", "group", None),
            P("pipe", None, "group"),
            P("pipe", "group", None),
            P("pipe", "group"),
            P("pipe", "group"),
            P("pipe", "group"),
            P("pipe", "group", None),
            P("pipe", "group"),
            P("pipe", "group", None),
            P("pipe", "group"),
        ),
        out_specs=(
            P("pipe", ("group", "rep"), None, None),
            P("pipe", ("group", "rep"), None, None),
            P("pipe", "group"),
            P("pipe", "group"),
            P("pipe", "group", None),
            P("pipe", None, "group"),
            P("pipe", "group", None),
            P("pipe", "group"),
            P("pipe", "group"),
            P("pipe", "group"),
            P("pipe", "group", None),
            P("pipe", "group"),
            P("pipe", "group", None),
            P("pipe", "group"),
        ),
        check_vma=False,
    )
```

```python
import functools

import jax
import jax.numpy as jnp
from jax import lax
from jax.experimental import pallas as pl
from jax.experimental.pallas import tpu as pltpu
from jax.sharding import PartitionSpec as P

D = 512
FF = 2048
HEADS = 16
WIN = 7
SIDE = 14
SHIFT = 3
HEAD_DIM = 32
TOK = 196
WINDOWS = 4
SLOTS = WIN * WIN
TABLE = 169
ROWS = 56
PAD = 64
IMG = WINDOWS * ROWS
PACK = 4
WIDE = PACK * HEAD_DIM
LANES = PACK * PAD
PACKS = HEADS // PACK
TILE = 512

EPSILON = 1e-05
ROOT_HALF = 0.7071067811865476
DENSITY = 0.3989422804014327
SCALE = HEAD_DIM ** (-0.5)
NEVER = -1e30
F32 = jnp.float32
BF16 = jnp.bfloat16
VMEM_LIMIT = 60 * 1024 * 1024

NN = (((1,), (0,)), ((), ()))
NT = (((1,), (1,)), ((), ()))
TN = (((0,), (0,)), ((), ()))


def mxu(left, right, dims=NN):
    return lax.dot_general(left, right, dims, preferred_element_type=F32)


def normalize(values):
    centre = jnp.mean(values, -1, keepdims=True)
    centred = values - centre
    inv_std = lax.rsqrt(jnp.mean(centred * centred, -1, keepdims=True) + EPSILON)
    return centred * inv_std, inv_std


def norm_back(grad_rows, unit_rows, inv_std, gain):
    scaled = grad_rows * gain
    average = jnp.mean(scaled, -1, keepdims=True)
    aligned = jnp.mean(scaled * unit_rows, -1, keepdims=True)
    return inv_std * (scaled - average - unit_rows * aligned)


def head_masks():
    lane = lax.broadcasted_iota(jnp.int32, (1, WIDE), 1) // HEAD_DIM
    return [(lane == h).astype(F32) for h in range(PACK)]


def spread(block, masks):
    return jnp.concatenate([block * m.astype(BF16) for m in masks], axis=0)


def collect(product, masks):
    total = product[:PAD] * masks[0]
    for h in range(1, PACK):
        total = total + product[h * PAD : (h + 1) * PAD] * masks[h]
    return total


def softmax_t(keys, queries_wide, bias):
    scores = mxu(keys, queries_wide, NT) * SCALE + bias
    weights = jnp.exp(scores - jnp.max(scores, axis=0, keepdims=True))
    return weights * (1.0 / jnp.sum(weights, axis=0, keepdims=True))


def copies(which, flags, refs, sems):
    own, other, x_own, y_own, x_other, y_other, base, target = refs
    side, low = flags[1], flags[3]
    pairs = []
    for b in range(BLOCKS):
        here = pl.ds((base + b) * 256, 256)
        pairs.append((own.at[here], other.at[here], target(side, b)))
    for over, over_other, half in ((x_own, x_other, low), (y_own, y_other, 1 - low)):
        for b in range(2):
            here = pl.ds(b * 256, 256)
            pairs.append((over.at[here], over_other.at[here], target(1 - side, 2 * half + b)))
    return [[(refs[m], refs[2], sems.at[k]) for m in range(2)] for k, refs in enumerate(pairs)]


def load_weights(which, flags, segments, sems):
    made = [copies(which, flags, refs, sems.at[k]) for k, refs in enumerate(segments)]

    @pl.when(flags[0] == which)
    def _():
        for segment in made:
            for copy, _ in segment:
                pltpu.make_async_copy(*copy).start()

    @pl.when(flags[0] != which)
    def _():
        for segment in made:
            for _, copy in segment:
                pltpu.make_async_copy(*copy).start()


def wait_weights(which, flags, segments, sems):
    for k, refs in enumerate(segments):
        for copy, _ in copies(which, flags, refs, sems.at[k]):
            pltpu.make_async_copy(*copy).wait()


def by_columns(ref):
    return lambda half, b: ref.at[b, pl.ds(pl.multiple_of(half * 256, 256), 256)]


def by_rows(ref):
    return lambda half, b: ref.at[half * BLOCKS + b]


def att_segments(refs, wqkv):
    return [tuple(refs) + (0, by_columns(wqkv))]


def mlp_segments(refs, wfc1, wfc2):
    own = tuple(refs[:2])
    return [own + tuple(refs[2:6]) + (4, by_columns(wfc1)), own + tuple(refs[6:10]) + (8, by_rows(wfc2))]


def vec(vecs, row, count=1):
    rows = [vecs[row + i : row + i + 1, :] for i in range(count)]
    return rows[0] if count == 1 else jnp.concatenate(rows, axis=1)


def attention_forward(mixed, bias, att):
    masks = head_masks()

    def image(n, carry):
        for w in range(WINDOWS):
            parts = []
            for g in range(PACKS):
                c = g * WIDE
                wide = spread(mixed[n, w, :, c : c + WIDE], masks)
                keys = mixed[n, w, :, D + c : D + c + WIDE]
                values = mixed[n, w, :, 2 * D + c : 2 * D + c + WIDE]
                probs = softmax_t(keys, wide, bias[w, :, g * LANES : (g + 1) * LANES]).astype(BF16)
                parts.append(collect(mxu(probs, values, TN), masks)[:ROWS])
            att[n, w] = jnp.concatenate(parts, axis=1)
        return carry

    lax.fori_loop(0, mixed.shape[0], image, 0)


def attention_backward(mixed, bias, datt, dmix, dscore):
    masks = head_masks()

    def image(n, carry):
        for w in range(WINDOWS):
            units = [slice(g * WIDE, (g + 1) * WIDE) for g in range(PACKS)]
            keys = [mixed[n, w, :, D + u.start : D + u.stop] for u in units]
            values = [mixed[n, w, :, 2 * D + u.start : 2 * D + u.stop] for u in units]
            wide = [spread(mixed[n, w, :, u], masks) for u in units]
            dwide = [spread(datt[n, w, :, u], masks) for u in units]
            probs = [softmax_t(k, q, bias[w, :, g * LANES : (g + 1) * LANES]) for g, (k, q) in enumerate(zip(keys, wide))]
            dprobs = [mxu(v, q, NT) for v, q in zip(values, dwide)]
            ds = []
            for p, d in zip(probs, dprobs):
                inner = jnp.sum(d * p, axis=0, keepdims=True)
                ds.append((p * (d - inner)).astype(BF16))
            dv = [mxu(p.astype(BF16), q)[:ROWS] for p, q in zip(probs, dwide)]
            dk = [mxu(s, q)[:ROWS] * SCALE for s, q in zip(ds, wide)]
            dq = [collect(mxu(s, k, TN), masks)[:ROWS] * SCALE for s, k in zip(ds, keys)]
            for g in range(PACKS):
                dscore[:, g * LANES : (g + 1) * LANES] += ds[g].astype(F32)
            dmix[n, w] = jnp.concatenate(dq + dk + dv, axis=1)
        return carry

    lax.fori_loop(0, mixed.shape[0], image, 0)


def tall(values):
    width = values.shape[-1]
    split = values.reshape(-1, ROWS, width)
    blank = jnp.zeros((split.shape[0], PAD - ROWS, width), F32)
    made = jnp.concatenate([split, blank], axis=1).astype(BF16)
    return made.reshape(-1, WINDOWS, PAD, width)


def place(perm, x):
    return jnp.concatenate([mxu(perm[...], x[n]) for n in range(x.shape[0])], axis=0)


def unplace(perm_back, rows, out, alive=None):
    for n in range(out.shape[0]):
        image = mxu(perm_back[...], rows[n * IMG : (n + 1) * IMG])
        out[n] = (image if alive is None else image * alive(n)).astype(BF16)


def flat(ref):
    return ref[...].reshape(-1, ref.shape[-1])


def attention_part(which, flags, x, perm, bias, vecs, *rest):
    residual_out, mixed, att_out, weights, att, sems = rest[6:]
    segments = att_segments(rest[:6], weights)
    first = pl.program_id(0) == 0

    @pl.when(first)
    def _():
        load_weights(which, flags, segments, sems)

    windowed = place(perm, x)
    unit, _ = normalize(windowed)
    low = (unit * vec(vecs, 0) + vec(vecs, 1)).astype(BF16)

    @pl.when(first)
    def _():
        wait_weights(which, flags, segments, sems)

    for j in range(3):
        cols = slice(j * D, (j + 1) * D)
        mixed[:, :, :, cols] = tall(mxu(low, weights[j]))
    attention_forward(mixed, bias, att)
    attended = att[...].reshape(-1, D).astype(BF16)
    att_out[...] = attended.reshape(att_out.shape)
    residual = windowed + mxu(attended, weights[3]) + vec(vecs, 2)
    residual_out[...] = residual.reshape(residual_out.shape)


def hidden_part(which, images, flags, residual_in, perm_back, vecs, *rest):
    out, act, slope, wfc1, wfc2, sems = rest[10:]
    segments = mlp_segments(rest[:10], wfc1, wfc2)
    i = pl.program_id(0)

    @pl.when(i == 0)
    def _():
        load_weights(which, flags, segments, sems)

    residual = flat(residual_in)
    unit, _ = normalize(residual)
    low = (unit * vec(vecs, 3) + vec(vecs, 4)).astype(BF16)

    @pl.when(i == 0)
    def _():
        wait_weights(which, flags, segments, sems)

    result = residual + vec(vecs, 5)
    block = act.shape[:2]
    for j in range(FF // TILE):
        cols = slice(j * TILE, (j + 1) * TILE)
        hidden = mxu(low, wfc1[j]) + vec(vecs, 6 + j)
        below = 0.5 * (1.0 + lax.erf(hidden * ROOT_HALF))
        low_act = (hidden * below).astype(BF16)
        act[:, :, cols] = low_act.reshape(block + (TILE,))
        steep = below + hidden * jnp.exp(-0.5 * hidden * hidden) * DENSITY
        slope[:, :, cols] = steep.astype(BF16).reshape(block + (TILE,))
        result = result + mxu(low_act, wfc2[2 * j : 2 * j + 2].reshape(TILE, D))
    step = out.shape[0]

    def alive(n):
        return (flags[0] * images + i * step + n < flags[2]).astype(F32)

    unplace(perm_back, result.astype(BF16), out, alive)


def hidden_forward(residual, low, vecs, wfc1, wfc2, act, slope):
    result = residual + vec(vecs, 5)
    shape = act.shape[:-1] + (TILE,)
    for j in range(FF // TILE):
        cols = slice(j * TILE, (j + 1) * TILE)
        hidden = mxu(low, wfc1[j]) + vec(vecs, 6 + j)
        below = 0.5 * (1.0 + lax.erf(hidden * ROOT_HALF))
        low_act = (hidden * below).astype(BF16)
        act[..., cols] = low_act.reshape(shape)
        steep = below + hidden * jnp.exp(-0.5 * hidden * hidden) * DENSITY
        slope[..., cols] = steep.astype(BF16).reshape(shape)
        result = result + mxu(low_act, wfc2[2 * j : 2 * j + 2].reshape(TILE, D))
    return result


def split_grads(part, left, right, outs, row):
    low = left[:, pl.ds(pl.multiple_of(part * 128, 128), 128)]
    high = left[:, pl.ds(pl.multiple_of(256 + part * 128, 128), 128)]
    both = jnp.concatenate([low, high], axis=1).T
    for j in range(right.shape[1] // TILE):
        product = mxu(both, right[:, j * TILE : (j + 1) * TILE]).astype(BF16)
        outs[0, row : row + 128, :] = product[:128]
        outs[1, row : row + 128, :] = product[128:]
        row += 128


def hidden_gradients(flags, rows, grad_out, unit, inv_std, slope, att, vecs, wfc1, wfc2, keep, dres, outs, sums):
    k_two, k_act, k_go, k_dh, k_att, k_dp = keep
    go = grad_out.astype(BF16)
    k_go[rows, :] = go
    grad_two = jnp.zeros(grad_out.shape, F32)
    for j in range(FF // TILE):
        cols = slice(j * TILE, (j + 1) * TILE)
        steep = slope[..., cols].reshape(-1, TILE).astype(F32)
        dh = (mxu(go, wfc2[2 * j : 2 * j + 2].reshape(TILE, D), NT) * steep).astype(BF16)
        k_dh[rows, cols] = dh
        sums[6 + j : 7 + j, :] += jnp.sum(dh.astype(F32), axis=0, keepdims=True)
        grad_two = grad_two + mxu(dh, wfc1[j], NT)
    sums[5:6, :] += jnp.sum(grad_out, axis=0, keepdims=True)
    sums[3:4, :] += jnp.sum(grad_two * unit, axis=0, keepdims=True)
    sums[4:5, :] += jnp.sum(grad_two, axis=0, keepdims=True)
    grad = grad_out + norm_back(grad_two, unit, inv_std, vec(vecs, 3))
    dres[...] = grad.reshape(dres.shape)
    dp = grad.astype(BF16)
    sums[2:3, :] += jnp.sum(dp.astype(F32), axis=0, keepdims=True)
    k_dp[rows, :] = dp
    k_att[rows, :] = flat(att)

    @pl.when(pl.program_id(0) == pl.num_programs(0) - 1)
    def _():
        two_keep, two_send, one_keep, one_send = outs
        for slot, (two, one) in enumerate(((two_keep, one_keep), (two_send, one_send))):
            part = flags[0] if slot == 0 else 1 - flags[0]
            for half in range(2):
                for q in range(2):
                    left = k_act[:, pl.ds(pl.multiple_of(half * 1024 + part * 512 + q * 256, 256), 256)]
                    two[half, q * 256 : (q + 1) * 256, :] = mxu(left, k_go[...], TN).astype(BF16)
            split_grads(part, k_two, k_dh, one, 0)
            split_grads(part, k_att, k_dp, one, 512)


def hidden_back(which, images, flags, residual_in, act, slope, att, og, perm, vecs, *rest):
    dres, outs, sums, wfc1, wfc2, keep, sems = rest[10], rest[11:15], *rest[15:18], rest[18:24], rest[24]
    segments = mlp_segments(rest[:10], wfc1, wfc2)
    i = pl.program_id(0)
    step = og.shape[0]

    @pl.when(i == 0)
    def _():
        load_weights(which, flags, segments, sems)
        sums[...] = jnp.zeros(sums.shape, F32)

    rows = pl.ds(pl.multiple_of(i * step * IMG, step * IMG), step * IMG)
    unit, inv_std = normalize(flat(residual_in))
    keep[0][rows, :] = (unit * vec(vecs, 3) + vec(vecs, 4)).astype(BF16)
    keep[1][rows, :] = flat(act)
    grad_out = place(perm, og)

    @pl.when(i == 0)
    def _():
        wait_weights(which, flags, segments, sems)

    hidden_gradients(flags, rows, grad_out, unit, inv_std, slope, att, vecs, wfc1, wfc2, keep, dres, outs, sums)


def hidden_both(which, images, flags, residual_in, att, og, perm, perm_back, vecs, *rest):
    out, dres, outs, sums, wfc1, wfc2 = *rest[10:12], rest[12:16], *rest[16:19]
    keep, slope, sems = rest[19:25], *rest[25:27]
    segments = mlp_segments(rest[:10], wfc1, wfc2)
    i = pl.program_id(0)
    step = og.shape[0]

    @pl.when(i == 0)
    def _():
        load_weights(which, flags, segments, sems)
        sums[...] = jnp.zeros(sums.shape, F32)

    def alive(n):
        return (flags[0] * images + i * step + n < flags[2]).astype(F32)

    rows = pl.ds(pl.multiple_of(i * step * IMG, step * IMG), step * IMG)
    residual = flat(residual_in)
    unit, inv_std = normalize(residual)
    low = (unit * vec(vecs, 3) + vec(vecs, 4)).astype(BF16)
    keep[0][rows, :] = low
    grad_out = jnp.concatenate([mxu(perm[...], og[n]) * alive(n) for n in range(step)], axis=0)

    @pl.when(i == 0)
    def _():
        wait_weights(which, flags, segments, sems)

    result = hidden_forward(residual, low, vecs, wfc1, wfc2, keep[1].at[rows], slope)
    unplace(perm_back, result.astype(BF16), out, alive)
    hidden_gradients(flags, rows, grad_out, unit, inv_std, slope, att, vecs, wfc1, wfc2, keep, dres, outs, sums)


def attention_back(which, flags, x, mixed, dres, perm, perm_back, bias, vecs, *rest):
    dx, grads_keep, grads_send, sums, dscore, weights, datt, dmix, k_one, k_dm, sems = rest[6:]
    segments = att_segments(rest[:6], weights)
    i = pl.program_id(0)
    step = x.shape[0]

    @pl.when(i == 0)
    def _():
        load_weights(which, flags, segments, sems)
        sums[...] = jnp.zeros(sums.shape, F32)
        dscore[...] = jnp.zeros(dscore.shape, F32)

    rows = pl.ds(pl.multiple_of(i * step * IMG, step * IMG), step * IMG)
    unit, inv_std = normalize(place(perm, x))
    k_one[rows, :] = (unit * vec(vecs, 0) + vec(vecs, 1)).astype(BF16)
    dp = flat(dres).astype(BF16)

    @pl.when(i == 0)
    def _():
        wait_weights(which, flags, segments, sems)

    datt[...] = tall(mxu(dp, weights[3], NT))
    attention_backward(mixed, bias, datt, dmix, dscore)
    dm = dmix[...].reshape(-1, 3 * D).astype(BF16)
    k_dm[rows, :] = dm
    grad_one = sum(mxu(dm[:, j * D : (j + 1) * D], weights[j], NT) for j in range(3))
    sums[0:1, :] += jnp.sum(grad_one * unit, axis=0, keepdims=True)
    sums[1:2, :] += jnp.sum(grad_one, axis=0, keepdims=True)
    grad = flat(dres) + norm_back(grad_one, unit, inv_std, vec(vecs, 0))
    unplace(perm_back, grad.astype(BF16), dx)

    @pl.when(i == pl.num_programs(0) - 1)
    def _():
        for slot, out in enumerate((grads_keep, grads_send)):
            part = flags[0] if slot == 0 else 1 - flags[0]
            split_grads(part, k_one, k_dm, out, 0)


ANY = pl.BlockSpec(memory_space=pl.ANY)
BLOCKS = 4
W_ATT = [pltpu.VMEM((BLOCKS, D, D), BF16)]
W_MLP = [pltpu.VMEM((BLOCKS, D, D), BF16), pltpu.VMEM((2 * BLOCKS, 256, D), BF16)]
SEMS = [pltpu.SemaphoreType.DMA((2, 8))]
STEPS = {"attention": 4, "hidden": 4, "hidden_back": 4, "hidden_both": 4, "attention_back": 4}


def whole(*shape):
    return pl.BlockSpec(shape, lambda i, flags: (0,) * len(shape), pipeline_mode=pl.Buffered(1))


def block(step, *shape):
    return pl.BlockSpec((step,) + shape, lambda i, flags: (i,) + (0,) * len(shape))


def core_block(step, count):
    return pl.BlockSpec((step, TOK, D), lambda i, flags: (flags[0] * (count // step) + i, 0, 0))


def struct(kind, *shape):
    return jax.ShapeDtypeStruct(shape, kind)


def call(body, images, step, in_specs, outs, scratch, flops, name):
    return pl.pallas_call(
        body,
        grid_spec=pltpu.PrefetchScalarGridSpec(
            num_scalar_prefetch=1,
            grid=(images // step,),
            in_specs=in_specs,
            out_specs=[spec for spec, _ in outs],
            scratch_shapes=scratch,
        ),
        out_shape=[shape for _, shape in outs],
        compiler_params=pltpu.CompilerParams(vmem_limit_bytes=VMEM_LIMIT, dimension_semantics=("arbitrary",)),
        cost_estimate=pl.CostEstimate(flops=flops * images, bytes_accessed=20_000_000, transcendentals=0),
        name=name,
    )


def step_of(name, images):
    step = STEPS[name]
    return step if images % step == 0 else 1


BIAS = (WINDOWS, PAD, HEADS * PAD)
MIXED = (WINDOWS, PAD, 3 * D)


def run_attention(which, flags, x, shared, weights, images):
    step = step_of("attention", images)
    perm, _, bias, vecs = shared
    entry = core_block(step, images) if which == 0 else block(step, TOK, D)
    return call(
        functools.partial(attention_part, which),
        images,
        step,
        [entry, whole(IMG, TOK), whole(*BIAS), whole(16, D)] + [ANY] * 6,
        [
            (block(step, IMG, D), struct(F32, images, IMG, D)),
            (block(step, *MIXED), struct(BF16, images, *MIXED)),
            (block(step, IMG, D), struct(BF16, images, IMG, D)),
        ],
        W_ATT + [pltpu.VMEM((step, WINDOWS, ROWS, D), F32)] + SEMS,
        800_000_000,
        "layer%d_attention" % which,
    )(flags, x, perm, bias, vecs, *weights)


def run_hidden(which, flags, residual, shared, weights, images):
    step = step_of("hidden", images)
    _, perm_back, _, vecs = shared
    return call(
        functools.partial(hidden_part, which, images),
        images,
        step,
        [block(step, IMG, D), whole(TOK, IMG), whole(16, D)] + [ANY] * 10,
        [
            (block(step, TOK, D), struct(BF16, images, TOK, D)),
            (block(step, IMG, FF), struct(BF16, images, IMG, FF)),
            (block(step, IMG, FF), struct(BF16, images, IMG, FF)),
        ],
        W_MLP + SEMS,
        1_000_000_000,
        "layer%d_hidden" % which,
    )(flags, residual, perm_back, vecs, *weights)


def hidden_outs(step, images):
    return [
        (block(step, IMG, D), struct(F32, images, IMG, D)),
        (whole(2, 512, D), struct(BF16, 2, 512, D)),
        (whole(2, 512, D), struct(BF16, 2, 512, D)),
        (whole(2, 640, D), struct(BF16, 2, 640, D)),
        (whole(2, 640, D), struct(BF16, 2, 640, D)),
        (whole(16, D), struct(F32, 16, D)),
    ]


def hidden_keep(images):
    return [pltpu.VMEM((images * IMG, width), BF16) for width in (D, FF, D, FF, D, D)]


def run_hidden_back(which, flags, residual, act, slope, att, og, shared, weights, images):
    step = step_of("hidden_back", images)
    perm, _, _, vecs = shared
    return call(
        functools.partial(hidden_back, which, images),
        images,
        step,
        [block(step, IMG, D), block(step, IMG, FF), block(step, IMG, FF), block(step, IMG, D), block(step, TOK, D)]
        + [whole(IMG, TOK), whole(16, D)]
        + [ANY] * 10,
        hidden_outs(step, images),
        W_MLP + hidden_keep(images) + SEMS,
        2_000_000_000,
        "layer%d_hidden_back" % which,
    )(flags, residual, act, slope, att, og, perm, vecs, *weights)


def run_hidden_both(which, flags, residual, att, og, shared, weights, images):
    step = step_of("hidden_both", images)
    perm, perm_back, _, vecs = shared
    return call(
        functools.partial(hidden_both, which, images),
        images,
        step,
        [block(step, IMG, D), block(step, IMG, D), core_block(step, images)]
        + [whole(IMG, TOK), whole(TOK, IMG), whole(16, D)]
        + [ANY] * 10,
        [(block(step, TOK, D), struct(BF16, images, TOK, D))] + hidden_outs(step, images),
        W_MLP + hidden_keep(images) + [pltpu.VMEM((step * IMG, FF), BF16)] + SEMS,
        3_000_000_000,
        "layer%d_hidden_both" % which,
    )(flags, residual, att, og, perm, perm_back, vecs, *weights)


def run_attention_back(which, flags, x, mixed, dres, shared, weights, images):
    step = step_of("attention_back", images)
    perm, perm_back, bias, vecs = shared
    rows = images * IMG
    entry = core_block(step, images) if which == 0 else block(step, TOK, D)
    return call(
        functools.partial(attention_back, which),
        images,
        step,
        [entry, block(step, *MIXED), block(step, IMG, D)]
        + [whole(IMG, TOK), whole(TOK, IMG), whole(*BIAS), whole(16, D)]
        + [ANY] * 6,
        [
            (block(step, TOK, D), struct(BF16, images, TOK, D)),
            (whole(2, 384, D), struct(BF16, 2, 384, D)),
            (whole(2, 384, D), struct(BF16, 2, 384, D)),
            (whole(16, D), struct(F32, 16, D)),
            (whole(PAD, HEADS * PAD), struct(F32, PAD, HEADS * PAD)),
        ],
        W_ATT
        + [pltpu.VMEM((step, WINDOWS, PAD, D), BF16), pltpu.VMEM((step, WINDOWS, ROWS, 3 * D), F32)]
        + [pltpu.VMEM((rows, width), BF16) for width in (D, 3 * D)]
        + SEMS,
        2_000_000_000,
        "layer%d_attention_back" % which,
    )(flags, x, mixed, dres, perm, perm_back, bias, vecs, *weights)


def choose(flags, zero, one, target, sems):
    rows = target.shape[1]

    def start(refs, order):
        for m in range(2):
            pltpu.make_async_copy(refs[m].at[pl.ds(refs[2], rows)], target.at[order[m]], sems.at[m]).start()

    @pl.when(flags[0] == 0)
    def _():
        start(zero, (0, 1))

    @pl.when(flags[0] != 0)
    def _():
        start(one, (1, 0))


def arrived(zero, target, sems):
    rows = target.shape[1]
    for m in range(2):
        pltpu.make_async_copy(zero[m].at[pl.ds(zero[2], rows)], target.at[m], sems.at[m]).wait()


def assemble_mlp(flags, *refs):
    first, second, third = (refs[2 * k : 2 * k + 2] for k in range(3))
    fc1_out, fc2_out, proj_out, two, one, sems = refs[6:]
    choose(flags, second + (384,), first + (0,), two, sems.at[0])
    choose(flags, third + (0,), first + (512,), one, sems.at[1])
    arrived(second + (384,), two, sems.at[0])
    fc2_out[0] = two[...].reshape(1024, D).astype(F32)
    arrived(third + (0,), one, sems.at[1])
    for part in range(2):
        rows = slice(part * 128, (part + 1) * 128)
        for j in range(FF // TILE):
            fc1_out[0, rows, j * TILE : (j + 1) * TILE] = one[part, j * 128 : (j + 1) * 128, :].astype(F32)
        proj_out[0, rows, :] = one[part, 512:640, :].astype(F32)


def assemble_qkv(flags, *refs):
    second, fourth = refs[:2], refs[2:4]
    out, parts, sems = refs[4:]
    choose(flags, fourth + (0,), second + (0,), parts, sems)
    arrived(fourth + (0,), parts, sems)
    for part in range(2):
        for j in range(3):
            out[0, part * 128 : (part + 1) * 128, j * D : (j + 1) * D] = parts[part, j * 128 : (j + 1) * 128, :].astype(F32)


def assemble(body, flags, arrays, shapes, scratch, name):
    return pl.pallas_call(
        body,
        grid_spec=pltpu.PrefetchScalarGridSpec(
            num_scalar_prefetch=1,
            grid=(1,),
            in_specs=[ANY] * len(arrays),
            out_specs=[whole(*shape) for shape in shapes],
            scratch_shapes=scratch,
        ),
        out_shape=[struct(F32, *shape) for shape in shapes],
        compiler_params=pltpu.CompilerParams(vmem_limit_bytes=VMEM_LIMIT),
        cost_estimate=pl.CostEstimate(flops=0, bytes_accessed=8_000_000, transcendentals=0),
        name=name,
    )(flags, *arrays)


def run_assemble_mlp(flags, arrays):
    shapes = [(1, 256, FF), (1, 1024, D), (1, 256, D)]
    scratch = [pltpu.VMEM((2, 512, D), BF16), pltpu.VMEM((2, 640, D), BF16), pltpu.SemaphoreType.DMA((2, 2))]
    return assemble(assemble_mlp, flags, arrays, shapes, scratch, "assemble_mlp")


def run_assemble_qkv(flags, arrays):
    scratch = [pltpu.VMEM((2, 384, D), BF16), pltpu.SemaphoreType.DMA((2,))]
    return assemble(assemble_qkv, flags, arrays, [(1, 256, 3 * D)], scratch, "assemble_qkv")


SWAP = [(0, 1), (1, 0)]


def swap(array, axis):
    return lax.ppermute(array, axis, SWAP)


def relative_onehot():
    t = jnp.arange(PAD, dtype=jnp.int32)[:, None]
    s = jnp.arange(PAD, dtype=jnp.int32)[None, :]
    relative = (s // WIN - t // WIN + WIN - 1) * (2 * WIN - 1) + s % WIN - t % WIN + WIN - 1
    relative = jnp.where((t < SLOTS) & (s < SLOTS), relative, -1).reshape(-1)
    return relative[None, :] == jnp.arange(TABLE, dtype=jnp.int32)[:, None]


def geometry(window_order, regions, layer):
    offset = layer * SHIFT
    source = (window_order // SIDE + offset) % SIDE * SIDE + (window_order % SIDE + offset) % SIDE
    padded = jnp.pad(source.reshape(WINDOWS, SLOTS), ((0, 0), (0, ROWS - SLOTS)), constant_values=-1).reshape(-1)
    places = jnp.arange(TOK, dtype=jnp.int32)
    perm = (padded[:, None] == places[None, :]).astype(BF16)
    perm_back = (places[:, None] == padded[None, :]).astype(BF16)
    masking = jnp.zeros((WINDOWS, PAD, PAD), F32)
    if layer:
        hits = window_order[:, None] == places[None, :]
        region = jnp.sum(jnp.where(hits, regions[None, :], 0), axis=1).reshape(WINDOWS, SLOTS)
        region = jnp.pad(region, ((0, 0), (0, PAD - SLOTS)))
        masking = jnp.where(region[:, :, None] != region[:, None, :], -100.0 * layer, 0.0)
    masking = jnp.where(jnp.arange(PAD)[None, :, None] < SLOTS, masking, NEVER)
    return perm, perm_back, masking.astype(F32)


def bias_of(table, masking):
    spread_bias = jnp.dot(table.T, relative_onehot().astype(BF16), preferred_element_type=F32)
    spread_bias = spread_bias.reshape(HEADS, PAD, PAD).transpose(1, 0, 2)
    return (spread_bias[None] + masking[:, :, None, :]).reshape(WINDOWS, PAD, HEADS * PAD)


def pick(array, index):
    return lax.dynamic_index_in_dim(array, index, 0, keepdims=False)


def after(values, *others):
    return lax.optimization_barrier((values, others))[0]


class Place:
    def __init__(self, replicas):
        self.replicas = replicas
        self.core = lax.axis_index("pipe")
        self.side = lax.axis_index("group")
        self.rep = lax.axis_index("rep")
        self.low = self.rep % 2

    def trade(self, array, bit):
        return lax.ppermute(array, "rep", [(r, r ^ bit) for r in range(self.replicas)])


def in_order(flag, mine, other):
    return jnp.where(flag == 0, jnp.concatenate([mine, other]), jnp.concatenate([other, mine]))


class Chain:
    def __init__(self, place):
        self.place, self.parts, self.ways = place, [], []

    def add(self, keep, send):
        self.parts.append((keep, swap(send, "pipe")))

    def half_of(self, side):
        sums = [pick(keep, side).astype(F32) + pick(got, side) for keep, got in self.parts]
        return sums[0] if len(sums) == 1 else jnp.concatenate(sums, axis=0)

    def ready_x(self):
        side = self.place.side
        self.sent, self.here = self.half_of(1 - side).astype(BF16), self.half_of(side)
        self.move = lambda array: swap(array, "group")
        return self

    def take(self, other):
        self.here = jnp.concatenate([self.here, other.here], axis=0)
        self.arrived = jnp.concatenate([self.arrived, other.arrived], axis=0)

    def total(self):
        return self.here.astype(F32) + self.arrived.astype(F32)

    def ready_half(self, bit):
        way = (self.place.rep // bit) % 2
        total = self.total()
        total = total.reshape(2, total.shape[0] // 2, D)
        self.sent, self.here = pick(total, 1 - way).astype(BF16), pick(total, way)
        self.move = lambda array: self.place.trade(array, bit)
        return self

    def ready_double(self, bit):
        self.sent = self.here = self.total().astype(BF16)
        self.move = lambda array: self.place.trade(array, bit)
        return self

    def ready_back(self, bit, last):
        way = (self.place.rep // bit) % 2
        if last is None:
            self.sent = self.total().astype(BF16)
        else:
            self.sent = self.joined(last)
        self.move = lambda array: self.place.trade(array, bit)
        return self

    def joined(self, bit):
        return in_order((self.place.rep // bit) % 2, self.sent, self.arrived)

    def send(self):
        self.arrived = self.move(self.sent)


def send_before(flags, *chains):
    flags, sent = lax.optimization_barrier((flags, [chain.sent for chain in chains]))
    for chain, array in zip(chains, sent):
        chain.sent = array
        chain.send()
    return flags


class Order:
    def __init__(self):
        self.last = None

    def go(self, chain):
        if self.last is not None:
            chain.sent = after(chain.sent, self.last)
        self.last = chain.sent
        chain.send()


def blocks_of(array):
    return jnp.concatenate([array[:, c : c + D] for c in range(0, array.shape[1], D)], axis=0)


def per_device(replicas, images, out_grad, window_order, regions, counts, *params):
    place = Place(replicas)
    core, side = place.core, place.side
    count = images.shape[0] // 2
    flags = jnp.stack([core, side, counts[0], place.low]).astype(jnp.int32)
    (gain_one, shift_one, qkv, table, proj, proj_shift, gain_two, shift_two, fc1, fc1_shift, fc2, fc2_shift) = params

    parts = [jnp.concatenate([blocks_of(qkv[0]), proj[0]], axis=0), blocks_of(fc1[0]), fc2[0]]
    first = place.low == 0
    halves = [
        jnp.where(first, blocks_of(qkv[0, :, : 2 * D]), jnp.concatenate([qkv[0, :, 2 * D :], proj[0]], axis=0)),
        jnp.where(first, blocks_of(fc1[0, :, : 2 * D]), blocks_of(fc1[0, :, 2 * D :])),
        lax.dynamic_slice_in_dim(fc2[0], place.low * 512, 512, 0),
    ]
    over_x = [swap(halves[0], "group")]
    vectors = [gain_one, shift_one, proj_shift, gain_two, shift_two, fc2_shift, fc1_shift, table]
    vectors = after(vectors, halves[0])
    parts = after(parts, over_x[0])
    own = jnp.concatenate(parts, axis=0)
    small = jnp.concatenate([v.reshape(-1) for v in vectors])
    small = jnp.pad(small, (0, 16 * D - small.shape[0])).reshape(16, D)
    own_other = swap(own, "pipe")
    small_x = swap(small, "group")
    small_both = jnp.concatenate([small, small_x], axis=0)
    small_other = swap(small_both, "pipe")
    over_x.append(swap(after(halves[1], over_x[0]), "group"))
    over_x.append(swap(after(halves[2], over_x[1]), "group"))
    over_y = [place.trade(over_x[0], 1), place.trade(over_x[1], 1)]
    att_weights = (own, own_other, over_x[0], over_y[0], swap(over_x[0], "pipe"), swap(over_y[0], "pipe"))

    shared = []
    for layer in range(2):
        chosen = jnp.where(core == layer, small_both, small_other).reshape(2, -1)
        pair = jnp.where(side == 0, chosen, jnp.concatenate([chosen[1:], chosen[:1]]))
        six = pair[:, :1536].reshape(2, 6, 256).transpose(1, 0, 2).reshape(6, D)
        vecs = jnp.concatenate([six, pair[:, 1536:2560].reshape(4, D), jnp.zeros((6, D), BF16)]).astype(F32)
        joined = pair[:, 2560 : 2560 + TABLE * 8].reshape(2, TABLE, 8).transpose(1, 0, 2).reshape(TABLE, HEADS)
        perm, perm_back, masking = geometry(window_order, regions, layer)
        shared.append((perm, perm_back, bias_of(joined, masking), vecs))

    residual_zero, mixed_zero, attended_zero = run_attention(
        0, after(flags, over_x[1]), images, shared[0], att_weights, count
    )
    over_y.append(place.trade(after(over_x[2], residual_zero), 1))
    mlp_weights = (own, own_other)
    for k in (1, 2):
        mlp_weights += (over_x[k], over_y[k], swap(after(over_x[k], residual_zero), "pipe"), swap(after(over_y[k], residual_zero), "pipe"))
    out_zero, act_zero, slope_zero = run_hidden(0, flags, residual_zero, shared[0], mlp_weights, count)
    residual_one, mixed_one, attended_one = run_attention(1, flags, out_zero, shared[1], att_weights, count)
    out_one, dres_one, two_keep, two_send, one_keep, one_send, sums_mlp_one = run_hidden_both(
        1, flags, residual_one, attended_one, out_grad, shared[1], mlp_weights, count
    )
    one, more = Chain(place), Chain(place)
    one.add(two_keep, two_send)
    more.add(one_keep, one_send)
    tied = send_before(flags, one.ready_x())
    outs = run_attention_back(1, tied, out_zero, mixed_one, dres_one, shared[1], att_weights, count)
    grad_one, keep, send, sums_att_one, score_one = after(outs, one.arrived)
    two = Chain(place)
    two.add(keep, send)
    tied = send_before(flags, more.ready_x())
    outs = run_hidden_back(
        0, tied, residual_zero, act_zero, slope_zero, attended_zero, grad_one, shared[0], mlp_weights, count
    )
    dres_zero, two_keep, two_send, one_keep, one_send, sums_mlp_zero = after(outs, more.arrived)
    one.take(more)
    two.add(two_keep, two_send)
    three = Chain(place)
    three.add(one_keep, one_send)
    tied = send_before(flags, one.ready_half(1), two.ready_x())
    outs = run_attention_back(0, tied, images, mixed_zero, dres_zero, shared[0], att_weights, count)
    grad_zero, keep, send, sums_att_zero, score_zero = after(outs, one.arrived, two.arrived)
    four = Chain(place)
    four.add(keep, send)

    def packed(sums, score):
        lookup = relative_onehot().astype(F32)
        flat_score = score.reshape(PAD, HEADS, PAD).transpose(1, 0, 2).reshape(HEADS, PAD * PAD)
        grad_table = lax.dot_general(lookup, flat_score, NT, precision=lax.Precision.HIGHEST)
        halves = [
            sums[:6].reshape(6, 2, 256).transpose(1, 0, 2).reshape(2, 1536),
            sums[6:10].reshape(2, 1024),
            grad_table.reshape(TABLE, 2, 8).transpose(1, 0, 2).reshape(2, TABLE * 8),
            jnp.zeros((2, 8 * D - 1536 - 1024 - TABLE * 8), F32),
        ]
        return jnp.concatenate(halves, axis=1).astype(BF16).reshape(2, 8, D)

    pack_zero = packed(sums_mlp_zero + sums_att_zero, score_zero)
    pack_one = packed(sums_mlp_one + sums_att_one, score_one)
    pack_keep = jnp.where(core == 0, pack_zero, pack_one)
    pack_send = jnp.where(core == 0, pack_one, pack_zero)
    four.add(pack_keep, pack_send)

    def both(first_array, second_array):
        mine = jnp.where(core == 0, first_array, second_array)
        other = swap(jnp.where(core == 0, second_array, first_array), "pipe")
        return in_order(core, mine, other)[None]

    activations = both(*after((out_zero, out_one), score_zero))
    input_grads = both(grad_zero, grad_one)

    order = Order()
    far = [bit for bit in (4, 8, 16, 32, 64, 128, 256) if bit < replicas]

    def doubled(chain):
        for bit in far:
            order.go(chain.ready_double(bit))

    order.go(three.ready_x())
    order.go(two.ready_half(1))
    order.go(one.ready_half(2))
    order.go(four.ready_x())
    order.go(two.ready_half(2))
    doubled(one)
    order.go(three.ready_half(1))
    doubled(two)
    order.go(four.ready_half(1))
    order.go(one.ready_back(2, None))
    order.go(three.ready_half(2))
    order.go(four.ready_half(2))
    order.go(one.ready_back(1, 2))
    order.go(two.ready_back(2, None))
    doubled(three)
    doubled(four)
    order.go(two.ready_back(1, 2))
    order.go(three.ready_back(2, None))
    order.go(four.ready_back(2, None))
    order.go(three.ready_back(1, 2))
    order.go(four.ready_back(1, 2))
    full = [chain.joined(1) for chain in (one, two, three, four)]
    came = [
        lax.ppermute(array, "pipe", pairs) for array, pairs in zip(full, ([(0, 1)], SWAP, [(1, 0)], [(1, 0)]))
    ]
    fc1_out, fc2_out, proj_out = run_assemble_mlp(flags, (full[0], came[0], full[1], came[1], full[2], came[2]))
    (qkv_out,) = run_assemble_qkv(flags, (full[1], came[1], full[3], came[3]))
    tail = full[3][384:392].reshape(-1).astype(F32)
    vectors = tail[:1536].reshape(6, 1, 256)
    return (
        activations,
        input_grads,
        vectors[0],
        vectors[1],
        qkv_out,
        tail[2560 : 2560 + TABLE * 8].reshape(1, TABLE, 8),
        proj_out,
        vectors[2],
        vectors[3],
        vectors[4],
        fc1_out,
        tail[1536:2560].reshape(1, 1024),
        fc2_out,
        vectors[5],
    )


def solution(mesh):
    return jax.shard_map(
        functools.partial(per_device, mesh.shape["rep"]),
        mesh=mesh,
        in_specs=(
            P(("group", "rep"), None, None),
            P(("group", "rep"), None, None),
            P(),
            P(),
            P(("group", "rep")),
            P("pipe", "group"),
            P("pipe", "group"),
            P("pipe", "group", None),
            P("pipe", None, "group"),
            P("pipe", "group", None),
            P("pipe", "group"),
            P("pipe", "group"),
            P("pipe", "group"),
            P("pipe", "group", None),
            P("pipe", "group"),
            P("pipe", "group", None),
            P("pipe", "group"),
        ),
        out_specs=(
            P("pipe", ("group", "rep"), None, None),
            P("pipe", ("group", "rep"), None, None),
            P("pipe", "group"),
            P("pipe", "group"),
            P("pipe", "group", None),
            P("pipe", None, "group"),
            P("pipe", "group", None),
            P("pipe", "group"),
            P("pipe", "group"),
            P("pipe", "group"),
            P("pipe", "group", None),
            P("pipe", "group"),
            P("pipe", "group", None),
            P("pipe", "group"),
        ),
        check_vma=False,
    )
```
